32 devices in a mesh: dp: 8 (over z, y), tensor: 4 (over x, core).
Axes of the slice: x: 2, y: 2, z: 4, core: 2. Of those that a mesh axis runs over, the one named last changes fastest.
Arguments:
- x_in: bfloat16 [2048, 5120], P('dp', 'tensor'), parts along dimension 0, may hold values from -6 to 6
- out_grad: bfloat16 [2048, 5120], P('dp', 'tensor'), parts along dimension 0, may hold values from -6 to 6
- gate_pre: bfloat16 [2048, 18432], P('dp', 'tensor'), parts along dimension 0, may hold values from -6 to 6
- up_pre: bfloat16 [2048, 18432], P('dp', 'tensor'), parts along dimension 0, may hold values from -6 to 6
- down_weight: bfloat16 [18432, 5120], P('tensor'), may hold values from -0.046875 to 0.046875
- x_factor: bfloat16 [5120, 64], P('tensor'), may hold values from -0.078125 to 0.078125
- gate_factor: bfloat16 [18432, 64], P('tensor'), may hold values from -0.046875 to 0.046875
- up_factor: bfloat16 [18432, 64], P('tensor'), may hold values from -0.046875 to 0.046875
- h_factor: bfloat16 [18432, 64], P('tensor'), may hold values from -0.046875 to 0.046875
- dy_factor: bfloat16 [5120, 64], P('tensor'), may hold values from -0.078125 to 0.078125
Outputs:
- gate_grad: float32 [16, 64, 64], P('dp'), parts along dimension 0
- up_grad: float32 [16, 64, 64], P('dp'), parts along dimension 0
- down_grad: float32 [16, 64, 64], P('dp'), parts along dimension 0
The draws below stay inside these ranges and needn't reach their ends.
There are 8 independent parts, one for each index of `dp`. The reference program is written for one: setup_inputs(seed, part) draws one part's arguments, and reference() takes and returns one part's arrays. A program takes and returns all parts, laid end to end along the dimension named above; an argument that names none is the same for every part. Nothing has to cross between parts.
All inputs are finite; a program needn't handle non-finite values.
Results may differ from the reference program's by a relative error of at most 0.0031.
Values may be sent and summed in bfloat16 or wider, within the bound.
No kernel may reach another device: no remote copies, remote signals or barrier semaphores. Data moves between devices by JAX's collectives and lax.ppermute only.
A program may use at most 128 MiB of HBM per device.

```python
import jax
import jax.numpy as jnp
from jax import lax

D = 5120
FFW = 18432
K = 64
SEQS = 2
LEN = 128
TOKENS = 256


def block_scale(rng, dims, shards, least, top_value):
    level = 1.0
    for dim, parts in shards:
        heights = jax.random.uniform(jax.random.fold_in(jax.random.fold_in(rng, 6), dim), (parts,), jnp.float32, least / len(shards), top_value / len(shards))
        level = level * jnp.repeat(jnp.exp(heights), dims[dim] // parts).reshape((-1,) + (1,) * (len(dims) - 1 - dim))
    return level


def scatter_about(own_key, extent, deviation, bound, pieces=(), held_as=jnp.bfloat16):
    array = jax.random.normal(own_key, extent, jnp.float32) * deviation
    if len(pieces) > 0:
        array = block_scale(own_key, extent, pieces, -0.22, 0.18) * array
    return jnp.clip(array, min=-bound, max=bound).astype(held_as)


def setup_inputs(seed: int = 0, part: int = 0) -> dict:
    keys = jax.random.split(jax.random.key(seed), 11)
    own_keys = jax.random.split(jax.random.fold_in(keys[10], part), 11)
    return {
        "x_in": scatter_about(own_keys[0], (TOKENS, D), 1.0, 6.0, ((1, 4),)),
        "out_grad": scatter_about(own_keys[1], (TOKENS, D), 1.0, 6.0, ((1, 4),)),
        "gate_pre": scatter_about(own_keys[2], (TOKENS, FFW), 1.5, 6.0, ((1, 4),)),
        "up_pre": scatter_about(own_keys[3], (TOKENS, FFW), 1.0, 6.0, ((1, 4),)),
        "down_weight": scatter_about(keys[4], (FFW, D), FFW ** -0.5, 0.046875, ((0, 4),)),
        "x_factor": scatter_about(keys[5], (D, K), D ** -0.5, 0.078125, ((0, 4),)),
        "gate_factor": scatter_about(keys[6], (FFW, K), FFW ** -0.5, 0.046875, ((0, 4),)),
        "up_factor": scatter_about(keys[7], (FFW, K), FFW ** -0.5, 0.046875, ((0, 4),)),
        "h_factor": scatter_about(keys[8], (FFW, K), FFW ** -0.5, 0.046875, ((0, 4),)),
        "dy_factor": scatter_about(keys[9], (D, K), D ** -0.5, 0.078125, ((0, 4),)),
    }


def product(left, right):
    return jnp.dot(left, right, preferred_element_type=jnp.float32)


def per_sequence(matrix):
    return matrix.reshape(SEQS, LEN, matrix.shape[1])


def reference(x_in, out_grad, gate_pre, up_pre, down_weight, x_factor, gate_factor, up_factor, h_factor, dy_factor):
    hidden_grad = lax.dot_general(out_grad, down_weight, (((1,), (1,)), ((), ())), preferred_element_type=jnp.float32)
    gate_val = gate_pre.astype(jnp.float32)
    up_val = up_pre.astype(jnp.float32)
    sigmoid_gate = jax.nn.sigmoid(gate_val)
    silu_gate = gate_val * sigmoid_gate
    hidden = (silu_gate * up_val).astype(jnp.bfloat16)
    d_gate = (hidden_grad * up_val * sigmoid_gate * (1.0 + gate_val * (1.0 - sigmoid_gate))).astype(jnp.bfloat16)
    d_up = (hidden_grad * silu_gate).astype(jnp.bfloat16)
    proj_x = product(x_in, x_factor)
    proj_gate = product(d_gate, gate_factor)
    proj_up = product(d_up, up_factor)
    proj_hidden = product(hidden, h_factor)
    proj_out = product(out_grad, dy_factor)
    highest = lax.Precision.HIGHEST
    gate_grad = jnp.einsum("sli,slj->sij", per_sequence(proj_x), per_sequence(proj_gate), precision=highest)
    up_grad = jnp.einsum("sli,slj->sij", per_sequence(proj_x), per_sequence(proj_up), precision=highest)
    down_grad = jnp.einsum("sli,slj->sij", per_sequence(proj_hidden), per_sequence(proj_out), precision=highest)
    return gate_grad, up_grad, down_grad
```

```python
import jax
import jax.numpy as jnp
from jax import lax
from jax.experimental import pallas as pl
from jax.experimental.pallas import tpu as pltpu
from jax.sharding import PartitionSpec as P

SEQS = 2
LEN = 128
BLOCK = 512
MIB = 1 << 20
HBM = pl.BlockSpec(memory_space=pl.ANY)
VMEM = pl.BlockSpec(memory_space=pltpu.VMEM)


def product(left, right):
    return jnp.dot(left, right, preferred_element_type=jnp.float32)


def rows_by_rows(left, right, precision=None):
    return lax.dot_general(
        left, right, (((1,), (1,)), ((), ())), precision=precision, preferred_element_type=jnp.float32
    )


def per_sequence(matrix):
    return matrix.reshape(SEQS, matrix.shape[0] // SEQS, matrix.shape[1])


def plain(x_in, out_grad, gate_pre, up_pre, down_weight, x_factor, gate_factor, up_factor, h_factor, dy_factor):
    hidden_grad = rows_by_rows(lax.all_gather(out_grad, "tensor", axis=1, tiled=True), down_weight)
    gate_val = gate_pre.astype(jnp.float32)
    up_val = up_pre.astype(jnp.float32)
    sigmoid_gate = jax.nn.sigmoid(gate_val)
    silu_gate = gate_val * sigmoid_gate
    hidden = (silu_gate * up_val).astype(jnp.bfloat16)
    d_gate = (hidden_grad * up_val * sigmoid_gate * (1.0 + gate_val * (1.0 - sigmoid_gate))).astype(jnp.bfloat16)
    d_up = (hidden_grad * silu_gate).astype(jnp.bfloat16)
    rows = [
        product(x_in, x_factor),
        product(d_gate, gate_factor),
        product(d_up, up_factor),
        product(hidden, h_factor),
        product(out_grad, dy_factor),
    ]
    totals = lax.psum(jnp.stack(rows), "tensor")
    p_x, q_gate, q_up, p_h, q_y = [per_sequence(totals[i]) for i in range(5)]
    highest = lax.Precision.HIGHEST
    return (
        jnp.einsum("sli,slj->sij", p_x, q_gate, precision=highest),
        jnp.einsum("sli,slj->sij", p_x, q_up, precision=highest),
        jnp.einsum("sli,slj->sij", p_h, q_y, precision=highest),
    )


def own_kernel(
    x_hbm, og_hbm, gate_hbm, up_hbm, w_hbm, xf_hbm, yf_hbm, hf_hbm,
    acc_ref, a_ref, b_ref, pq_ref, ph_ref,
    x_v, og_v, gate_v, up_v, w_v, xf_v, yf_v, hf_v, sems, block_sems,
):
    me = lax.axis_index("tensor")
    blocks, _, width = w_v.shape
    columns = pl.ds(pl.multiple_of(me * width, 128), width)

    def plain_copies():
        pairs = ((og_hbm, og_v), (hf_hbm, hf_v), (x_hbm, x_v), (xf_hbm, xf_v), (yf_hbm, yf_v))
        return [pltpu.make_async_copy(src, dst, sems.at[i]) for i, (src, dst) in enumerate(pairs)]

    def block_copies(i):
        units = pl.ds(i * BLOCK, BLOCK)
        return (
            pltpu.make_async_copy(w_hbm.at[units, columns], w_v.at[i], block_sems.at[i, 0]),
            pltpu.make_async_copy(gate_hbm.at[:, units], gate_v.at[i], block_sems.at[i, 1]),
            pltpu.make_async_copy(up_hbm.at[:, units], up_v.at[i], block_sems.at[i, 2]),
        )

    early = plain_copies()
    for copy in early[:2]:
        copy.start()
    for i in range(blocks):
        for copy in block_copies(i):
            copy.start()
    for copy in early[2:]:
        copy.start()
    for copy in early[:2]:
        copy.wait()
    ph_ref[...] = jnp.zeros_like(ph_ref)

    @pl.loop(0, blocks)
    def _(i):
        units = pl.ds(pl.multiple_of(i * BLOCK, BLOCK), BLOCK)
        for ref, dst, k in ((w_hbm, w_v, 0), (gate_hbm, gate_v, 1), (up_hbm, up_v, 2)):
            src = ref.at[units, columns] if k == 0 else ref.at[:, units]
            pltpu.make_async_copy(src, dst.at[i], block_sems.at[i, k]).wait()
        acc_ref[i] = rows_by_rows(og_v[...], w_v[i])
        g = gate_v[i].astype(jnp.float32)
        u = up_v[i].astype(jnp.float32)
        s = 0.5 * jnp.tanh(0.5 * g) + 0.5
        silu = g * s
        a_ref[i] = u * s * (1.0 + g * (1.0 - s))
        b_ref[i] = silu
        ph_ref[...] += rows_by_rows(hf_v[:, units], (silu * u).astype(jnp.bfloat16))

    for copy in early[2:]:
        copy.wait()
    rank = ph_ref.shape[0]
    pq_ref[:rank] = rows_by_rows(xf_v[...], x_v[...])
    pq_ref[rank:] = rows_by_rows(yf_v[...], og_v[...])


def mate_kernel(acc_in, og_ref, w_hbm, acc_ref, w_v, sems):
    mate = lax.axis_index("tensor") ^ 1
    blocks, _, width = w_v.shape
    columns = pl.ds(pl.multiple_of(mate * width, 128), width)

    def copy(i):
        units = pl.ds(i * BLOCK, BLOCK)
        return pltpu.make_async_copy(w_hbm.at[units, columns], w_v.at[i], sems.at[i])

    for i in range(blocks):
        copy(i).start()

    @pl.loop(0, blocks)
    def _(i):
        copy(i).wait()
        acc_ref[i] = acc_in[i] + rows_by_rows(og_ref[...], w_v[i])


def fetch_kernel(w_hbm, token_ref, near_ref, far_ref, sems):
    me = lax.axis_index("tensor")
    width = near_ref.shape[2]
    copies = []
    for k, (owner, ref) in enumerate(((me ^ 2, near_ref), (me ^ 3, far_ref))):
        columns = pl.ds(pl.multiple_of(owner * width, 128), width)
        for i in range(ref.shape[0]):
            copies.append(
                pltpu.make_async_copy(w_hbm.at[pl.ds(i * BLOCK, BLOCK), columns], ref.at[i], sems.at[k, i])
            )
    for copy in copies:
        copy.start()
    for copy in copies:
        copy.wait()


def near_kernel(acc_in, og_ref, w_ref, acc_ref):
    @pl.loop(0, acc_in.shape[0])
    def _(i):
        acc_ref[i] = acc_in[i] + rows_by_rows(og_ref[...], w_ref[i])


def far_kernel(
    acc_ref, og_ref, w_ref, a_ref, b_ref, gf_ref, uf_ref, mine_ref, theirs_ref, ph_ref, gu_ref, dn_ref, q_ref
):
    q_ref[...] = jnp.zeros_like(q_ref)
    rank = ph_ref.shape[0]

    @pl.loop(0, acc_ref.shape[0])
    def _(i):
        units = pl.ds(pl.multiple_of(i * BLOCK, BLOCK), BLOCK)
        hidden_grad = acc_ref[i] + rows_by_rows(og_ref[...], w_ref[i])
        d_gate = (hidden_grad * a_ref[i]).astype(jnp.bfloat16)
        d_up = (hidden_grad * b_ref[i]).astype(jnp.bfloat16)
        q_ref[:rank] += rows_by_rows(gf_ref[:, units], d_gate)
        q_ref[rank:] += rows_by_rows(uf_ref[:, units], d_up)

    first = lax.rem(lax.axis_index("tensor"), 2) == 0
    mine, theirs = mine_ref[...], theirs_ref[...]
    p_x = jnp.where(first, mine, theirs)
    q_y = jnp.where(first, theirs, mine)
    highest = lax.Precision.HIGHEST
    for s in range(SEQS):
        tokens = slice(s * LEN, (s + 1) * LEN)
        gu_ref[s] = rows_by_rows(p_x[:, tokens], q_ref[:, tokens], highest)
        dn_ref[s] = rows_by_rows(ph_ref[:, tokens], q_y[:, tokens], highest)


def sum_kernel(*refs):
    gu, dn, (gate_ref, up_ref, down_ref) = refs[:4], refs[4:8], refs[8:]
    rank = gate_ref.shape[1]
    total = (gu[0][...] + gu[1][...]) + (gu[2][...] + gu[3][...])
    gate_ref[...] = total[:, :, :rank]
    up_ref[...] = total[:, :, rank:]
    down_ref[...] = (dn[0][...] + dn[1][...]) + (dn[2][...] + dn[3][...])


def f32(*shape):
    return jax.ShapeDtypeStruct(shape, jnp.float32)


def fast(x_in, out_grad, gate_pre, up_pre, down_weight, x_factor, gate_factor, up_factor, h_factor, dy_factor):
    tokens, width = out_grad.shape
    units, rank = h_factor.shape
    blocks = units // BLOCK
    bf16 = jnp.bfloat16
    dma = pltpu.SemaphoreType.DMA

    def swap(array, bits):
        return lax.ppermute(array, "tensor", [(i, i ^ bits) for i in range(4)])

    def call(kernel, out_shape, in_specs, out_specs, mib, flops=0, moved=0, scratch=(), **kwargs):
        return pl.pallas_call(
            kernel,
            out_shape=out_shape,
            in_specs=in_specs,
            out_specs=out_specs,
            scratch_shapes=list(scratch),
            compiler_params=pltpu.CompilerParams(vmem_limit_bytes=mib * MIB),
            cost_estimate=pl.CostEstimate(flops=flops, bytes_accessed=moved, transcendentals=0),
            **kwargs,
        )

    per_product = 2 * tokens * width * units
    near = swap(out_grad, 2)
    mate = swap(out_grad, 1)
    held = pltpu.VMEM((blocks, tokens, BLOCK), jnp.float32)
    columns = pltpu.VMEM((blocks, BLOCK, width), bf16)

    acc, a, b, pq, ph = call(
        own_kernel,
        (held, held, held, f32(2 * rank, tokens), f32(rank, tokens)),
        [HBM] * 8,
        (VMEM,) * 5,
        26,
        per_product,
        2 * units * (width + 2 * tokens),
        [
            pltpu.VMEM((tokens, width), bf16),
            pltpu.VMEM((tokens, width), bf16),
            pltpu.VMEM((blocks, tokens, BLOCK), bf16),
            pltpu.VMEM((blocks, tokens, BLOCK), bf16),
            pltpu.VMEM((blocks, BLOCK, width), bf16),
            pltpu.VMEM((rank, width), bf16),
            pltpu.VMEM((rank, width), bf16),
            pltpu.VMEM((rank, units), bf16),
            dma((5,)),
            dma((blocks, 3)),
        ],
    )(x_in, out_grad, gate_pre, up_pre, down_weight, x_factor.T, dy_factor.T, h_factor.T)

    pq_mate = swap(pq, 1)
    acc = call(
        mate_kernel, held, [VMEM, VMEM, HBM], VMEM, 16, per_product, 2 * units * width,
        [pltpu.VMEM((blocks, BLOCK, width), bf16), dma((blocks,))],
        input_output_aliases={0: 0},
    )(acc, mate, down_weight)

    core = lax.rem(lax.axis_index("tensor"), 2)
    half = lax.dynamic_slice_in_dim(pq + pq_mate, core * rank, rank, 0)
    half_across = swap(half, 2)
    w_near, w_far = call(
        fetch_kernel, (columns, columns), [HBM, HBM], (VMEM, VMEM), 4, 0, 4 * units * width, [dma((2, blocks))]
    )(down_weight, half)
    half = half + half_across
    half_mate = swap(half, 1)
    far = swap(near, 1)
    acc = call(
        near_kernel, held, [VMEM] * 3, VMEM, 16, per_product, input_output_aliases={0: 0}
    )(acc, near, w_near)
    gu, dn = call(
        far_kernel,
        (f32(SEQS, rank, 2 * rank), f32(SEQS, rank, rank)),
        [VMEM] * 10,
        (VMEM, VMEM),
        16,
        per_product,
        0,
        [pltpu.VMEM((2 * rank, tokens), jnp.float32)],
    )(acc, far, w_far, a, b, gate_factor.T, up_factor.T, half, half_mate, ph)

    shares = [gu] + [swap(gu, k) for k in (1, 2, 3)] + [dn] + [swap(dn, k) for k in (1, 2, 3)]
    out = f32(SEQS, rank, rank)
    return tuple(call(sum_kernel, (out, out, out), [VMEM] * 8, (VMEM,) * 3, 4)(*shares))


def solution(mesh):
    def per_device(*arrays):
        out_grad, h_factor = arrays[1], arrays[8]
        fits = mesh.shape["tensor"] == 4 and out_grad.shape[1] % 128 == 0 and h_factor.shape[0] % BLOCK == 0
        return (fast if fits else plain)(*arrays)

    return jax.shard_map(
        per_device,
        mesh=mesh,
        in_specs=(P("dp", "tensor"),) * 4 + (P("tensor", None),) * 6,
        out_specs=(P("dp", None, None),) * 3,
        check_vma=False,
    )
```

```python
import functools

import jax
import jax.numpy as jnp
from jax import lax
from jax.experimental import pallas as pl
from jax.experimental.pallas import tpu as pltpu
from jax.sharding import PartitionSpec as P

SEQS = 2
LEN = 128
BLOCK = 512
HEAD = 2
AHEAD = 4
FIRST = 768
MIB = 1 << 20
ANY = pl.BlockSpec(memory_space=pl.ANY)
VMEM = pl.BlockSpec(memory_space=pltpu.VMEM)
BF16 = jnp.bfloat16
F32 = jnp.float32


def product(left, right):
    return jnp.dot(left, right, preferred_element_type=F32)


def rows_by_rows(left, right, precision=None):
    return lax.dot_general(
        left, right, (((1,), (1,)), ((), ())), precision=precision, preferred_element_type=F32
    )


def per_sequence(matrix):
    return matrix.reshape(SEQS, matrix.shape[0] // SEQS, matrix.shape[1])


def plain(x_in, out_grad, gate_pre, up_pre, down_weight, x_factor, gate_factor, up_factor, h_factor, dy_factor):
    hidden_grad = rows_by_rows(lax.all_gather(out_grad, "tensor", axis=1, tiled=True), down_weight)
    gate_val = gate_pre.astype(F32)
    up_val = up_pre.astype(F32)
    sigmoid_gate = jax.nn.sigmoid(gate_val)
    silu_gate = gate_val * sigmoid_gate
    hidden = (silu_gate * up_val).astype(BF16)
    d_gate = (hidden_grad * up_val * sigmoid_gate * (1.0 + gate_val * (1.0 - sigmoid_gate))).astype(BF16)
    d_up = (hidden_grad * silu_gate).astype(BF16)
    rows = [
        product(x_in, x_factor),
        product(d_gate, gate_factor),
        product(d_up, up_factor),
        product(hidden, h_factor),
        product(out_grad, dy_factor),
    ]
    totals = lax.psum(jnp.stack(rows), "tensor")
    p_x, q_gate, q_up, p_h, q_y = [per_sequence(totals[i]) for i in range(5)]
    highest = lax.Precision.HIGHEST
    return (
        jnp.einsum("sli,slj->sij", p_x, q_gate, precision=highest),
        jnp.einsum("sli,slj->sij", p_x, q_up, precision=highest),
        jnp.einsum("sli,slj->sij", p_h, q_y, precision=highest),
    )


class Columns:
    def __init__(self, bits, start, width):
        self.bits, self.start, self.width = bits, start, width

    def copy(self, w_hbm, i, dst, sem, per_device):
        owner = lax.axis_index("tensor") ^ self.bits
        columns = pl.ds(pl.multiple_of(owner * per_device + self.start, 128), self.width)
        units = pl.ds(pl.multiple_of(i * BLOCK, BLOCK), BLOCK)
        return pltpu.make_async_copy(w_hbm.at[units, columns], dst, sem)


def stream(step, following, blocks, per_device, w_hbm, head, w_v, next_head, sems, body):
    def start(j):
        @pl.when(j < blocks)
        def _():
            step.copy(w_hbm, j, w_v.at[j - HEAD], sems.at[j], per_device).start()

        if following is not None:

            @pl.when((j >= blocks) & (j < blocks + HEAD))
            def _():
                following.copy(w_hbm, j - blocks, next_head.at[j - blocks], sems.at[j], per_device).start()

    for j in range(HEAD, HEAD + AHEAD):
        step.copy(w_hbm, j, w_v.at[j - HEAD], sems.at[j], per_device).start()
    for i in range(HEAD):
        body(i, head[i])

    @pl.loop(HEAD, blocks)
    def _(i):
        start(i + AHEAD)
        step.copy(w_hbm, i, w_v.at[i - HEAD], sems.at[i], per_device).wait()
        body(i, w_v[i - HEAD])

    if following is not None:
        for j in range(HEAD):
            following.copy(w_hbm, j, next_head.at[j], sems.at[blocks + j], per_device).wait()


def two_terms(value):
    high = value.astype(BF16)
    return high, (value - high.astype(F32)).astype(BF16)


def entry_kernel(first_step, x_hbm, og_hbm, xf_hbm, yf_hbm, w_hbm, mate_ref, piece_ref, pq_ref, head_ref,
                 x_v, og_v, xf_v, yf_v, sems):
    width = og_hbm.shape[1]
    rank = xf_hbm.shape[0]
    pairs = ((og_hbm, og_v), (x_hbm, x_v), (xf_hbm, xf_v), (yf_hbm, yf_v))
    copies = [pltpu.make_async_copy(src, dst, sems.at[i]) for i, (src, dst) in enumerate(pairs)]
    copies += [first_step.copy(w_hbm, i, head_ref.at[i], sems.at[4 + i], width) for i in range(HEAD)]
    for copy in copies:
        copy.start()
    copies[0].wait()
    features = og_v[...].T
    mate_ref[:width] = features
    piece_ref[...] = features[:FIRST]
    for copy in copies[1:4]:
        copy.wait()
    pq_ref[:rank] = rows_by_rows(xf_v[...], x_v[...])
    pq_ref[rank:] = product(yf_v[...], mate_ref[:width])
    high, rest = two_terms(pq_ref[...])
    mate_ref[width : width + 2 * rank] = high
    mate_ref[width + 2 * rank :] = rest
    for copy in copies[4:]:
        copy.wait()


def own_kernel(step, following, og_ref, head_ref, gate_hbm, up_hbm, w_hbm, hf_hbm,
               acc_ref, a_ref, b_ref, ph_ref, next_ref, gate_v, up_v, w_v, hf_v, sems, gate_sems, up_sems, hf_sem):
    blocks = acc_ref.shape[0]
    width = step.width

    def units(i):
        return pl.ds(pl.multiple_of(i * BLOCK, BLOCK), BLOCK)

    def gate_up(i):
        return (
            pltpu.make_async_copy(gate_hbm.at[:, units(i)], gate_v.at[i], gate_sems.at[i]),
            pltpu.make_async_copy(up_hbm.at[:, units(i)], up_v.at[i], up_sems.at[i]),
        )

    whole = pltpu.make_async_copy(hf_hbm, hf_v, hf_sem)
    for copy in gate_up(0):
        copy.start()
    whole.start()
    for i in range(1, AHEAD):
        for copy in gate_up(i):
            copy.start()
    ph_ref[...] = jnp.zeros_like(ph_ref)

    def body(i, weights):
        @pl.when(i + AHEAD < blocks)
        def _():
            for copy in gate_up(i + AHEAD):
                copy.start()

        acc_ref[i] = product(weights, og_ref[:width])
        for copy in gate_up(i):
            copy.wait()
        if isinstance(i, int) and i == 0:
            whole.wait()
        g = gate_v[i].T.astype(F32)
        u = up_v[i].T.astype(F32)
        s = 0.5 * jnp.tanh(0.5 * g) + 0.5
        silu = g * s
        a_ref[i] = u * s * (1.0 + g * (1.0 - s))
        b_ref[i] = silu
        ph_ref[...] += product(hf_v[:, units(i)], (silu * u).astype(BF16))

    stream(step, following, blocks, width, w_hbm, head_ref, w_v, next_ref, sems, body)


def pack_kernel(mine_ref, theirs_ref, pq_ref, token_ref, chip_ref, across_ref):
    width = mine_ref.shape[0] - 2 * pq_ref.shape[0]
    rank = pq_ref.shape[0] // 2
    high = theirs_ref[width : width + 2 * rank].astype(F32)
    rest = theirs_ref[width + 2 * rank :].astype(F32)
    chip = pq_ref[...] + (high + rest)
    chip_ref[...] = chip
    even = lax.rem(lax.axis_index("tensor"), 2) == 0
    high, rest = two_terms(jnp.where(even, chip[:rank], chip[rank:]))
    across_ref[: width - FIRST] = mine_ref[FIRST:width]
    across_ref[width - FIRST : width - FIRST + rank] = high
    across_ref[width - FIRST + rank :] = rest


def step_kernel(step, following, per_device, acc_in, og_ref, head_ref, w_hbm, token_ref, acc_ref, next_ref, w_v, sems):
    def body(i, weights):
        acc_ref[i] = acc_in[i] + product(weights, og_ref[: step.width])

    stream(step, following, acc_in.shape[0], per_device, w_hbm, head_ref, w_v, next_ref, sems, body)


def after_kernel(array_ref, token_ref, same_ref):
    pass


def last_kernel(step, per_device, acc_ref, og_ref, head_ref, w_hbm, a_ref, b_ref, gf_ref, uf_ref, chip_ref, near_ref, ph_ref,
                share_ref, w_v, q_ref, sems):
    q_ref[...] = jnp.zeros_like(q_ref)
    rank = ph_ref.shape[0]

    def body(i, weights):
        hidden_grad = acc_ref[i] + product(weights, og_ref[: step.width])
        units = pl.ds(pl.multiple_of(i * BLOCK, BLOCK), BLOCK)
        q_ref[:rank] += product(gf_ref[:, units], (hidden_grad * a_ref[i]).astype(BF16))
        q_ref[rank:] += product(uf_ref[:, units], (hidden_grad * b_ref[i]).astype(BF16))

    stream(step, None, acc_ref.shape[0], per_device, w_hbm, head_ref, w_v, None, sems, body)

    def sums(ref):
        return ref[step.width : step.width + rank].astype(F32) + ref[step.width + rank :].astype(F32)

    even = lax.rem(lax.axis_index("tensor"), 2) == 0
    near, far = sums(near_ref), sums(og_ref)
    p_x = chip_ref[:rank] + jnp.where(even, near, far)
    q_y = chip_ref[rank:] + jnp.where(even, far, near)
    highest = lax.Precision.HIGHEST
    for s in range(SEQS):
        tokens = slice(s * LEN, (s + 1) * LEN)
        share_ref[s * rank : (s + 1) * rank] = rows_by_rows(p_x[:, tokens], q_ref[:, tokens], highest)
        share_ref[SEQS * rank :, s * rank : (s + 1) * rank] = rows_by_rows(ph_ref[:, tokens], q_y[:, tokens], highest)


def sum_kernel(mine_ref, theirs_ref, gate_ref, up_ref, down_ref):
    rank = gate_ref.shape[1]
    total = mine_ref[...] + theirs_ref[...]
    for s in range(SEQS):
        gate_ref[s] = total[s * rank : (s + 1) * rank, :rank]
        up_ref[s] = total[s * rank : (s + 1) * rank, rank:]
        down_ref[s] = total[SEQS * rank :, s * rank : (s + 1) * rank]


def fast(x_in, out_grad, gate_pre, up_pre, down_weight, x_factor, gate_factor, up_factor, h_factor, dy_factor):
    tokens, width = out_grad.shape
    units, rank = h_factor.shape
    blocks = units // BLOCK
    dma = pltpu.SemaphoreType.DMA

    def in_hbm(array):
        return pltpu.with_memory_space_constraint(array, pltpu.HBM)

    def swap(array, bits):
        return lax.ppermute(array, "tensor", [(i, i ^ bits) for i in range(4)])

    def call(kernel, out_shape, in_specs, scratch, mib, flops=0, moved=0, **kwargs):
        several = isinstance(out_shape, tuple)
        return pl.pallas_call(
            kernel,
            out_shape=out_shape,
            in_specs=in_specs,
            out_specs=(VMEM,) * len(out_shape) if several else VMEM,
            scratch_shapes=list(scratch),
            compiler_params=pltpu.CompilerParams(vmem_limit_bytes=mib * MIB),
            cost_estimate=pl.CostEstimate(flops=flops, bytes_accessed=moved, transcendentals=0),
            **kwargs,
        )

    def head(step):
        return pltpu.VMEM((HEAD, BLOCK, step.width), BF16)

    def body(step):
        return pltpu.VMEM((blocks - HEAD, BLOCK, step.width), BF16)

    own, mate = Columns(0, 0, width), Columns(1, 0, width)
    near_a, far_a = Columns(2, 0, FIRST), Columns(3, 0, FIRST)
    near_b, far_b = Columns(2, FIRST, width - FIRST), Columns(3, FIRST, width - FIRST)
    held = pltpu.VMEM((blocks, BLOCK, tokens), F32)
    weight, x_hbm, og_hbm = in_hbm(down_weight), in_hbm(x_in), in_hbm(out_grad)
    xf_hbm, yf_hbm, hf_hbm = in_hbm(x_factor.T), in_hbm(dy_factor.T), in_hbm(h_factor.T)

    to_mate, piece, pq, heads = call(
        functools.partial(entry_kernel, own),
        (
            pltpu.VMEM((width + 4 * rank, tokens), BF16),
            pltpu.VMEM((FIRST, tokens), BF16),
            pltpu.VMEM((2 * rank, tokens), F32),
            head(own),
        ),
        [ANY] * 5,
        [
            pltpu.VMEM((tokens, width), BF16),
            pltpu.VMEM((tokens, width), BF16),
            pltpu.VMEM((rank, width), BF16),
            pltpu.VMEM((rank, width), BF16),
            dma((4 + HEAD,)),
        ],
        8,
    )(x_hbm, og_hbm, xf_hbm, yf_hbm, weight)
    near_first = swap(piece, 2)
    from_mate = swap(to_mate, 1)

    acc, a, b, ph, heads = call(
        functools.partial(own_kernel, own, mate),
        (held, held, held, pltpu.VMEM((rank, tokens), F32), head(mate)),
        [VMEM, VMEM] + [ANY] * 4,
        [
            pltpu.VMEM((blocks, tokens, BLOCK), BF16),
            pltpu.VMEM((blocks, tokens, BLOCK), BF16),
            body(own),
            pltpu.VMEM((rank, units), BF16),
            dma((blocks + HEAD,)),
            dma((blocks,)),
            dma((blocks,)),
            dma,
        ],
        22,
        2 * tokens * width * units,
        2 * units * (width + 2 * tokens),
    )(to_mate, heads, in_hbm(gate_pre), in_hbm(up_pre), weight, hf_hbm)

    chip, across = call(
        pack_kernel,
        (pltpu.VMEM((2 * rank, tokens), F32), pltpu.VMEM((width - FIRST + 2 * rank, tokens), BF16)),
        [VMEM] * 3 + [ANY],
        [],
        4,
    )(to_mate, from_mate, pq, ph)
    near_second = swap(across, 2)

    def add(step, following, acc, features, heads, token):
        return call(
            functools.partial(step_kernel, step, following, width),
            (held, head(following)),
            [VMEM] * 3 + [ANY] * 2,
            [body(step), dma((blocks + HEAD,))],
            16,
            2 * tokens * step.width * units,
            2 * units * step.width,
            input_output_aliases={0: 0},
        )(acc, features, heads, weight, token)

    def after(array, token):
        return pl.pallas_call(
            after_kernel,
            out_shape=pltpu.VMEM(array.shape, array.dtype),
            in_specs=[ANY, ANY],
            out_specs=ANY,
            input_output_aliases={0: 0},
        )(array, token)

    acc, heads = add(mate, near_a, acc, from_mate, heads, chip)
    near_first = after(near_first, heads)
    far_first = swap(near_first, 1)
    acc, heads = add(near_a, far_a, acc, near_first, heads, chip)
    acc, heads = add(far_a, near_b, acc, far_first, heads, chip)
    near_second = after(near_second, heads)
    far_second = swap(near_second, 1)
    acc, heads = add(near_b, far_b, acc, near_second, heads, chip)
    share = call(
        functools.partial(last_kernel, far_b, width),
        pltpu.VMEM(((SEQS + 1) * rank, 2 * rank), F32),
        [VMEM] * 3 + [ANY] + [VMEM] * 7,
        [body(far_b), pltpu.VMEM((2 * rank, tokens), F32), dma((blocks,))],
        16,
        2 * tokens * far_b.width * units,
        2 * units * far_b.width,
    )(acc, far_second, heads, weight, a, b, gate_factor.T, up_factor.T, chip, near_second, ph)

    chip_share = share + swap(share, 1)
    out = jax.ShapeDtypeStruct((SEQS, rank, rank), F32)
    return call(sum_kernel, (out, out, out), [VMEM] * 2, [], 4)(chip_share, swap(chip_share, 2))


def solution(mesh):
    def per_device(*arrays):
        (tokens, width), (units, rank) = arrays[1].shape, arrays[8].shape
        fits = (
            mesh.shape["tensor"] == 4
            and (tokens, rank) == (SEQS * LEN, LEN // 2)
            and width % 128 == 0
            and width > FIRST
            and units % BLOCK == 0
            and units // BLOCK > HEAD + AHEAD
        )
        return tuple((fast if fits else plain)(*arrays))

    return jax.shard_map(
        per_device,
        mesh=mesh,
        in_specs=(P("dp", "tensor"),) * 4 + (P("tensor", None),) * 6,
        out_specs=(P("dp", None, None),) * 3,
        check_vma=False,
    )
```

```python
import functools

import jax
import jax.numpy as jnp
from jax import lax
from jax.experimental import pallas as pl
from jax.experimental.pallas import tpu as pltpu
from jax.sharding import PartitionSpec as P

SEQS = 2
LEN = 128
FIRST = 768
MIB = 1 << 20
ANY = pl.BlockSpec(memory_space=pl.ANY)
VMEM = pl.BlockSpec(memory_space=pltpu.VMEM)
BF16 = jnp.bfloat16
F32 = jnp.float32


def product(left, right):
    return jnp.dot(left, right, preferred_element_type=F32)


def rows_by_rows(left, right, precision=None):
    return lax.dot_general(
        left, right, (((1,), (1,)), ((), ())), precision=precision, preferred_element_type=F32
    )


def per_sequence(matrix):
    return matrix.reshape(SEQS, matrix.shape[0] // SEQS, matrix.shape[1])


def plain(x_in, out_grad, gate_pre, up_pre, down_weight, x_factor, gate_factor, up_factor, h_factor, dy_factor):
    hidden_grad = rows_by_rows(lax.all_gather(out_grad, "tensor", axis=1, tiled=True), down_weight)
    gate_val = gate_pre.astype(F32)
    up_val = up_pre.astype(F32)
    sigmoid_gate = jax.nn.sigmoid(gate_val)
    silu_gate = gate_val * sigmoid_gate
    hidden = (silu_gate * up_val).astype(BF16)
    d_gate = (hidden_grad * up_val * sigmoid_gate * (1.0 + gate_val * (1.0 - sigmoid_gate))).astype(BF16)
    d_up = (hidden_grad * silu_gate).astype(BF16)
    rows = [
        product(x_in, x_factor),
        product(d_gate, gate_factor),
        product(d_up, up_factor),
        product(hidden, h_factor),
        product(out_grad, dy_factor),
    ]
    totals = lax.psum(jnp.stack(rows), "tensor")
    p_x, q_gate, q_up, p_h, q_y = [per_sequence(totals[i]) for i in range(5)]
    highest = lax.Precision.HIGHEST
    return (
        jnp.einsum("sli,slj->sij", p_x, q_gate, precision=highest),
        jnp.einsum("sli,slj->sij", p_x, q_up, precision=highest),
        jnp.einsum("sli,slj->sij", p_h, q_y, precision=highest),
    )


class Step:
    def __init__(self, bits, start, width, block, heads, ahead):
        self.bits, self.start, self.width = bits, start, width
        self.block, self.heads, self.ahead = block, heads, ahead

    def copy(self, w_hbm, i, dst, sem, per_device):
        owner = lax.axis_index("tensor") ^ self.bits
        columns = pl.ds(pl.multiple_of(owner * per_device + self.start, 128), self.width)
        return pltpu.make_async_copy(w_hbm.at[self.units(i), columns], dst, sem)

    def units(self, i):
        return pl.ds(pl.multiple_of(i * self.block, self.block), self.block)

    def head(self):
        return pltpu.VMEM((self.heads, self.block, self.width), BF16)

    def body(self, units):
        return pltpu.VMEM((units // self.block - self.heads, self.block, self.width), BF16)


def stream(step, following, units, per_device, w_hbm, head, w_v, next_head, sems, body):
    blocks = units // step.block

    def following_copy(j):
        return following.copy(w_hbm, j, next_head.at[j], sems.at[blocks + j], per_device)

    def start(j):
        @pl.when(j < blocks)
        def _():
            step.copy(w_hbm, j, w_v.at[j - step.heads], sems.at[j], per_device).start()

        if following is not None:

            @pl.when(j == blocks)
            def _():
                for k in range(following.heads):
                    following_copy(k).start()

    for j in range(step.heads, step.heads + step.ahead):
        step.copy(w_hbm, j, w_v.at[j - step.heads], sems.at[j], per_device).start()
    for i in range(step.heads):
        body(i, head.at[i])

    @pl.loop(step.heads, blocks)
    def _(i):
        start(i + step.ahead)
        step.copy(w_hbm, i, w_v.at[i - step.heads], sems.at[i], per_device).wait()
        body(i, w_v.at[i - step.heads])

    if following is not None:
        for j in range(following.heads):
            following_copy(j).wait()


def two_terms(value):
    high = value.astype(BF16)
    return high, (value - high.astype(F32)).astype(BF16)


def entry_kernel(first_step, x_hbm, og_hbm, xf_hbm, yf_hbm, w_hbm, mate_ref, piece_ref, pq_ref, head_ref,
                 x_v, og_v, xf_v, yf_v, sems):
    tokens, width = og_hbm.shape
    rank = xf_hbm.shape[0]
    pairs = ((og_hbm, og_v), (x_hbm, x_v), (xf_hbm, xf_v), (yf_hbm, yf_v))
    copies = [pltpu.make_async_copy(src, dst, sems.at[i]) for i, (src, dst) in enumerate(pairs)]
    copies += [first_step.copy(w_hbm, i, head_ref.at[i], sems.at[4 + i], width) for i in range(first_step.heads)]
    for copy in copies:
        copy.start()
    copies[0].wait()
    mate_ref[:tokens] = og_v[...]
    piece_ref[...] = og_v[:, :FIRST]
    for copy in copies[1:4]:
        copy.wait()
    pq_ref[:rank] = rows_by_rows(xf_v[...], x_v[...])
    pq_ref[rank:] = rows_by_rows(yf_v[...], og_v[...])
    high, rest = two_terms(pq_ref[...])
    for k, part in enumerate((high[:rank], high[rank:], rest[:rank], rest[rank:])):
        mate_ref[tokens:, k * tokens : (k + 1) * tokens] = part
    mate_ref[tokens:, 4 * tokens :] = jnp.zeros_like(mate_ref[tokens:, 4 * tokens :])
    for copy in copies[4:]:
        copy.wait()


def own_kernel(step, following, og_ref, head_ref, gate_hbm, up_hbm, w_hbm, hf_hbm,
               acc_ref, a_ref, b_ref, ph_ref, next_ref, gate_v, up_v, w_v, hf_v, sems, gate_sems, up_sems, hf_sem):
    tokens, units = acc_ref.shape
    blocks = units // step.block

    def gate_up(i):
        return (
            pltpu.make_async_copy(gate_hbm.at[:, step.units(i)], gate_v.at[i], gate_sems.at[i]),
            pltpu.make_async_copy(up_hbm.at[:, step.units(i)], up_v.at[i], up_sems.at[i]),
        )

    whole = pltpu.make_async_copy(hf_hbm, hf_v, hf_sem)
    for copy in gate_up(0):
        copy.start()
    whole.start()
    for i in range(1, step.ahead):
        for copy in gate_up(i):
            copy.start()
    ph_ref[...] = jnp.zeros_like(ph_ref)

    def body(i, weights):
        @pl.when(i + step.ahead < blocks)
        def _():
            for copy in gate_up(i + step.ahead):
                copy.start()

        for copy in gate_up(i):
            copy.wait()
        if isinstance(i, int) and i == 0:
            whole.wait()
        at = step.units(i)
        acc_ref[:, at] = rows_by_rows(og_ref[:tokens], weights[...])
        g = gate_v[i].astype(F32)
        u = up_v[i].astype(F32)
        s = 0.5 * jnp.tanh(0.5 * g) + 0.5
        silu = g * s
        a_ref[:, at] = u * s * (1.0 + g * (1.0 - s))
        b_ref[:, at] = silu
        ph_ref[...] += rows_by_rows(hf_v[:, at], (silu * u).astype(BF16))

    stream(step, following, units, step.width, w_hbm, head_ref, w_v, next_ref, sems, body)


def pack_kernel(mine_ref, theirs_ref, pq_ref, token_ref, chip_ref, across_ref):
    rank, tokens = pq_ref.shape[0] // 2, pq_ref.shape[1]

    def theirs(k):
        part = theirs_ref[tokens:, k * tokens : (k + 1) * tokens]
        return part.astype(F32)

    p_x = pq_ref[:rank] + (theirs(0) + theirs(2))
    q_y = pq_ref[rank:] + (theirs(1) + theirs(3))
    chip_ref[:rank] = p_x
    chip_ref[rank:] = q_y
    even = lax.rem(lax.axis_index("tensor"), 2) == 0
    high, rest = two_terms(jnp.where(even, p_x, q_y))
    across_ref[:tokens] = mine_ref[:tokens, FIRST:]
    across_ref[tokens:, :tokens] = high
    across_ref[tokens:, tokens:] = rest


def step_kernel(step, following, per_device, acc_in, og_ref, head_ref, w_hbm, token_ref, acc_ref, next_ref, w_v, sems):
    tokens, units = acc_in.shape

    def body(i, weights):
        at = step.units(i)
        acc_ref[:, at] = acc_in[:, at] + rows_by_rows(og_ref[:tokens], weights[...])

    stream(step, following, units, per_device, w_hbm, head_ref, w_v, next_ref, sems, body)


def after_kernel(array_ref, token_ref, same_ref):
    pass


def last_kernel(step, per_device, acc_ref, og_ref, head_ref, w_hbm, a_ref, b_ref, gf_ref, uf_ref, chip_ref, near_ref, ph_ref,
                share_ref, w_v, q_ref, sems):
    q_ref[...] = jnp.zeros_like(q_ref)
    rank = ph_ref.shape[0]
    tokens, units = acc_ref.shape

    def body(i, weights):
        at = step.units(i)
        hidden_grad = acc_ref[:, at] + rows_by_rows(og_ref[:tokens], weights[...])
        q_ref[:rank] += rows_by_rows(gf_ref[:, at], (hidden_grad * a_ref[:, at]).astype(BF16))
        q_ref[rank:] += rows_by_rows(uf_ref[:, at], (hidden_grad * b_ref[:, at]).astype(BF16))

    stream(step, None, units, per_device, w_hbm, head_ref, w_v, None, sems, body)

    def sums(ref):
        high, rest = ref[tokens:, :tokens], ref[tokens:, tokens:]
        return high.astype(F32) + rest.astype(F32)

    even = lax.rem(lax.axis_index("tensor"), 2) == 0
    near, far = sums(near_ref), sums(og_ref)
    p_x = chip_ref[:rank] + jnp.where(even, near, far)
    q_y = chip_ref[rank:] + jnp.where(even, far, near)
    highest = lax.Precision.HIGHEST
    for s in range(SEQS):
        at = slice(s * LEN, (s + 1) * LEN)
        share_ref[s * rank : (s + 1) * rank] = rows_by_rows(p_x[:, at], q_ref[:, at], highest)
        share_ref[SEQS * rank :, s * rank : (s + 1) * rank] = rows_by_rows(ph_ref[:, at], q_y[:, at], highest)


def sum_kernel(mine_ref, theirs_ref, gate_ref, up_ref, down_ref):
    rank = gate_ref.shape[1]
    total = mine_ref[...] + theirs_ref[...]
    for s in range(SEQS):
        gate_ref[s] = total[s * rank : (s + 1) * rank, :rank]
        up_ref[s] = total[s * rank : (s + 1) * rank, rank:]
        down_ref[s] = total[SEQS * rank :, s * rank : (s + 1) * rank]


def fast(x_in, out_grad, gate_pre, up_pre, down_weight, x_factor, gate_factor, up_factor, h_factor, dy_factor):
    tokens, width = out_grad.shape
    units, rank = h_factor.shape
    dma = pltpu.SemaphoreType.DMA

    def in_hbm(array):
        return pltpu.with_memory_space_constraint(array, pltpu.HBM)

    def swap(array, bits):
        return lax.ppermute(array, "tensor", [(i, i ^ bits) for i in range(4)])

    def call(kernel, out_shape, in_specs, scratch, mib, flops=0, moved=0, **kwargs):
        several = isinstance(out_shape, tuple)
        return pl.pallas_call(
            kernel,
            out_shape=out_shape,
            in_specs=in_specs,
            out_specs=(VMEM,) * len(out_shape) if several else VMEM,
            scratch_shapes=list(scratch),
            compiler_params=pltpu.CompilerParams(vmem_limit_bytes=mib * MIB),
            cost_estimate=pl.CostEstimate(flops=flops, bytes_accessed=moved, transcendentals=0),
            **kwargs,
        )

    own, mate = Step(0, 0, width, 512, 2, 4), Step(1, 0, width, 1536, 1, 2)
    near_a, far_a = Step(2, 0, FIRST, 768, 2, 3), Step(3, 0, FIRST, 1152, 1, 2)
    near_b, far_b = Step(2, FIRST, width - FIRST, 1536, 1, 2), Step(3, FIRST, width - FIRST, 768, 2, 3)
    held = pltpu.VMEM((tokens, units), F32)
    rows = tokens + rank
    weight, x_hbm, og_hbm = in_hbm(down_weight), in_hbm(x_in), in_hbm(out_grad)
    xf_hbm, yf_hbm, hf_hbm = in_hbm(x_factor.T), in_hbm(dy_factor.T), in_hbm(h_factor.T)

    to_mate, piece, pq, heads = call(
        functools.partial(entry_kernel, own),
        (
            pltpu.VMEM((rows, width), BF16),
            pltpu.VMEM((tokens, FIRST), BF16),
            pltpu.VMEM((2 * rank, tokens), F32),
            own.head(),
        ),
        [ANY] * 5,
        [
            pltpu.VMEM((tokens, width), BF16),
            pltpu.VMEM((tokens, width), BF16),
            pltpu.VMEM((rank, width), BF16),
            pltpu.VMEM((rank, width), BF16),
            dma((4 + own.heads,)),
        ],
        8,
    )(x_hbm, og_hbm, xf_hbm, yf_hbm, weight)
    near_first = swap(piece, 2)
    from_mate = swap(to_mate, 1)

    acc, a, b, ph, heads = call(
        functools.partial(own_kernel, own, mate),
        (held, held, held, pltpu.VMEM((rank, tokens), F32), mate.head()),
        [VMEM, VMEM] + [ANY] * 4,
        [
            pltpu.VMEM((units // own.block, tokens, own.block), BF16),
            pltpu.VMEM((units // own.block, tokens, own.block), BF16),
            own.body(units),
            pltpu.VMEM((rank, units), BF16),
            dma((units // own.block + mate.heads,)),
            dma((units // own.block,)),
            dma((units // own.block,)),
            dma,
        ],
        22,
        2 * tokens * width * units,
        2 * units * (width + 2 * tokens),
    )(to_mate, heads, in_hbm(gate_pre), in_hbm(up_pre), weight, hf_hbm)

    chip, across = call(
        pack_kernel,
        (pltpu.VMEM((2 * rank, tokens), F32), pltpu.VMEM((rows, width - FIRST), BF16)),
        [VMEM] * 3 + [ANY],
        [],
        4,
    )(to_mate, from_mate, pq, ph)
    near_second = swap(across, 2)

    def add(step, following, acc, features, heads, token):
        return call(
            functools.partial(step_kernel, step, following, width),
            (held, following.head()),
            [VMEM] * 3 + [ANY] * 2,
            [step.body(units), dma((units // step.block + following.heads,))],
            16,
            2 * tokens * step.width * units,
            2 * units * step.width,
            input_output_aliases={0: 0},
        )(acc, features, heads, weight, token)

    def after(array, token):
        return pl.pallas_call(
            after_kernel,
            out_shape=pltpu.VMEM(array.shape, array.dtype),
            in_specs=[ANY, ANY],
            out_specs=ANY,
            input_output_aliases={0: 0},
            compiler_params=pltpu.CompilerParams(vmem_limit_bytes=MIB),
        )(array, token)

    acc, heads = add(mate, near_a, acc, from_mate, heads, chip)
    near_first = after(near_first, heads)
    far_first = swap(near_first, 1)
    acc, heads = add(near_a, far_a, acc, near_first, heads, chip)
    acc, heads = add(far_a, near_b, acc, far_first, heads, chip)
    near_second = after(near_second, heads)
    far_second = swap(near_second, 1)
    acc, heads = add(near_b, far_b, acc, near_second, heads, chip)
    share = call(
        functools.partial(last_kernel, far_b, width),
        pltpu.VMEM(((SEQS + 1) * rank, 2 * rank), F32),
        [VMEM] * 3 + [ANY] + [VMEM] * 7,
        [far_b.body(units), pltpu.VMEM((2 * rank, tokens), F32), dma((units // far_b.block,))],
        16,
        2 * tokens * far_b.width * units,
        2 * units * far_b.width,
    )(acc, far_second, heads, weight, a, b, gate_factor.T, up_factor.T, chip, near_second, ph)

    chip_share = share + swap(share, 1)
    out = jax.ShapeDtypeStruct((SEQS, rank, rank), F32)
    return call(sum_kernel, (out, out, out), [VMEM] * 2, [], 4)(chip_share, swap(chip_share, 2))


def solution(mesh):
    def per_device(*arrays):
        (tokens, width), (units, rank) = arrays[1].shape, arrays[8].shape
        fits = (
            mesh.shape["tensor"] == 4
            and (tokens, rank) == (SEQS * LEN, LEN // 2)
            and width == FIRST + 2 * tokens
            and units % 4608 == 0
        )
        return tuple((fast if fits else plain)(*arrays))

    return jax.shard_map(
        per_device,
        mesh=mesh,
        in_specs=(P("dp", "tensor"),) * 4 + (P("tensor", None),) * 6,
        out_specs=(P("dp", None, None),) * 3,
        check_vma=False,
    )
```

```python
import functools

import jax
import jax.numpy as jnp
from jax import lax
from jax.experimental import pallas as pl
from jax.experimental.pallas import tpu as pltpu
from jax.sharding import PartitionSpec as P

SEQS = 2
LEN = 128
PIECE = 512
BLOCK = 1536
LAST = 768
MIB = 1 << 20
ANY = pl.BlockSpec(memory_space=pl.ANY)
VMEM = pl.BlockSpec(memory_space=pltpu.VMEM)
BF16 = jnp.bfloat16
F32 = jnp.float32


def product(left, right):
    return jnp.dot(left, right, preferred_element_type=F32)


def rows_by_rows(left, right, precision=None):
    return lax.dot_general(
        left, right, (((1,), (1,)), ((), ())), precision=precision, preferred_element_type=F32
    )


def per_sequence(matrix):
    return matrix.reshape(SEQS, matrix.shape[0] // SEQS, matrix.shape[1])


def plain(x_in, out_grad, gate_pre, up_pre, down_weight, x_factor, gate_factor, up_factor, h_factor, dy_factor):
    hidden_grad = rows_by_rows(lax.all_gather(out_grad, "tensor", axis=1, tiled=True), down_weight)
    gate_val = gate_pre.astype(F32)
    up_val = up_pre.astype(F32)
    sigmoid_gate = jax.nn.sigmoid(gate_val)
    silu_gate = gate_val * sigmoid_gate
    hidden = (silu_gate * up_val).astype(BF16)
    d_gate = (hidden_grad * up_val * sigmoid_gate * (1.0 + gate_val * (1.0 - sigmoid_gate))).astype(BF16)
    d_up = (hidden_grad * silu_gate).astype(BF16)
    rows = [
        product(x_in, x_factor),
        product(d_gate, gate_factor),
        product(d_up, up_factor),
        product(hidden, h_factor),
        product(out_grad, dy_factor),
    ]
    totals = lax.psum(jnp.stack(rows), "tensor")
    p_x, q_gate, q_up, p_h, q_y = [per_sequence(totals[i]) for i in range(5)]
    highest = lax.Precision.HIGHEST
    return (
        jnp.einsum("sli,slj->sij", p_x, q_gate, precision=highest),
        jnp.einsum("sli,slj->sij", p_x, q_up, precision=highest),
        jnp.einsum("sli,slj->sij", p_h, q_y, precision=highest),
    )


def weight_copies(w_hbm, bits, dst, sems, first_row=0):
    width = dst.shape[1]
    columns = pl.ds(pl.multiple_of((lax.axis_index("tensor") ^ bits) * width, 128), width)
    return [
        pltpu.make_async_copy(
            w_hbm.at[pl.ds(first_row + k * PIECE, PIECE), columns], dst.at[pl.ds(k * PIECE, PIECE)], sems.at[k]
        )
        for k in range(dst.shape[0] // PIECE)
    ]


def start(copies):
    for copy in copies:
        copy.start()


def wait(copies):
    for copy in copies:
        copy.wait()


def own_kernel(x_hbm, og_hbm, gate_hbm, up_hbm, w_hbm, xf_hbm, yf_hbm, hf_hbm,
               acc_ref, a_ref, b_ref, ph_ref, pq_ref, next_ref,
               x_v, og_v, gate_v, up_v, w_v, xf_v, yf_v, hf_v, hidden_v, sems, gate_sems, up_sems, w_sems, next_sems):
    units = acc_ref.shape[1]
    rank = ph_ref.shape[0]
    per_turn = BLOCK // PIECE
    turns = units // BLOCK

    def gate_up(k):
        at, slot, to = pl.ds(k * PIECE, PIECE), k // per_turn % 2, pl.ds(k % per_turn * PIECE, PIECE)
        return [
            pltpu.make_async_copy(gate_hbm.at[:, at], gate_v.at[slot, :, to], gate_sems.at[k]),
            pltpu.make_async_copy(up_hbm.at[:, at], up_v.at[slot, :, to], up_sems.at[k]),
        ]

    def weights(i):
        return weight_copies(w_hbm, 0, w_v.at[i % 2], w_sems.at[i], i * BLOCK)

    pairs = ((og_hbm, og_v), (hf_hbm, hf_v), (x_hbm, x_v), (xf_hbm, xf_v), (yf_hbm, yf_v))
    small = [pltpu.make_async_copy(src, dst, sems.at[i]) for i, (src, dst) in enumerate(pairs)]
    following = weight_copies(w_hbm, 1, next_ref, next_sems)

    def start_turn(i):
        for k in range(i * per_turn, (i + 1) * per_turn):
            start(gate_up(k))
            if k == 0:
                start(small[:2])
        start(weights(i))

    start_turn(0)
    start_turn(1)
    start(small[2:])
    ph_ref[...] = jnp.zeros_like(ph_ref)
    for i in range(turns):
        slot = i % 2
        for k in range(per_turn):
            at = slice(i * BLOCK + k * PIECE, i * BLOCK + (k + 1) * PIECE)
            part = slice(k * PIECE, (k + 1) * PIECE)
            wait(gate_up(i * per_turn + k))
            g = gate_v[slot, :, part].astype(F32)
            u = up_v[slot, :, part].astype(F32)
            s = 0.5 * jnp.tanh(0.5 * g) + 0.5
            silu = g * s
            a_ref[:, at] = u * s * (1.0 + g * (1.0 - s))
            b_ref[:, at] = silu
            hidden_v[:, part] = (silu * u).astype(BF16)
        at = slice(i * BLOCK, (i + 1) * BLOCK)
        if i == 0:
            wait(small[:2])
        wait(weights(i))
        acc_ref[:, at] = rows_by_rows(og_v[...], w_v[slot])
        ph_ref[...] += rows_by_rows(hf_v[:, at], hidden_v[...])
        if i + 2 < turns:
            start_turn(i + 2)
        if i + 2 == turns:
            start(following)
    wait(small[2:])
    pq_ref[:rank] = rows_by_rows(xf_v[...], x_v[...])
    pq_ref[rank:] = rows_by_rows(yf_v[...], og_v[...])
    wait(following)


def add_kernel(bits, following_bits, acc_in, og_ref, head_ref, w_hbm, acc_ref, next_ref, w_v, sems, next_sems):
    first = head_ref.shape[0]
    weights = weight_copies(w_hbm, bits, w_v, sems, first)
    following = weight_copies(w_hbm, following_bits, next_ref, next_sems)
    start(weights)
    start(following)
    for i in range(acc_in.shape[1] // BLOCK):
        row = i * BLOCK
        at = slice(row, row + BLOCK)
        if row < first:
            block = head_ref[at]
        else:
            wait(weights[(row - first) // PIECE : (row + BLOCK - first) // PIECE])
            block = w_v[row - first : row + BLOCK - first]
        acc_ref[:, at] = acc_in[:, at] + rows_by_rows(og_ref[...], block)
    wait(following)


def far_kernel(bits, acc_ref, og_ref, head_ref, w_hbm, a_ref, b_ref, gf_ref, uf_ref, q_ref, w_v, sems):
    rank = gf_ref.shape[0]
    first = head_ref.shape[0]
    weights = weight_copies(w_hbm, bits, w_v, sems, first)
    start(weights)
    q_ref[...] = jnp.zeros_like(q_ref)

    def turn(at, block):
        hidden_grad = acc_ref[:, at] + rows_by_rows(og_ref[...], block)
        q_ref[:rank] += rows_by_rows(gf_ref[:, at], (hidden_grad * a_ref[:, at]).astype(BF16))
        q_ref[rank:] += rows_by_rows(uf_ref[:, at], (hidden_grad * b_ref[:, at]).astype(BF16))

    @pl.loop(0, first // LAST)
    def _(i):
        at = pl.ds(pl.multiple_of(i * LAST, LAST), LAST)
        turn(at, head_ref[at])

    wait(weights)

    @pl.loop(0, w_v.shape[0] // LAST)
    def _(i):
        row = pl.multiple_of(i * LAST, LAST)
        turn(pl.ds(pl.multiple_of(first + row, LAST), LAST), w_v[pl.ds(row, LAST)])


def after_kernel(array_ref, token_ref, same_ref):
    pass


def chip_kernel(mine_ref, theirs_ref, token_ref, chip_ref):
    chip_ref[...] = mine_ref[...] + theirs_ref[...]


def gradients_kernel(chip_ref, other_ref, q_ref, ph_ref, share_ref):
    rank = ph_ref.shape[0]
    highest = lax.Precision.HIGHEST
    total = chip_ref[...] + other_ref[...]
    for s in range(SEQS):
        at = slice(s * LEN, (s + 1) * LEN)
        share_ref[s * rank : (s + 1) * rank] = rows_by_rows(total[:rank, at], q_ref[:, at], highest)
        share_ref[SEQS * rank :, s * rank : (s + 1) * rank] = rows_by_rows(ph_ref[:, at], total[rank:, at], highest)


def sum_kernel(mine_ref, theirs_ref, gate_ref, up_ref, down_ref):
    rank = gate_ref.shape[1]
    total = mine_ref[...] + theirs_ref[...]
    for s in range(SEQS):
        gate_ref[s] = total[s * rank : (s + 1) * rank, :rank]
        up_ref[s] = total[s * rank : (s + 1) * rank, rank:]
        down_ref[s] = total[SEQS * rank :, s * rank : (s + 1) * rank]


def fast(x_in, out_grad, gate_pre, up_pre, down_weight, x_factor, gate_factor, up_factor, h_factor, dy_factor):
    tokens, width = out_grad.shape
    units, rank = h_factor.shape
    dma = pltpu.SemaphoreType.DMA

    def in_hbm(array):
        return pltpu.with_memory_space_constraint(array, pltpu.HBM)

    def swap(array, bits):
        return lax.ppermute(array, "tensor", [(i, i ^ bits) for i in range(4)])

    def call(kernel, out_shape, in_specs, scratch, mib, flops=0, moved=0, **kwargs):
        several = isinstance(out_shape, tuple)
        return pl.pallas_call(
            kernel,
            out_shape=out_shape,
            in_specs=in_specs,
            out_specs=(VMEM,) * len(out_shape) if several else VMEM,
            scratch_shapes=list(scratch),
            compiler_params=pltpu.CompilerParams(vmem_limit_bytes=mib * MIB),
            cost_estimate=pl.CostEstimate(flops=flops, bytes_accessed=moved, transcendentals=0),
            **kwargs,
        )

    held = pltpu.VMEM((tokens, units), F32)
    per_product = 2 * tokens * width * units
    pieces = units // PIECE
    per_turn = BLOCK // PIECE
    weight, og_hbm = in_hbm(down_weight), in_hbm(out_grad)

    near = swap(out_grad, 2)
    mate = swap(out_grad, 1)
    acc, a, b, ph, pq, head = call(
        own_kernel,
        (held, held, held, pltpu.VMEM((rank, tokens), F32), pltpu.VMEM((2 * rank, tokens), F32), pltpu.VMEM((BLOCK, width), BF16)),
        [ANY] * 8,
        [
            pltpu.VMEM((tokens, width), BF16),
            pltpu.VMEM((tokens, width), BF16),
            pltpu.VMEM((2, tokens, BLOCK), BF16),
            pltpu.VMEM((2, tokens, BLOCK), BF16),
            pltpu.VMEM((2, BLOCK, width), BF16),
            pltpu.VMEM((rank, width), BF16),
            pltpu.VMEM((rank, width), BF16),
            pltpu.VMEM((rank, units), BF16),
            pltpu.VMEM((tokens, BLOCK), BF16),
            dma((5,)),
            dma((pieces,)),
            dma((pieces,)),
            dma((units // BLOCK, per_turn)),
            dma((per_turn,)),
        ],
        20,
        per_product,
        2 * units * (width + 2 * tokens),
    )(in_hbm(x_in), og_hbm, in_hbm(gate_pre), in_hbm(up_pre), weight, in_hbm(x_factor.T), in_hbm(dy_factor.T), in_hbm(h_factor.T))
    pq_mate = swap(pq, 1)

    def add(bits, following_bits, acc, features, head):
        rest = units - head.shape[0]
        return call(
            functools.partial(add_kernel, bits, following_bits),
            (held, pltpu.VMEM((2 * BLOCK, width), BF16)),
            [VMEM] * 3 + [ANY],
            [pltpu.VMEM((rest, width), BF16), dma((rest // PIECE,)), dma((2 * per_turn,))],
            12,
            per_product,
            4 * units * width,
            input_output_aliases={0: 0},
        )(acc, features, head, weight)

    acc, head = add(1, 2, acc, mate, head)
    near = pl.pallas_call(
        after_kernel,
        out_shape=pltpu.VMEM(near.shape, near.dtype),
        in_specs=[ANY, ANY],
        out_specs=ANY,
        input_output_aliases={0: 0},
        compiler_params=pltpu.CompilerParams(vmem_limit_bytes=MIB),
    )(near, head)
    far = swap(near, 1)
    acc, head = add(2, 3, acc, near, head)
    chip = call(chip_kernel, pltpu.VMEM(pq.shape, F32), [VMEM, VMEM, ANY], [], 1)(pq, pq_mate, head)
    chip_across = swap(chip, 2)
    rest = units - 2 * BLOCK
    q = call(
        functools.partial(far_kernel, 3),
        pltpu.VMEM((2 * rank, tokens), F32),
        [VMEM] * 3 + [ANY] + [VMEM] * 4,
        [pltpu.VMEM((rest, width), BF16), dma((rest // PIECE,))],
        10,
        per_product,
        2 * units * width,
    )(acc, far, head, weight, a, b, gate_factor.T, up_factor.T)
    share = call(gradients_kernel, pltpu.VMEM(((SEQS + 1) * rank, 2 * rank), F32), [VMEM] * 4, [], 4)(chip, chip_across, q, ph)
    chip_share = share + swap(share, 1)
    out = jax.ShapeDtypeStruct((SEQS, rank, rank), F32)
    return call(sum_kernel, (out, out, out), [VMEM] * 2, [], 4)(chip_share, swap(chip_share, 2))


def solution(mesh):
    def per_device(*arrays):
        (tokens, width), (units, rank) = arrays[1].shape, arrays[8].shape
        fits = (
            mesh.shape["tensor"] == 4
            and (tokens, rank) == (SEQS * LEN, LEN // 2)
            and width % 128 == 0
            and units % BLOCK == 0
            and units // BLOCK > 2
        )
        return tuple((fast if fits else plain)(*arrays))

    return jax.shard_map(
        per_device,
        mesh=mesh,
        in_specs=(P("dp", "tensor"),) * 4 + (P("tensor", None),) * 6,
        out_specs=(P("dp", None, None),) * 3,
        check_vma=False,
    )
```

```python
import functools

import jax
import jax.numpy as jnp
from jax import lax
from jax.experimental import pallas as pl
from jax.experimental.pallas import tpu as pltpu
from jax.sharding import PartitionSpec as P

SEQS = 2
LEN = 128
PIECE = 384
BLOCK = 1152
MIB = 1 << 20
ANY = pl.BlockSpec(memory_space=pl.ANY)
VMEM = pl.BlockSpec(memory_space=pltpu.VMEM)
BF16 = jnp.bfloat16
F32 = jnp.float32


def product(left, right):
    return jnp.dot(left, right, preferred_element_type=F32)


def rows_by_rows(left, right, precision=None):
    return lax.dot_general(
        left, right, (((1,), (1,)), ((), ())), precision=precision, preferred_element_type=F32
    )


def per_sequence(matrix):
    return matrix.reshape(SEQS, matrix.shape[0] // SEQS, matrix.shape[1])


def plain(x_in, out_grad, gate_pre, up_pre, down_weight, x_factor, gate_factor, up_factor, h_factor, dy_factor):
    hidden_grad = rows_by_rows(lax.all_gather(out_grad, "tensor", axis=1, tiled=True), down_weight)
    gate_val = gate_pre.astype(F32)
    up_val = up_pre.astype(F32)
    sigmoid_gate = jax.nn.sigmoid(gate_val)
    silu_gate = gate_val * sigmoid_gate
    hidden = (silu_gate * up_val).astype(BF16)
    d_gate = (hidden_grad * up_val * sigmoid_gate * (1.0 + gate_val * (1.0 - sigmoid_gate))).astype(BF16)
    d_up = (hidden_grad * silu_gate).astype(BF16)
    rows = [
        product(x_in, x_factor),
        product(d_gate, gate_factor),
        product(d_up, up_factor),
        product(hidden, h_factor),
        product(out_grad, dy_factor),
    ]
    totals = lax.psum(jnp.stack(rows), "tensor")
    p_x, q_gate, q_up, p_h, q_y = [per_sequence(totals[i]) for i in range(5)]
    highest = lax.Precision.HIGHEST
    return (
        jnp.einsum("sli,slj->sij", p_x, q_gate, precision=highest),
        jnp.einsum("sli,slj->sij", p_x, q_up, precision=highest),
        jnp.einsum("sli,slj->sij", p_h, q_y, precision=highest),
    )


def weight_copies(w_hbm, owner, first_row, dst, sems):
    width = dst.shape[1]
    columns = pl.ds(pl.multiple_of(owner * width, 128), width)
    return [
        pltpu.make_async_copy(
            w_hbm.at[pl.ds(pl.multiple_of(first_row + k * PIECE, PIECE), PIECE), columns],
            dst.at[pl.ds(k * PIECE, PIECE)],
            sems.at[k],
        )
        for k in range(dst.shape[0] // PIECE)
    ]


def start(copies):
    for copy in copies:
        copy.start()


def wait(copies):
    for copy in copies:
        copy.wait()


def rows(i):
    return pl.ds(pl.multiple_of(i * BLOCK, BLOCK), BLOCK)


def chip_features_kernel(x_hbm, og_hbm, mate_ref, gate_hbm, up_hbm, w_hbm, xf_hbm, yf_hbm, hf_hbm,
                         acc_ref, a_ref, b_ref, ph_ref, pq_ref, next_ref,
                         x_v, og_v, gate_v, up_v, w_v, xf_v, yf_v, hf_v, sems, gate_sems, up_sems, w_sems, next_sems):
    me = lax.axis_index("tensor")
    width = og_hbm.shape[1]
    units = acc_ref.shape[1]
    rank = ph_ref.shape[1]
    turns = units // BLOCK
    mine = pl.ds(pl.multiple_of(me % 2 * width, 128), width)
    theirs = pl.ds(pl.multiple_of((me + 1) % 2 * width, 128), width)

    def gate_up(i):
        slot = i % 2
        return [
            pltpu.make_async_copy(gate_hbm.at[:, rows(i)], gate_v.at[slot], gate_sems.at[i]),
            pltpu.make_async_copy(up_hbm.at[:, rows(i)], up_v.at[slot], up_sems.at[i]),
        ]

    def weights(i):
        return weight_copies(w_hbm, me // 2, i * BLOCK, w_v.at[i % 2], w_sems.at[i])

    def elementwise(i):
        wait(gate_up(i))
        at = rows(i)
        slot = i % 2
        g = gate_v[slot].astype(F32)
        u = up_v[slot].astype(F32)
        s = 0.5 * jnp.tanh(0.5 * g) + 0.5
        silu = g * s
        a_ref[:, at] = u * s * ((1.0 + g) - silu)
        b_ref[:, at] = silu
        ph_ref[...] += rows_by_rows((silu * u).astype(BF16), hf_v[:, at])

    def multiply(i):
        acc_ref[:, rows(i)] = rows_by_rows(og_v[...], w_v[i % 2])

    pairs = ((og_hbm, og_v.at[:, mine]), (hf_hbm, hf_v), (x_hbm, x_v), (xf_hbm, xf_v), (yf_hbm, yf_v))
    small = [pltpu.make_async_copy(src, dst, sems.at[i]) for i, (src, dst) in enumerate(pairs)]
    following = weight_copies(w_hbm, me ^ 2, 0, next_ref, next_sems)

    start(gate_up(0))
    start(small[:2])
    start(weights(0))
    start(gate_up(1))
    start(weights(1))
    start(small[2:])
    ph_ref[...] = jnp.zeros_like(ph_ref)
    og_v[:, theirs] = mate_ref[...]
    wait(small[:2])
    elementwise(0)

    @pl.loop(0, turns - 1)
    def _(i):
        @pl.when(i + 2 < turns)
        def _():
            start(gate_up(i + 2))

        wait(weights(i))
        multiply(i)

        @pl.when(i + 2 < turns)
        def _():
            start(weights(i + 2))

        @pl.when(i + 2 == turns)
        def _():
            start(following)

        elementwise(i + 1)

    wait(small[2:])
    pq_ref[:rank] = rows_by_rows(xf_v[...], x_v[...])
    pq_ref[rank:] = rows_by_rows(yf_v[...], og_v[:, mine])
    wait(weights(turns - 1))
    multiply(turns - 1)
    wait(following)


def add_kernel(bits, following_bits, acc_in, og_ref, head_ref, w_hbm, acc_ref, next_ref, w_v, sems, next_sems):
    me = lax.axis_index("tensor")
    first = head_ref.shape[0]
    turns = w_v.shape[0] // BLOCK

    def weights(i):
        return weight_copies(w_hbm, me ^ bits, first + i * BLOCK, w_v.at[rows(i)], sems.at[i])

    following = weight_copies(w_hbm, me ^ following_bits, 0, next_ref, next_sems)
    for i in range(turns):
        start(weights(i))
    start(following)

    def add(at, block):
        acc_ref[:, at] = acc_in[:, at] + rows_by_rows(og_ref[...], block)

    @pl.loop(0, first // BLOCK)
    def _(i):
        add(rows(i), head_ref[rows(i)])

    @pl.loop(0, turns)
    def _(i):
        wait(weights(i))
        add(rows(first // BLOCK + i), w_v[rows(i)])

    wait(following)


def far_kernel(bits, acc_ref, og_ref, head_ref, w_hbm, a_ref, b_ref, gf_hbm, uf_hbm, gate_ref, up_ref, w_v, gf_ref, uf_ref,
               sems, factor_sems):
    me = lax.axis_index("tensor")
    first = head_ref.shape[0]
    turns = w_v.shape[0] // BLOCK

    def weights(i):
        return weight_copies(w_hbm, me ^ bits, first + i * BLOCK, w_v.at[rows(i)], sems.at[i])

    factors = [
        pltpu.make_async_copy(src, dst, factor_sems.at[k]) for k, (src, dst) in enumerate(((gf_hbm, gf_ref), (uf_hbm, uf_ref)))
    ]
    start(factors)
    for i in range(turns):
        start(weights(i))
    gate_ref[...] = jnp.zeros_like(gate_ref)
    up_ref[...] = jnp.zeros_like(up_ref)

    def add(at, block):
        hidden_grad = acc_ref[:, at] + rows_by_rows(og_ref[...], block)
        gate_ref[...] += rows_by_rows((hidden_grad * a_ref[:, at]).astype(BF16), gf_ref[:, at])
        up_ref[...] += rows_by_rows((hidden_grad * b_ref[:, at]).astype(BF16), uf_ref[:, at])

    @pl.loop(0, first // BLOCK)
    def _(i):
        @pl.when(i == 0)
        def _():
            wait(factors)

        add(rows(i), head_ref[rows(i)])

    @pl.loop(0, turns)
    def _(i):
        wait(weights(i))
        add(rows(first // BLOCK + i), w_v[rows(i)])


def after_kernel(array_ref, token_ref, same_ref):
    pass


def chip_kernel(mine_ref, theirs_ref, token_ref, chip_ref):
    chip_ref[...] = mine_ref[...] + theirs_ref[...]


def gradients_kernel(chip_ref, other_ref, gate_ref, up_ref, ph_ref, share_ref):
    rank = ph_ref.shape[1]
    total = chip_ref[...] + other_ref[...]

    def columns(left, right):
        return jnp.dot(left, right, precision=lax.Precision.HIGHEST, preferred_element_type=F32)

    for s in range(SEQS):
        at = slice(s * LEN, (s + 1) * LEN)
        out = slice(s * rank, (s + 1) * rank)
        share_ref[out, :rank] = columns(total[:rank, at], gate_ref[at])
        share_ref[out, rank:] = columns(total[:rank, at], up_ref[at])
        share_ref[SEQS * rank :, out] = columns(total[rank:, at], ph_ref[at]).T


def sum_kernel(mine_ref, theirs_ref, gate_ref, up_ref, down_ref):
    rank = gate_ref.shape[1]
    total = mine_ref[...] + theirs_ref[...]
    for s in range(SEQS):
        gate_ref[s] = total[s * rank : (s + 1) * rank, :rank]
        up_ref[s] = total[s * rank : (s + 1) * rank, rank:]
        down_ref[s] = total[SEQS * rank :, s * rank : (s + 1) * rank]


def fast(x_in, out_grad, gate_pre, up_pre, down_weight, x_factor, gate_factor, up_factor, h_factor, dy_factor):
    tokens, width = out_grad.shape
    units, rank = h_factor.shape
    dma = pltpu.SemaphoreType.DMA

    def in_hbm(array):
        return pltpu.with_memory_space_constraint(array, pltpu.HBM)

    def swap(array, bits):
        return lax.ppermute(array, "tensor", [(i, i ^ bits) for i in range(4)])

    def call(kernel, out_shape, in_specs, scratch, mib, flops=0, moved=0, **kwargs):
        several = isinstance(out_shape, tuple)
        return pl.pallas_call(
            kernel,
            out_shape=out_shape,
            in_specs=in_specs,
            out_specs=(VMEM,) * len(out_shape) if several else VMEM,
            scratch_shapes=list(scratch),
            compiler_params=pltpu.CompilerParams(vmem_limit_bytes=mib * MIB),
            cost_estimate=pl.CostEstimate(flops=flops, bytes_accessed=moved, transcendentals=0),
            **kwargs,
        )

    held = pltpu.VMEM((tokens, units), F32)
    per_product = 2 * tokens * width * units
    turns, per_turn = units // BLOCK, BLOCK // PIECE
    first = turns // 2 * BLOCK
    rest = units - first
    narrow = pltpu.VMEM((tokens, rank), F32)
    head = pltpu.VMEM((first, width), BF16)
    weight = in_hbm(down_weight)

    near = swap(out_grad, 2)
    mate = swap(out_grad, 1)
    acc, a, b, ph, pq, w_head = call(
        chip_features_kernel,
        (held, held, held, narrow, pltpu.VMEM((2 * rank, tokens), F32), head),
        [ANY] * 2 + [VMEM] + [ANY] * 6,
        [
            pltpu.VMEM((tokens, width), BF16),
            pltpu.VMEM((tokens, 2 * width), BF16),
            pltpu.VMEM((2, tokens, BLOCK), BF16),
            pltpu.VMEM((2, tokens, BLOCK), BF16),
            pltpu.VMEM((2, BLOCK, 2 * width), BF16),
            pltpu.VMEM((rank, width), BF16),
            pltpu.VMEM((rank, width), BF16),
            pltpu.VMEM((rank, units), BF16),
            dma((5,)),
            dma((turns,)),
            dma((turns,)),
            dma((turns, per_turn)),
            dma((first // PIECE,)),
        ],
        24,
        2 * per_product,
        2 * units * (2 * width + 2 * tokens),
    )(
        in_hbm(x_in),
        in_hbm(out_grad),
        mate,
        in_hbm(gate_pre),
        in_hbm(up_pre),
        weight,
        in_hbm(x_factor.T),
        in_hbm(dy_factor.T),
        in_hbm(h_factor.T),
    )
    pq_mate = swap(pq, 1)

    near = pl.pallas_call(
        after_kernel,
        out_shape=pltpu.VMEM(near.shape, near.dtype),
        in_specs=[ANY, ANY],
        out_specs=ANY,
        input_output_aliases={0: 0},
        compiler_params=pltpu.CompilerParams(vmem_limit_bytes=MIB),
    )(near, w_head)
    far = swap(near, 1)
    acc, w_head = call(
        functools.partial(add_kernel, 2, 3),
        (held, head),
        [VMEM] * 3 + [ANY],
        [pltpu.VMEM((rest, width), BF16), dma((rest // BLOCK, per_turn)), dma((first // PIECE,))],
        10,
        per_product,
        2 * units * width,
        input_output_aliases={0: 0},
    )(acc, near, w_head, weight)
    chip = call(chip_kernel, pltpu.VMEM(pq.shape, F32), [VMEM, VMEM, ANY], [], 1)(pq, pq_mate, w_head)
    chip_across = swap(chip, 2)
    q_gate, q_up = call(
        functools.partial(far_kernel, 3),
        (narrow, narrow),
        [VMEM] * 3 + [ANY] + [VMEM] * 2 + [ANY] * 2,
        [
            pltpu.VMEM((rest, width), BF16),
            pltpu.VMEM((rank, units), BF16),
            pltpu.VMEM((rank, units), BF16),
            dma((rest // BLOCK, per_turn)),
            dma((2,)),
        ],
        10,
        per_product,
        2 * units * width,
    )(acc, far, w_head, weight, a, b, in_hbm(gate_factor.T), in_hbm(up_factor.T))
    share = call(gradients_kernel, pltpu.VMEM(((SEQS + 1) * rank, 2 * rank), F32), [VMEM] * 5, [], 4)(
        chip, chip_across, q_gate, q_up, ph
    )
    chip_share = share + swap(share, 1)
    out = jax.ShapeDtypeStruct((SEQS, rank, rank), F32)
    return call(sum_kernel, (out, out, out), [VMEM] * 2, [], 4)(chip_share, swap(chip_share, 2))


def solution(mesh):
    def per_device(*arrays):
        (tokens, width), (units, rank) = arrays[1].shape, arrays[8].shape
        fits = (
            mesh.shape["tensor"] == 4
            and (tokens, rank) == (SEQS * LEN, LEN // 2)
            and width % 128 == 0
            and units % BLOCK == 0
            and units // BLOCK > 3
        )
        return tuple((fast if fits else plain)(*arrays))

    return jax.shard_map(
        per_device,
        mesh=mesh,
        in_specs=(P("dp", "tensor"),) * 4 + (P("tensor", None),) * 6,
        out_specs=(P("dp", None, None),) * 3,
        check_vma=False,
    )
```

```python
import functools

import jax
import jax.numpy as jnp
from jax import lax
from jax.experimental import pallas as pl
from jax.experimental.pallas import tpu as pltpu
from jax.sharding import PartitionSpec as P

SEQS = 2
LEN = 128
BLOCK = 1152
CHIP_BLOCK = 768
AHEAD = 2
PARTS = 2
SUMS = 3
MIB = 1 << 20
ANY = pl.BlockSpec(memory_space=pl.ANY)
VMEM = pl.BlockSpec(memory_space=pltpu.VMEM)
BF16 = jnp.bfloat16
F32 = jnp.float32


def product(left, right):
    return jnp.dot(left, right, preferred_element_type=F32)


def rows_by_rows(left, right, precision=None):
    return lax.dot_general(
        left, right, (((1,), (1,)), ((), ())), precision=precision, preferred_element_type=F32
    )


def per_sequence(matrix):
    return matrix.reshape(SEQS, matrix.shape[0] // SEQS, matrix.shape[1])


def plain(x_in, out_grad, gate_pre, up_pre, down_weight, x_factor, gate_factor, up_factor, h_factor, dy_factor):
    hidden_grad = rows_by_rows(lax.all_gather(out_grad, "tensor", axis=1, tiled=True), down_weight)
    gate_val = gate_pre.astype(F32)
    up_val = up_pre.astype(F32)
    sigmoid_gate = jax.nn.sigmoid(gate_val)
    silu_gate = gate_val * sigmoid_gate
    hidden = (silu_gate * up_val).astype(BF16)
    d_gate = (hidden_grad * up_val * sigmoid_gate * (1.0 + gate_val * (1.0 - sigmoid_gate))).astype(BF16)
    d_up = (hidden_grad * silu_gate).astype(BF16)
    rows = [
        product(x_in, x_factor),
        product(d_gate, gate_factor),
        product(d_up, up_factor),
        product(hidden, h_factor),
        product(out_grad, dy_factor),
    ]
    totals = lax.psum(jnp.stack(rows), "tensor")
    p_x, q_gate, q_up, p_h, q_y = [per_sequence(totals[i]) for i in range(5)]
    highest = lax.Precision.HIGHEST
    return (
        jnp.einsum("sli,slj->sij", p_x, q_gate, precision=highest),
        jnp.einsum("sli,slj->sij", p_x, q_up, precision=highest),
        jnp.einsum("sli,slj->sij", p_h, q_y, precision=highest),
    )


class Step:
    def __init__(self, owner, width, block, w_hbm):
        self.owner, self.width, self.block, self.w_hbm = owner, width, block, w_hbm

    def units(self, i):
        return pl.ds(pl.multiple_of(i * self.block, self.block), self.block)

    def copies(self, i, dst, sems):
        columns = pl.ds(pl.multiple_of(self.owner * self.width, 128), self.width)
        part = self.block // PARTS
        return [
            pltpu.make_async_copy(
                self.w_hbm.at[pl.ds(pl.multiple_of(i * self.block + k * part, part), part), columns],
                dst.at[pl.ds(k * part, part)],
                sems.at[k],
            )
            for k in range(PARTS)
        ]


def start(copies):
    for copy in copies:
        copy.start()


def wait(copies):
    for copy in copies:
        copy.wait()


def stream(step, following, blocks, head, w_v, next_head, sems, body):
    heads = head.shape[0]
    slots = w_v.shape[0]

    def copies(j):
        return step.copies(j, w_v.at[(j - heads) % slots], sems.at[j])

    def next_copies(j):
        return following.copies(j, next_head.at[j], sems.at[blocks + j])

    last = blocks + (0 if following is None else next_head.shape[0])

    def begin(j):
        @pl.when(j < blocks)
        def _():
            start(copies(j))

        if following is not None:

            @pl.when((j >= blocks) & (j < last))
            def _():
                start(next_copies(j - blocks))

    for j in range(heads, AHEAD):
        start(copies(j))

    @pl.loop(0, heads)
    def _(i):
        begin(i + AHEAD)
        body(i, head.at[i])

    @pl.loop(heads, blocks)
    def _(i):
        begin(i + AHEAD)
        wait(copies(i))
        body(i, w_v.at[(i - heads) % slots])

    for j in range(blocks + AHEAD, last):
        start(next_copies(j - blocks))
    for j in range(last - blocks):
        wait(next_copies(j))


def project(sums_ref, rows, factor):
    parts = sums_ref.shape[0]
    part = factor.shape[1] // parts
    for k in range(parts):
        at = slice(k * part, (k + 1) * part)
        sums_ref[k] += rows_by_rows(rows[:, at], factor[:, at])


def elementwise_kernel(x_hbm, og_hbm, gate_hbm, up_hbm, w_hbm, xf_hbm, yf_hbm, hf_hbm,
                       a_ref, b_ref, ph_ref, pq_ref, head_ref, og_v,
                       x_v, gate_v, up_v, xf_v, yf_v, hf_v, sums_v, sems, gate_sems, up_sems, w_sems):
    tokens, units = a_ref.shape
    rank = ph_ref.shape[1]
    turns = units // BLOCK

    def at(i):
        return pl.ds(pl.multiple_of(i * BLOCK, BLOCK), BLOCK)

    def gate_up(i):
        return [
            pltpu.make_async_copy(gate_hbm.at[:, at(i)], gate_v.at[i], gate_sems.at[i]),
            pltpu.make_async_copy(up_hbm.at[:, at(i)], up_v.at[i], up_sems.at[i]),
        ]

    pairs = ((hf_hbm, hf_v), (og_hbm, og_v), (x_hbm, x_v), (xf_hbm, xf_v), (yf_hbm, yf_v))
    small = [pltpu.make_async_copy(src, dst, sems.at[i]) for i, (src, dst) in enumerate(pairs)]
    following = Step(lax.axis_index("tensor") // 2, head_ref.shape[2], head_ref.shape[1], w_hbm)
    heads = head_ref.shape[0]

    start(gate_up(0))
    start(small[:1])
    start(gate_up(1))
    start(small[1:])
    sums_v[...] = jnp.zeros_like(sums_v)
    wait(gate_up(0))
    wait(small[:1])

    @pl.loop(0, turns)
    def _(i):
        @pl.when(i + 2 < turns)
        def _():
            start(gate_up(i + 2))

        @pl.when(i < heads)
        def _():
            start(following.copies(i, head_ref.at[i], w_sems.at[i]))

        @pl.when(i > 0)
        def _():
            wait(gate_up(i))

        g = gate_v[i].astype(F32)
        u = up_v[i].astype(F32)
        s = 0.5 * jnp.tanh(0.5 * g) + 0.5
        silu = g * s
        a_ref[:, at(i)] = u * s * ((1.0 + g) - silu)
        b_ref[:, at(i)] = silu
        project(sums_v, (silu * u).astype(BF16), hf_v.at[:, at(i)])

    wait(small[1:])
    pq_ref[:rank] = rows_by_rows(xf_v[...], x_v[...])
    pq_ref[rank:] = rows_by_rows(yf_v[...], og_v[...])
    ph_ref[...] = jnp.sum(sums_v[...], axis=0)
    for i in range(heads):
        wait(following.copies(i, head_ref.at[i], w_sems.at[i]))


def chip_features_kernel(own_ref, mate_ref, head_ref, w_hbm, acc_ref, next_ref, og_v, w_v, sems):
    me = lax.axis_index("tensor")
    width = own_ref.shape[1]
    step = Step(me // 2, 2 * width, w_v.shape[1], w_hbm)
    following = Step(me ^ 2, width, next_ref.shape[1], w_hbm)
    mine = pl.ds(pl.multiple_of(me % 2 * width, 128), width)
    theirs = pl.ds(pl.multiple_of((me + 1) % 2 * width, 128), width)
    og_v[:, mine] = own_ref[...]
    og_v[:, theirs] = mate_ref[...]

    def body(i, weights):
        acc_ref[:, step.units(i)] = rows_by_rows(og_v[...], weights[...])

    stream(step, following, acc_ref.shape[1] // step.block, head_ref, w_v, next_ref, sems, body)


def add_kernel(bits, following_bits, acc_in, og_ref, head_ref, w_hbm, acc_ref, next_ref, w_v, sems):
    me = lax.axis_index("tensor")
    _, block, width = w_v.shape
    step = Step(me ^ bits, width, block, w_hbm)
    following = Step(me ^ following_bits, width, block, w_hbm)

    def body(i, weights):
        at = step.units(i)
        acc_ref[:, at] = acc_in[:, at] + rows_by_rows(og_ref[...], weights[...])

    stream(step, following, acc_in.shape[1] // block, head_ref, w_v, next_ref, sems, body)


def far_kernel(bits, acc_ref, og_ref, head_ref, w_hbm, a_ref, b_ref, gf_hbm, uf_hbm, gate_ref, up_ref,
               w_v, gf_ref, uf_ref, gate_v, up_v, sems, factor_sems):
    _, block, width = w_v.shape
    step = Step(lax.axis_index("tensor") ^ bits, width, block, w_hbm)
    factors = [
        pltpu.make_async_copy(src, dst, factor_sems.at[k]) for k, (src, dst) in enumerate(((gf_hbm, gf_ref), (uf_hbm, uf_ref)))
    ]
    start(factors)
    gate_v[...] = jnp.zeros_like(gate_v)
    up_v[...] = jnp.zeros_like(up_v)

    def body(i, weights):
        at = step.units(i)
        hidden_grad = acc_ref[:, at] + rows_by_rows(og_ref[...], weights[...])

        @pl.when(i == 0)
        def _():
            wait(factors)

        project(gate_v, (hidden_grad * a_ref[:, at]).astype(BF16), gf_ref.at[:, at])
        project(up_v, (hidden_grad * b_ref[:, at]).astype(BF16), uf_ref.at[:, at])

    stream(step, None, acc_ref.shape[1] // block, head_ref, w_v, None, sems, body)
    gate_ref[...] = jnp.sum(gate_v[...], axis=0)
    up_ref[...] = jnp.sum(up_v[...], axis=0)


def after_kernel(array_ref, token_ref, same_ref):
    pass


def chip_kernel(mine_ref, theirs_ref, token_ref, chip_ref):
    chip_ref[...] = mine_ref[...] + theirs_ref[...]


def gradients_kernel(chip_ref, other_ref, gate_ref, up_ref, ph_ref, share_ref):
    rank = ph_ref.shape[1]
    total = chip_ref[...] + other_ref[...]

    def columns(left, right):
        return jnp.dot(left, right, precision=lax.Precision.HIGHEST, preferred_element_type=F32)

    for s in range(SEQS):
        at = slice(s * LEN, (s + 1) * LEN)
        out = slice(s * rank, (s + 1) * rank)
        share_ref[out, :rank] = columns(total[:rank, at], gate_ref[at])
        share_ref[out, rank:] = columns(total[:rank, at], up_ref[at])
        share_ref[SEQS * rank :, out] = columns(total[rank:, at], ph_ref[at]).T


def sum_kernel(mine_ref, theirs_ref, gate_ref, up_ref, down_ref):
    rank = gate_ref.shape[1]
    total = mine_ref[...] + theirs_ref[...]
    for s in range(SEQS):
        gate_ref[s] = total[s * rank : (s + 1) * rank, :rank]
        up_ref[s] = total[s * rank : (s + 1) * rank, rank:]
        down_ref[s] = total[SEQS * rank :, s * rank : (s + 1) * rank]


def fast(x_in, out_grad, gate_pre, up_pre, down_weight, x_factor, gate_factor, up_factor, h_factor, dy_factor):
    tokens, width = out_grad.shape
    units, rank = h_factor.shape
    dma = pltpu.SemaphoreType.DMA

    def in_hbm(array):
        return pltpu.with_memory_space_constraint(array, pltpu.HBM)

    def swap(array, bits):
        return lax.ppermute(array, "tensor", [(i, i ^ bits) for i in range(4)])

    def call(kernel, out_shape, in_specs, scratch, mib, flops=0, moved=0, **kwargs):
        several = isinstance(out_shape, tuple)
        return pl.pallas_call(
            kernel,
            out_shape=out_shape,
            in_specs=in_specs,
            out_specs=(VMEM,) * len(out_shape) if several else VMEM,
            scratch_shapes=list(scratch),
            compiler_params=pltpu.CompilerParams(vmem_limit_bytes=mib * MIB),
            cost_estimate=pl.CostEstimate(flops=flops, bytes_accessed=moved, transcendentals=0),
            **kwargs,
        )

    held = pltpu.VMEM((tokens, units), F32)
    per_product = 2 * tokens * width * units
    turns = units // BLOCK
    narrow = pltpu.VMEM((tokens, rank), F32)
    sums = pltpu.VMEM((SUMS, tokens, rank), F32)
    weight = in_hbm(down_weight)

    def blocks(count):
        return pltpu.VMEM((count, BLOCK, width), BF16)

    def chip_blocks(count):
        return pltpu.VMEM((count, CHIP_BLOCK, 2 * width), BF16)

    near = swap(out_grad, 2)
    mate = swap(out_grad, 1)
    a, b, ph, pq, head, own = call(
        elementwise_kernel,
        (held, held, narrow, pltpu.VMEM((2 * rank, tokens), F32), chip_blocks(2), pltpu.VMEM((tokens, width), BF16)),
        [ANY] * 8,
        [
            pltpu.VMEM((tokens, width), BF16),
            pltpu.VMEM((turns, tokens, BLOCK), BF16),
            pltpu.VMEM((turns, tokens, BLOCK), BF16),
            pltpu.VMEM((rank, width), BF16),
            pltpu.VMEM((rank, width), BF16),
            pltpu.VMEM((rank, units), BF16),
            sums,
            dma((5,)),
            dma((turns,)),
            dma((turns,)),
            dma((2, PARTS)),
        ],
        14,
        per_product // 4,
        4 * units * tokens,
    )(
        in_hbm(x_in),
        in_hbm(out_grad),
        in_hbm(gate_pre),
        in_hbm(up_pre),
        weight,
        in_hbm(x_factor.T),
        in_hbm(dy_factor.T),
        in_hbm(h_factor.T),
    )
    pq_mate = swap(pq, 1)
    acc, head = call(
        chip_features_kernel,
        (held, blocks(2)),
        [VMEM] * 3 + [ANY],
        [pltpu.VMEM((tokens, 2 * width), BF16), chip_blocks(AHEAD + 1), dma((units // CHIP_BLOCK + 2, PARTS))],
        16,
        2 * per_product,
        4 * units * width,
    )(own, mate, head, weight)

    near = pl.pallas_call(
        after_kernel,
        out_shape=pltpu.VMEM(near.shape, near.dtype),
        in_specs=[ANY, ANY],
        out_specs=ANY,
        input_output_aliases={0: 0},
        compiler_params=pltpu.CompilerParams(vmem_limit_bytes=MIB),
    )(near, head)
    far = swap(near, 1)
    acc, head = call(
        functools.partial(add_kernel, 2, 3),
        (held, blocks(1)),
        [VMEM] * 3 + [ANY],
        [blocks(AHEAD), dma((turns + 1, PARTS))],
        10,
        per_product,
        2 * units * width,
        input_output_aliases={0: 0},
    )(acc, near, head, weight)
    chip = call(chip_kernel, pltpu.VMEM(pq.shape, F32), [VMEM, VMEM, ANY], [], 1)(pq, pq_mate, head)
    chip_across = swap(chip, 2)
    factor = pltpu.VMEM((rank, units), BF16)
    q_gate, q_up = call(
        functools.partial(far_kernel, 3),
        (narrow, narrow),
        [VMEM] * 3 + [ANY] + [VMEM] * 2 + [ANY] * 2,
        [blocks(AHEAD + 1), factor, factor, sums, sums, dma((turns, PARTS)), dma((2,))],
        16,
        per_product,
        2 * units * width,
    )(acc, far, head, weight, a, b, in_hbm(gate_factor.T), in_hbm(up_factor.T))
    share = call(gradients_kernel, pltpu.VMEM(((SEQS + 1) * rank, 2 * rank), F32), [VMEM] * 5, [], 4)(
        chip, chip_across, q_gate, q_up, ph
    )
    chip_share = share + swap(share, 1)
    out = jax.ShapeDtypeStruct((SEQS, rank, rank), F32)
    return call(sum_kernel, (out, out, out), [VMEM] * 2, [], 4)(chip_share, swap(chip_share, 2))


def solution(mesh):
    def per_device(*arrays):
        (tokens, width), (units, rank) = arrays[1].shape, arrays[8].shape
        fits = (
            mesh.shape["tensor"] == 4
            and (tokens, rank) == (SEQS * LEN, LEN // 2)
            and width % 128 == 0
            and units % BLOCK == 0
            and units % CHIP_BLOCK == 0
            and units // BLOCK > 3
        )
        return tuple((fast if fits else plain)(*arrays))

    return jax.shard_map(
        per_device,
        mesh=mesh,
        in_specs=(P("dp", "tensor"),) * 4 + (P("tensor", None),) * 6,
        out_specs=(P("dp", None, None),) * 3,
        check_vma=False,
    )
```

```python
import functools

import jax
import jax.numpy as jnp
from jax import lax
from jax.experimental import pallas as pl
from jax.experimental.pallas import tpu as pltpu
from jax.sharding import PartitionSpec as P

SEQS = 2
LEN = 128
BLOCK = 1152
CHIP_BLOCK = 768
AHEAD = 2
PARTS = 2
MIB = 1 << 20
ANY = pl.BlockSpec(memory_space=pl.ANY)
VMEM = pl.BlockSpec(memory_space=pltpu.VMEM)
BF16 = jnp.bfloat16
F32 = jnp.float32


def product(left, right):
    return jnp.dot(left, right, preferred_element_type=F32)


def rows_by_rows(left, right, precision=None):
    return lax.dot_general(
        left, right, (((1,), (1,)), ((), ())), precision=precision, preferred_element_type=F32
    )


def per_sequence(matrix):
    return matrix.reshape(SEQS, matrix.shape[0] // SEQS, matrix.shape[1])


def plain(x_in, out_grad, gate_pre, up_pre, down_weight, x_factor, gate_factor, up_factor, h_factor, dy_factor):
    hidden_grad = rows_by_rows(lax.all_gather(out_grad, "tensor", axis=1, tiled=True), down_weight)
    gate_val = gate_pre.astype(F32)
    up_val = up_pre.astype(F32)
    sigmoid_gate = jax.nn.sigmoid(gate_val)
    silu_gate = gate_val * sigmoid_gate
    hidden = (silu_gate * up_val).astype(BF16)
    d_gate = (hidden_grad * up_val * sigmoid_gate * (1.0 + gate_val * (1.0 - sigmoid_gate))).astype(BF16)
    d_up = (hidden_grad * silu_gate).astype(BF16)
    rows = [
        product(x_in, x_factor),
        product(d_gate, gate_factor),
        product(d_up, up_factor),
        product(hidden, h_factor),
        product(out_grad, dy_factor),
    ]
    totals = lax.psum(jnp.stack(rows), "tensor")
    p_x, q_gate, q_up, p_h, q_y = [per_sequence(totals[i]) for i in range(5)]
    highest = lax.Precision.HIGHEST
    return (
        jnp.einsum("sli,slj->sij", p_x, q_gate, precision=highest),
        jnp.einsum("sli,slj->sij", p_x, q_up, precision=highest),
        jnp.einsum("sli,slj->sij", p_h, q_y, precision=highest),
    )


class Step:
    def __init__(self, owner, width, block, w_hbm):
        self.owner, self.width, self.block, self.w_hbm = owner, width, block, w_hbm

    def units(self, i):
        return pl.ds(pl.multiple_of(i * self.block, self.block), self.block)

    def copies(self, i, dst, sems):
        columns = pl.ds(pl.multiple_of(self.owner * self.width, 128), self.width)
        part = self.block // PARTS
        return [
            pltpu.make_async_copy(
                self.w_hbm.at[pl.ds(pl.multiple_of(i * self.block + k * part, part), part), columns],
                dst.at[pl.ds(k * part, part)],
                sems.at[k],
            )
            for k in range(PARTS)
        ]


def start(copies):
    for copy in copies:
        copy.start()


def wait(copies):
    for copy in copies:
        copy.wait()


def stream(step, following, blocks, head, w_v, next_head, sems, body):
    heads = head.shape[0]
    slots = w_v.shape[0]

    def copies(j):
        return step.copies(j, w_v.at[(j - heads) % slots], sems.at[j])

    def next_copies(j):
        return following.copies(j, next_head.at[j], sems.at[blocks + j])

    last = blocks + (0 if following is None else next_head.shape[0])

    def begin(j):
        @pl.when(j < blocks)
        def _():
            start(copies(j))

        if following is not None:

            @pl.when((j >= blocks) & (j < last))
            def _():
                start(next_copies(j - blocks))

    for j in range(heads, AHEAD):
        start(copies(j))

    @pl.loop(0, heads)
    def _(i):
        begin(i + AHEAD)
        body(i, head.at[i])

    @pl.loop(heads, blocks)
    def _(i):
        begin(i + AHEAD)
        wait(copies(i))
        body(i, w_v.at[(i - heads) % slots])

    for j in range(blocks + AHEAD, last):
        start(next_copies(j - blocks))
    for j in range(last - blocks):
        wait(next_copies(j))


def elementwise_kernel(x_hbm, og_hbm, gate_hbm, up_hbm, w_hbm, xf_hbm, yf_hbm, hf_hbm,
                       a_ref, b_ref, ph_ref, pq_ref, head_ref, own_ref,
                       x_v, og_v, gate_v, up_v, xf_v, yf_v, hf_v, sems, gate_sems, up_sems, w_sems):
    units = a_ref.shape[0]
    rank = ph_ref.shape[0]
    turns = units // BLOCK

    def at(i):
        return pl.ds(pl.multiple_of(i * BLOCK, BLOCK), BLOCK)

    def gate_up(i):
        return [
            pltpu.make_async_copy(gate_hbm.at[:, at(i)], gate_v.at[i], gate_sems.at[i]),
            pltpu.make_async_copy(up_hbm.at[:, at(i)], up_v.at[i], up_sems.at[i]),
        ]

    pairs = ((hf_hbm, hf_v), (og_hbm, og_v), (x_hbm, x_v), (xf_hbm, xf_v), (yf_hbm, yf_v))
    small = [pltpu.make_async_copy(src, dst, sems.at[i]) for i, (src, dst) in enumerate(pairs)]
    following = Step(lax.axis_index("tensor") // 2, head_ref.shape[2], head_ref.shape[1], w_hbm)
    heads = head_ref.shape[0]

    start(gate_up(0))
    start(small[:1])
    start(gate_up(1))
    start(small[1:])
    ph_ref[...] = jnp.zeros_like(ph_ref)
    wait(gate_up(0))
    wait(small[:1])

    @pl.loop(0, turns)
    def _(i):
        @pl.when(i + 2 < turns)
        def _():
            start(gate_up(i + 2))

        @pl.when(i < heads)
        def _():
            start(following.copies(i, head_ref.at[i], w_sems.at[i]))

        @pl.when(i > 0)
        def _():
            wait(gate_up(i))

        g = gate_v[i].T.astype(F32)
        u = up_v[i].T.astype(F32)
        s = 0.5 * jnp.tanh(0.5 * g) + 0.5
        silu = g * s
        a_ref[at(i)] = u * s * ((1.0 + g) - silu)
        b_ref[at(i)] = silu
        ph_ref[...] += product(hf_v[:, at(i)], (silu * u).astype(BF16))

    wait(small[1:])
    pq_ref[:rank] = rows_by_rows(xf_v[...], x_v[...])
    own_ref[...] = og_v[...].T
    pq_ref[rank:] = product(yf_v[...], own_ref[...])
    for i in range(heads):
        wait(following.copies(i, head_ref.at[i], w_sems.at[i]))


def chip_features_kernel(own_ref, mate_ref, head_ref, w_hbm, acc_ref, next_ref, og_v, w_v, sems):
    me = lax.axis_index("tensor")
    width = own_ref.shape[0]
    step = Step(me // 2, 2 * width, w_v.shape[1], w_hbm)
    following = Step(me ^ 2, width, next_ref.shape[1], w_hbm)
    mine = pl.ds(pl.multiple_of(me % 2 * width, 128), width)
    theirs = pl.ds(pl.multiple_of((me + 1) % 2 * width, 128), width)
    og_v[mine] = own_ref[...]
    og_v[theirs] = mate_ref[...].T

    def body(i, weights):
        acc_ref[step.units(i)] = product(weights[...], og_v[...])

    stream(step, following, acc_ref.shape[0] // step.block, head_ref, w_v, next_ref, sems, body)


def add_kernel(bits, following_bits, acc_in, og_ref, head_ref, w_hbm, acc_ref, next_ref, og_v, w_v, sems):
    me = lax.axis_index("tensor")
    _, block, width = w_v.shape
    step = Step(me ^ bits, width, block, w_hbm)
    following = Step(me ^ following_bits, width, block, w_hbm)

    og_v[...] = og_ref[...].T

    def body(i, weights):
        at = step.units(i)
        acc_ref[at] = acc_in[at] + product(weights[...], og_v[...])

    stream(step, following, acc_in.shape[0] // block, head_ref, w_v, next_ref, sems, body)


def far_kernel(bits, acc_ref, og_ref, head_ref, w_hbm, a_ref, b_ref, gf_hbm, uf_hbm, gate_ref, up_ref,
               og_v, w_v, gf_ref, uf_ref, sems, factor_sems):
    _, block, width = w_v.shape
    step = Step(lax.axis_index("tensor") ^ bits, width, block, w_hbm)
    factors = [
        pltpu.make_async_copy(src, dst, factor_sems.at[k]) for k, (src, dst) in enumerate(((gf_hbm, gf_ref), (uf_hbm, uf_ref)))
    ]
    start(factors)
    gate_ref[...] = jnp.zeros_like(gate_ref)
    up_ref[...] = jnp.zeros_like(up_ref)
    og_v[...] = og_ref[...].T

    def body(i, weights):
        at = step.units(i)
        hidden_grad = acc_ref[at] + product(weights[...], og_v[...])

        @pl.when(i == 0)
        def _():
            wait(factors)

        gate_ref[...] += product(gf_ref[:, at], (hidden_grad * a_ref[at]).astype(BF16))
        up_ref[...] += product(uf_ref[:, at], (hidden_grad * b_ref[at]).astype(BF16))

    stream(step, None, acc_ref.shape[0] // block, head_ref, w_v, None, sems, body)


def after_kernel(array_ref, token_ref, same_ref):
    pass


def chip_kernel(mine_ref, theirs_ref, token_ref, chip_ref):
    chip_ref[...] = mine_ref[...] + theirs_ref[...]


def gradients_kernel(chip_ref, other_ref, gate_ref, up_ref, ph_ref, share_ref):
    rank = ph_ref.shape[0]
    total = chip_ref[...] + other_ref[...]
    highest = lax.Precision.HIGHEST
    for s in range(SEQS):
        at = slice(s * LEN, (s + 1) * LEN)
        out = slice(s * rank, (s + 1) * rank)
        share_ref[out, :rank] = rows_by_rows(total[:rank, at], gate_ref[:, at], highest)
        share_ref[out, rank:] = rows_by_rows(total[:rank, at], up_ref[:, at], highest)
        share_ref[SEQS * rank :, out] = rows_by_rows(ph_ref[:, at], total[rank:, at], highest)


def sum_kernel(mine_ref, theirs_ref, gate_ref, up_ref, down_ref):
    rank = gate_ref.shape[1]
    total = mine_ref[...] + theirs_ref[...]
    for s in range(SEQS):
        gate_ref[s] = total[s * rank : (s + 1) * rank, :rank]
        up_ref[s] = total[s * rank : (s + 1) * rank, rank:]
        down_ref[s] = total[SEQS * rank :, s * rank : (s + 1) * rank]


def fast(x_in, out_grad, gate_pre, up_pre, down_weight, x_factor, gate_factor, up_factor, h_factor, dy_factor):
    tokens, width = out_grad.shape
    units, rank = h_factor.shape
    dma = pltpu.SemaphoreType.DMA

    def in_hbm(array):
        return pltpu.with_memory_space_constraint(array, pltpu.HBM)

    def swap(array, bits):
        return lax.ppermute(array, "tensor", [(i, i ^ bits) for i in range(4)])

    def call(kernel, out_shape, in_specs, scratch, mib, flops=0, moved=0, **kwargs):
        several = isinstance(out_shape, tuple)
        return pl.pallas_call(
            kernel,
            out_shape=out_shape,
            in_specs=in_specs,
            out_specs=(VMEM,) * len(out_shape) if several else VMEM,
            scratch_shapes=list(scratch),
            compiler_params=pltpu.CompilerParams(vmem_limit_bytes=mib * MIB),
            cost_estimate=pl.CostEstimate(flops=flops, bytes_accessed=moved, transcendentals=0),
            **kwargs,
        )

    held = pltpu.VMEM((units, tokens), F32)
    per_product = 2 * tokens * width * units
    turns = units // BLOCK
    narrow = pltpu.VMEM((rank, tokens), F32)
    turned = pltpu.VMEM((width, tokens), BF16)
    weight = in_hbm(down_weight)

    def blocks(count):
        return pltpu.VMEM((count, BLOCK, width), BF16)

    def chip_blocks(count):
        return pltpu.VMEM((count, CHIP_BLOCK, 2 * width), BF16)

    near = swap(out_grad, 2)
    mate = swap(out_grad, 1)
    a, b, ph, pq, head, own = call(
        elementwise_kernel,
        (held, held, narrow, pltpu.VMEM((2 * rank, tokens), F32), chip_blocks(2), turned),
        [ANY] * 8,
        [
            pltpu.VMEM((tokens, width), BF16),
            pltpu.VMEM((tokens, width), BF16),
            pltpu.VMEM((turns, tokens, BLOCK), BF16),
            pltpu.VMEM((turns, tokens, BLOCK), BF16),
            pltpu.VMEM((rank, width), BF16),
            pltpu.VMEM((rank, width), BF16),
            pltpu.VMEM((rank, units), BF16),
            dma((5,)),
            dma((turns,)),
            dma((turns,)),
            dma((2, PARTS)),
        ],
        14,
        per_product // 4,
        4 * units * tokens,
    )(
        in_hbm(x_in),
        in_hbm(out_grad),
        in_hbm(gate_pre),
        in_hbm(up_pre),
        weight,
        in_hbm(x_factor.T),
        in_hbm(dy_factor.T),
        in_hbm(h_factor.T),
    )
    pq_mate = swap(pq, 1)
    acc, head = call(
        chip_features_kernel,
        (held, blocks(2)),
        [VMEM] * 3 + [ANY],
        [pltpu.VMEM((2 * width, tokens), BF16), chip_blocks(AHEAD + 1), dma((units // CHIP_BLOCK + 2, PARTS))],
        16,
        2 * per_product,
        4 * units * width,
    )(own, mate, head, weight)

    near = pl.pallas_call(
        after_kernel,
        out_shape=pltpu.VMEM(near.shape, near.dtype),
        in_specs=[ANY, ANY],
        out_specs=ANY,
        input_output_aliases={0: 0},
        compiler_params=pltpu.CompilerParams(vmem_limit_bytes=MIB),
    )(near, head)
    far = swap(near, 1)
    acc, head = call(
        functools.partial(add_kernel, 2, 3),
        (held, blocks(1)),
        [VMEM] * 3 + [ANY],
        [turned, blocks(AHEAD), dma((turns + 1, PARTS))],
        10,
        per_product,
        2 * units * width,
        input_output_aliases={0: 0},
    )(acc, near, head, weight)
    chip = call(chip_kernel, pltpu.VMEM(pq.shape, F32), [VMEM, VMEM, ANY], [], 1)(pq, pq_mate, head)
    chip_across = swap(chip, 2)
    factor = pltpu.VMEM((rank, units), BF16)
    q_gate, q_up = call(
        functools.partial(far_kernel, 3),
        (narrow, narrow),
        [VMEM] * 3 + [ANY] + [VMEM] * 2 + [ANY] * 2,
        [turned, blocks(AHEAD + 1), factor, factor, dma((turns, PARTS)), dma((2,))],
        16,
        per_product,
        2 * units * width,
    )(acc, far, head, weight, a, b, in_hbm(gate_factor.T), in_hbm(up_factor.T))
    share = call(gradients_kernel, pltpu.VMEM(((SEQS + 1) * rank, 2 * rank), F32), [VMEM] * 5, [], 4)(
        chip, chip_across, q_gate, q_up, ph
    )
    chip_share = share + swap(share, 1)
    out = jax.ShapeDtypeStruct((SEQS, rank, rank), F32)
    return call(sum_kernel, (out, out, out), [VMEM] * 2, [], 4)(chip_share, swap(chip_share, 2))


def solution(mesh):
    def per_device(*arrays):
        (tokens, width), (units, rank) = arrays[1].shape, arrays[8].shape
        fits = (
            mesh.shape["tensor"] == 4
            and (tokens, rank) == (SEQS * LEN, LEN // 2)
            and width % 128 == 0
            and units % BLOCK == 0
            and units % CHIP_BLOCK == 0
            and units // BLOCK > 3
        )
        return tuple((fast if fits else plain)(*arrays))

    return jax.shard_map(
        per_device,
        mesh=mesh,
        in_specs=(P("dp", "tensor"),) * 4 + (P("tensor", None),) * 6,
        out_specs=(P("dp", None, None),) * 3,
        check_vma=False,
    )
```

```python
import functools

import jax
import jax.numpy as jnp
from jax import lax
from jax.experimental import pallas as pl
from jax.experimental.pallas import tpu as pltpu
from jax.sharding import PartitionSpec as P

SEQS = 2
LEN = 128
BLOCK = 1152
CHIP_BLOCK = 512
PARTS = 2
MIB = 1 << 20
ANY = pl.BlockSpec(memory_space=pl.ANY)
VMEM = pl.BlockSpec(memory_space=pltpu.VMEM)
BF16 = jnp.bfloat16
F32 = jnp.float32


def product(left, right):
    return jnp.dot(left, right, preferred_element_type=F32)


def rows_by_rows(left, right, precision=None):
    return lax.dot_general(
        left, right, (((1,), (1,)), ((), ())), precision=precision, preferred_element_type=F32
    )


def per_sequence(matrix):
    return matrix.reshape(SEQS, matrix.shape[0] // SEQS, matrix.shape[1])


def plain(x_in, out_grad, gate_pre, up_pre, down_weight, x_factor, gate_factor, up_factor, h_factor, dy_factor):
    hidden_grad = rows_by_rows(lax.all_gather(out_grad, "tensor", axis=1, tiled=True), down_weight)
    gate_val = gate_pre.astype(F32)
    up_val = up_pre.astype(F32)
    sigmoid_gate = jax.nn.sigmoid(gate_val)
    silu_gate = gate_val * sigmoid_gate
    hidden = (silu_gate * up_val).astype(BF16)
    d_gate = (hidden_grad * up_val * sigmoid_gate * (1.0 + gate_val * (1.0 - sigmoid_gate))).astype(BF16)
    d_up = (hidden_grad * silu_gate).astype(BF16)
    rows = [
        product(x_in, x_factor),
        product(d_gate, gate_factor),
        product(d_up, up_factor),
        product(hidden, h_factor),
        product(out_grad, dy_factor),
    ]
    totals = lax.psum(jnp.stack(rows), "tensor")
    p_x, q_gate, q_up, p_h, q_y = [per_sequence(totals[i]) for i in range(5)]
    highest = lax.Precision.HIGHEST
    return (
        jnp.einsum("sli,slj->sij", p_x, q_gate, precision=highest),
        jnp.einsum("sli,slj->sij", p_x, q_up, precision=highest),
        jnp.einsum("sli,slj->sij", p_h, q_y, precision=highest),
    )


class Step:
    def __init__(self, owner, width, block, w_hbm):
        self.owner, self.width, self.block, self.w_hbm = owner, width, block, w_hbm

    def units(self, i):
        return pl.ds(pl.multiple_of(i * self.block, self.block), self.block)

    def copies(self, i, dst, sems):
        columns = pl.ds(pl.multiple_of(self.owner * self.width, 128), self.width)
        part = self.block // PARTS
        return [
            pltpu.make_async_copy(
                self.w_hbm.at[pl.ds(pl.multiple_of(i * self.block + k * part, part), part), columns],
                dst.at[pl.ds(k * part, part)],
                sems.at[k],
            )
            for k in range(PARTS)
        ]


def start(copies):
    for copy in copies:
        copy.start()


def wait(copies):
    for copy in copies:
        copy.wait()


def stream(step, following, ahead, blocks, head, w_v, next_head, sems, body, body_of_head=None):
    heads = head.shape[0]
    slots = w_v.shape[0]

    def copies(j):
        return step.copies(j, w_v.at[(j - heads) % slots], sems.at[j])

    def next_copies(j):
        return following.copies(j, next_head.at[j], sems.at[blocks + j])

    last = blocks + (0 if following is None else next_head.shape[0])

    def begin(j):
        @pl.when(j < blocks)
        def _():
            start(copies(j))

        if following is not None:

            @pl.when((j >= blocks) & (j < last))
            def _():
                start(next_copies(j - blocks))

    for j in range(heads, ahead):
        start(copies(j))

    @pl.loop(0, heads)
    def _(i):
        begin(i + ahead)
        (body_of_head or body)(i, head.at[i])

    @pl.loop(heads, blocks)
    def _(i):
        begin(i + ahead)
        wait(copies(i))
        body(i, w_v.at[(i - heads) % slots])

    for j in range(blocks + ahead, last):
        start(next_copies(j - blocks))
    for j in range(last - blocks):
        wait(next_copies(j))


def elementwise_kernel(x_hbm, og_hbm, gate_hbm, up_hbm, w_hbm, xf_hbm, yf_hbm, hf_hbm,
                       a_ref, b_ref, ph_ref, pq_ref, head_ref, own_ref,
                       x_v, og_v, gate_v, up_v, xf_v, yf_v, hf_v, sems, gate_sems, up_sems, w_sems):
    units = a_ref.shape[0]
    rank = ph_ref.shape[0]
    turns = units // BLOCK

    def at(i):
        return pl.ds(pl.multiple_of(i * BLOCK, BLOCK), BLOCK)

    def gate_up(i):
        return [
            pltpu.make_async_copy(gate_hbm.at[:, at(i)], gate_v.at[i], gate_sems.at[i]),
            pltpu.make_async_copy(up_hbm.at[:, at(i)], up_v.at[i], up_sems.at[i]),
        ]

    pairs = ((hf_hbm, hf_v), (og_hbm, og_v), (x_hbm, x_v), (xf_hbm, xf_v), (yf_hbm, yf_v))
    small = [pltpu.make_async_copy(src, dst, sems.at[i]) for i, (src, dst) in enumerate(pairs)]
    following = Step(lax.axis_index("tensor") // 2, head_ref.shape[2], head_ref.shape[1], w_hbm)
    heads = head_ref.shape[0]

    start(gate_up(0))
    start(small[:1])
    for i in range(1, turns):
        start(gate_up(i))
    start(small[1:])
    for i in range(heads):
        start(following.copies(i, head_ref.at[i], w_sems.at[i]))
    ph_ref[...] = jnp.zeros_like(ph_ref)
    wait(gate_up(0))
    wait(small[:1])

    @pl.loop(0, turns)
    def _(i):
        @pl.when(i > 0)
        def _():
            wait(gate_up(i))

        g = gate_v[i].T.astype(F32)
        u = up_v[i].T.astype(F32)
        s = 0.5 * jnp.tanh(0.5 * g) + 0.5
        silu = g * s
        a_ref[at(i)] = u * s * ((1.0 + g) - silu)
        b_ref[at(i)] = silu
        ph_ref[...] += product(hf_v[:, at(i)], (silu * u).astype(BF16))

    wait(small[1:])
    pq_ref[:rank] = rows_by_rows(xf_v[...], x_v[...])
    own_ref[...] = og_v[...].T
    pq_ref[rank:] = product(yf_v[...], own_ref[...])
    for i in range(heads):
        wait(following.copies(i, head_ref.at[i], w_sems.at[i]))


def chip_features_kernel(own_ref, mate_ref, head_ref, w_hbm, acc_ref, next_ref, og_v, w_v, sems):
    me = lax.axis_index("tensor")
    width = own_ref.shape[0]
    step = Step(me // 2, 2 * width, w_v.shape[1], w_hbm)
    following = Step(me ^ 2, width, next_ref.shape[1], w_hbm)
    mine = pl.ds(pl.multiple_of(me % 2 * width, 128), width)
    theirs = pl.ds(pl.multiple_of((me + 1) % 2 * width, 128), width)
    og_v[mine] = own_ref[...]
    og_v[theirs] = mate_ref[...].T

    def body(i, weights):
        acc_ref[step.units(i)] = product(weights[...], og_v[...])

    stream(step, following, 4, acc_ref.shape[0] // step.block, head_ref, w_v, next_ref, sems, body)


def add_kernel(bits, following_bits, acc_in, og_ref, head_ref, w_hbm, acc_ref, next_ref, og_v, w_v, sems):
    me = lax.axis_index("tensor")
    _, block, width = w_v.shape
    step = Step(me ^ bits, width, block, w_hbm)
    following = Step(me ^ following_bits, width, block, w_hbm)

    og_v[...] = og_ref[...].T

    def body(i, weights):
        at = step.units(i)
        acc_ref[at] = acc_in[at] + product(weights[...], og_v[...])

    stream(step, following, 3, acc_in.shape[0] // block, head_ref, w_v, next_ref, sems, body)


def far_kernel(bits, acc_ref, og_ref, head_ref, w_hbm, a_ref, b_ref, gf_hbm, uf_hbm, gate_ref, up_ref,
               og_v, w_v, gf_ref, uf_ref, hidden_v, sems, factor_sems):
    _, block, width = w_v.shape
    step = Step(lax.axis_index("tensor") ^ bits, width, block, w_hbm)
    factors = [
        pltpu.make_async_copy(src, dst, factor_sems.at[k]) for k, (src, dst) in enumerate(((gf_hbm, gf_ref), (uf_hbm, uf_ref)))
    ]
    start(factors)
    gate_ref[...] = jnp.zeros_like(gate_ref)
    up_ref[...] = jnp.zeros_like(up_ref)
    og_v[...] = og_ref[...].T

    blocks = acc_ref.shape[0] // block

    def multiply(i, weights):
        hidden_v[i % 2] = acc_ref[step.units(i)] + product(weights[...], og_v[...])

    def use(i):
        at = step.units(i)
        hidden_grad = hidden_v[i % 2]
        gate_ref[...] += product(gf_ref[:, at], (hidden_grad * a_ref[at]).astype(BF16))
        up_ref[...] += product(uf_ref[:, at], (hidden_grad * b_ref[at]).astype(BF16))

    def body(i, weights):
        use(i - 1)
        multiply(i, weights)

    def body_of_head(i, weights):
        multiply(i, weights)
        wait(factors)

    stream(step, None, 3, blocks, head_ref, w_v, None, sems, body, body_of_head)
    use(blocks - 1)


def after_kernel(array_ref, token_ref, same_ref):
    pass


def chip_kernel(mine_ref, theirs_ref, token_ref, chip_ref):
    chip_ref[...] = mine_ref[...] + theirs_ref[...]


def gradients_kernel(chip_ref, other_ref, gate_ref, up_ref, ph_ref, share_ref):
    rank = ph_ref.shape[0]
    total = chip_ref[...] + other_ref[...]
    highest = lax.Precision.HIGHEST
    for s in range(SEQS):
        at = slice(s * LEN, (s + 1) * LEN)
        out = slice(s * rank, (s + 1) * rank)
        share_ref[out, :rank] = rows_by_rows(total[:rank, at], gate_ref[:, at], highest)
        share_ref[out, rank:] = rows_by_rows(total[:rank, at], up_ref[:, at], highest)
        share_ref[SEQS * rank :, out] = rows_by_rows(ph_ref[:, at], total[rank:, at], highest)


def sum_kernel(mine_ref, theirs_ref, gate_ref, up_ref, down_ref):
    rank = gate_ref.shape[1]
    total = mine_ref[...] + theirs_ref[...]
    for s in range(SEQS):
        gate_ref[s] = total[s * rank : (s + 1) * rank, :rank]
        up_ref[s] = total[s * rank : (s + 1) * rank, rank:]
        down_ref[s] = total[SEQS * rank :, s * rank : (s + 1) * rank]


def fast(x_in, out_grad, gate_pre, up_pre, down_weight, x_factor, gate_factor, up_factor, h_factor, dy_factor):
    tokens, width = out_grad.shape
    units, rank = h_factor.shape
    dma = pltpu.SemaphoreType.DMA

    def in_hbm(array):
        return pltpu.with_memory_space_constraint(array, pltpu.HBM)

    def swap(array, bits):
        return lax.ppermute(array, "tensor", [(i, i ^ bits) for i in range(4)])

    def call(kernel, out_shape, in_specs, scratch, mib, flops=0, moved=0, **kwargs):
        several = isinstance(out_shape, tuple)
        return pl.pallas_call(
            kernel,
            out_shape=out_shape,
            in_specs=in_specs,
            out_specs=(VMEM,) * len(out_shape) if several else VMEM,
            scratch_shapes=list(scratch),
            compiler_params=pltpu.CompilerParams(vmem_limit_bytes=mib * MIB),
            cost_estimate=pl.CostEstimate(flops=flops, bytes_accessed=moved, transcendentals=0),
            **kwargs,
        )

    held = pltpu.VMEM((units, tokens), F32)
    per_product = 2 * tokens * width * units
    turns = units // BLOCK
    narrow = pltpu.VMEM((rank, tokens), F32)
    turned = pltpu.VMEM((width, tokens), BF16)
    weight = in_hbm(down_weight)

    def blocks(count):
        return pltpu.VMEM((count, BLOCK, width), BF16)

    def chip_blocks(count):
        return pltpu.VMEM((count, CHIP_BLOCK, 2 * width), BF16)

    near = swap(out_grad, 2)
    mate = swap(out_grad, 1)
    a, b, ph, pq, head, own = call(
        elementwise_kernel,
        (held, held, narrow, pltpu.VMEM((2 * rank, tokens), F32), chip_blocks(2), turned),
        [ANY] * 8,
        [
            pltpu.VMEM((tokens, width), BF16),
            pltpu.VMEM((tokens, width), BF16),
            pltpu.VMEM((turns, tokens, BLOCK), BF16),
            pltpu.VMEM((turns, tokens, BLOCK), BF16),
            pltpu.VMEM((rank, width), BF16),
            pltpu.VMEM((rank, width), BF16),
            pltpu.VMEM((rank, units), BF16),
            dma((5,)),
            dma((turns,)),
            dma((turns,)),
            dma((2, PARTS)),
        ],
        14,
        per_product // 4,
        4 * units * tokens,
    )(
        in_hbm(x_in),
        in_hbm(out_grad),
        in_hbm(gate_pre),
        in_hbm(up_pre),
        weight,
        in_hbm(x_factor.T),
        in_hbm(dy_factor.T),
        in_hbm(h_factor.T),
    )
    pq_mate = swap(pq, 1)
    acc, head = call(
        chip_features_kernel,
        (held, blocks(2)),
        [VMEM] * 3 + [ANY],
        [pltpu.VMEM((2 * width, tokens), BF16), chip_blocks(5), dma((units // CHIP_BLOCK + 2, PARTS))],
        16,
        2 * per_product,
        4 * units * width,
    )(own, mate, head, weight)

    near = pl.pallas_call(
        after_kernel,
        out_shape=pltpu.VMEM(near.shape, near.dtype),
        in_specs=[ANY, ANY],
        out_specs=ANY,
        input_output_aliases={0: 0},
        compiler_params=pltpu.CompilerParams(vmem_limit_bytes=MIB),
    )(near, head)
    far = swap(near, 1)
    acc, head = call(
        functools.partial(add_kernel, 2, 3),
        (held, blocks(1)),
        [VMEM] * 3 + [ANY],
        [turned, blocks(2), dma((turns + 1, PARTS))],
        10,
        per_product,
        2 * units * width,
        input_output_aliases={0: 0},
    )(acc, near, head, weight)
    chip = call(chip_kernel, pltpu.VMEM(pq.shape, F32), [VMEM, VMEM, ANY], [], 1)(pq, pq_mate, head)
    chip_across = swap(chip, 2)
    factor = pltpu.VMEM((rank, units), BF16)
    q_gate, q_up = call(
        functools.partial(far_kernel, 3),
        (narrow, narrow),
        [VMEM] * 3 + [ANY] + [VMEM] * 2 + [ANY] * 2,
        [turned, blocks(3), factor, factor, pltpu.VMEM((2, BLOCK, tokens), F32), dma((turns, PARTS)), dma((2,))],
        16,
        per_product,
        2 * units * width,
    )(acc, far, head, weight, a, b, in_hbm(gate_factor.T), in_hbm(up_factor.T))
    share = call(gradients_kernel, pltpu.VMEM(((SEQS + 1) * rank, 2 * rank), F32), [VMEM] * 5, [], 4)(
        chip, chip_across, q_gate, q_up, ph
    )
    chip_share = share + swap(share, 1)
    out = jax.ShapeDtypeStruct((SEQS, rank, rank), F32)
    return call(sum_kernel, (out, out, out), [VMEM] * 2, [], 4)(chip_share, swap(chip_share, 2))


def solution(mesh):
    def per_device(*arrays):
        (tokens, width), (units, rank) = arrays[1].shape, arrays[8].shape
        fits = (
            mesh.shape["tensor"] == 4
            and (tokens, rank) == (SEQS * LEN, LEN // 2)
            and width % 128 == 0
            and units % BLOCK == 0
            and units % CHIP_BLOCK == 0
            and units // BLOCK > 3
        )
        return tuple((fast if fits else plain)(*arrays))

    return jax.shard_map(
        per_device,
        mesh=mesh,
        in_specs=(P("dp", "tensor"),) * 4 + (P("tensor", None),) * 6,
        out_specs=(P("dp", None, None),) * 3,
        check_vma=False,
    )
```

```python
import functools

import jax
import jax.numpy as jnp
from jax import lax
from jax.experimental import pallas as pl
from jax.experimental.pallas import tpu as pltpu
from jax.sharding import PartitionSpec as P

SEQS = 2
LEN = 128
BLOCK = 1152
CHIP_BLOCK = 512
FIRST = 512
PARTS = 2
MIB = 1 << 20
ANY = pl.BlockSpec(memory_space=pl.ANY)
VMEM = pl.BlockSpec(memory_space=pltpu.VMEM)
BF16 = jnp.bfloat16
F32 = jnp.float32


def product(left, right):
    return jnp.dot(left, right, preferred_element_type=F32)


def rows_by_rows(left, right, precision=None):
    return lax.dot_general(
        left, right, (((1,), (1,)), ((), ())), precision=precision, preferred_element_type=F32
    )


def per_sequence(matrix):
    return matrix.reshape(SEQS, matrix.shape[0] // SEQS, matrix.shape[1])


def plain(x_in, out_grad, gate_pre, up_pre, down_weight, x_factor, gate_factor, up_factor, h_factor, dy_factor):
    hidden_grad = rows_by_rows(lax.all_gather(out_grad, "tensor", axis=1, tiled=True), down_weight)
    gate_val = gate_pre.astype(F32)
    up_val = up_pre.astype(F32)
    sigmoid_gate = jax.nn.sigmoid(gate_val)
    silu_gate = gate_val * sigmoid_gate
    hidden = (silu_gate * up_val).astype(BF16)
    d_gate = (hidden_grad * up_val * sigmoid_gate * (1.0 + gate_val * (1.0 - sigmoid_gate))).astype(BF16)
    d_up = (hidden_grad * silu_gate).astype(BF16)
    rows = [
        product(x_in, x_factor),
        product(d_gate, gate_factor),
        product(d_up, up_factor),
        product(hidden, h_factor),
        product(out_grad, dy_factor),
    ]
    totals = lax.psum(jnp.stack(rows), "tensor")
    p_x, q_gate, q_up, p_h, q_y = [per_sequence(totals[i]) for i in range(5)]
    highest = lax.Precision.HIGHEST
    return (
        jnp.einsum("sli,slj->sij", p_x, q_gate, precision=highest),
        jnp.einsum("sli,slj->sij", p_x, q_up, precision=highest),
        jnp.einsum("sli,slj->sij", p_h, q_y, precision=highest),
    )


class Step:
    def __init__(self, column, width, block, w_hbm):
        self.column, self.width, self.block, self.w_hbm = column, width, block, w_hbm

    def units(self, i):
        return pl.ds(pl.multiple_of(i * self.block, self.block), self.block)

    def copies(self, i, dst, sems):
        columns = pl.ds(pl.multiple_of(self.column, 128), self.width)
        part = self.block // PARTS
        return [
            pltpu.make_async_copy(
                self.w_hbm.at[pl.ds(pl.multiple_of(i * self.block + k * part, part), part), columns],
                dst.at[pl.ds(k * part, part)],
                sems.at[k],
            )
            for k in range(PARTS)
        ]


def start(copies):
    for copy in copies:
        copy.start()


def wait(copies):
    for copy in copies:
        copy.wait()


def stream(step, following, ahead, blocks, head, w_v, next_head, sems, body):
    heads = head.shape[0]
    slots = 1 if w_v is None else w_v.shape[0]

    def copies(j):
        return step.copies(j, w_v.at[(j - heads) % slots], sems.at[j])

    def next_copies(j):
        return following.copies(j, next_head.at[j], sems.at[blocks + j])

    last = blocks + (0 if following is None else next_head.shape[0])

    def begin(j):
        @pl.when(j < blocks)
        def _():
            start(copies(j))

        if following is not None:

            @pl.when((j >= blocks) & (j < last))
            def _():
                start(next_copies(j - blocks))

    for j in range(heads, ahead):
        start(copies(j))

    @pl.loop(0, heads)
    def _(i):
        begin(i + ahead)
        body(i, head.at[i])

    @pl.loop(heads, blocks)
    def _(i):
        begin(i + ahead)
        wait(copies(i))
        body(i, w_v.at[(i - heads) % slots])

    for j in range(blocks + ahead, last):
        start(next_copies(j - blocks))
    for j in range(last - blocks):
        wait(next_copies(j))


def entry_kernel(og_hbm, own_ref, first_ref, second_ref, og_v, sem):
    copy = pltpu.make_async_copy(og_hbm, og_v, sem)
    copy.start()
    copy.wait()
    own_ref[...] = og_v[...].T
    first_ref[...] = own_ref[:FIRST]
    second_ref[...] = own_ref[FIRST:]


def elementwise_kernel(x_hbm, own_ref, gate_hbm, up_hbm, w_hbm, xf_hbm, yf_hbm, hf_hbm,
                       a_ref, b_ref, ph_ref, pq_ref, head_ref,
                       x_v, gate_v, up_v, xf_v, yf_v, hf_v, sems, gate_sems, up_sems, w_sems):
    units = a_ref.shape[0]
    rank = ph_ref.shape[0]
    turns = units // BLOCK

    def at(i):
        return pl.ds(pl.multiple_of(i * BLOCK, BLOCK), BLOCK)

    def gate_up(i):
        return [
            pltpu.make_async_copy(gate_hbm.at[:, at(i)], gate_v.at[i], gate_sems.at[i]),
            pltpu.make_async_copy(up_hbm.at[:, at(i)], up_v.at[i], up_sems.at[i]),
        ]

    pairs = ((hf_hbm, hf_v), (x_hbm, x_v), (xf_hbm, xf_v), (yf_hbm, yf_v))
    small = [pltpu.make_async_copy(src, dst, sems.at[i]) for i, (src, dst) in enumerate(pairs)]
    following = Step(lax.axis_index("tensor") // 2 * head_ref.shape[2], head_ref.shape[2], head_ref.shape[1], w_hbm)
    heads = head_ref.shape[0]

    start(gate_up(0))
    start(small[:1])
    for i in range(1, turns):
        start(gate_up(i))
    start(small[1:])
    for i in range(heads):
        start(following.copies(i, head_ref.at[i], w_sems.at[i]))
    ph_ref[...] = jnp.zeros_like(ph_ref)
    wait(gate_up(0))
    wait(small[:1])

    @pl.loop(0, turns)
    def _(i):
        @pl.when(i > 0)
        def _():
            wait(gate_up(i))

        g = gate_v[i].T.astype(F32)
        u = up_v[i].T.astype(F32)
        s = 0.5 * jnp.tanh(0.5 * g) + 0.5
        silu = g * s
        a_ref[at(i)] = u * s * ((1.0 + g) - silu)
        b_ref[at(i)] = silu
        ph_ref[...] += product(hf_v[:, at(i)], (silu * u).astype(BF16))

    wait(small[1:])
    pq_ref[:rank] = rows_by_rows(xf_v[...], x_v[...])
    pq_ref[rank:] = product(yf_v[...], own_ref[...])
    for i in range(heads):
        wait(following.copies(i, head_ref.at[i], w_sems.at[i]))


def chip_features_kernel(own_ref, mate_ref, head_ref, w_hbm, acc_ref, next_ref, og_v, w_v, sems):
    me = lax.axis_index("tensor")
    width = own_ref.shape[0]
    step = Step(me // 2 * 2 * width, 2 * width, w_v.shape[1], w_hbm)
    following = Step((me ^ 2) * width, next_ref.shape[2], next_ref.shape[1], w_hbm)
    mine = pl.ds(pl.multiple_of(me % 2 * width, 128), width)
    theirs = pl.ds(pl.multiple_of((me + 1) % 2 * width, 128), width)
    og_v[mine] = own_ref[...]
    og_v[theirs] = mate_ref[...]

    def body(i, weights):
        acc_ref[step.units(i)] = product(weights[...], og_v[...])

    stream(step, following, 4, acc_ref.shape[0] // step.block, head_ref, w_v, next_ref, sems, body)


def add_kernel(step_at, following_at, per_device, acc_in, og_ref, head_ref, w_hbm, acc_ref, next_ref, w_v, sems):
    me = lax.axis_index("tensor")
    block, width = head_ref.shape[1:]
    step = Step((me ^ step_at[0]) * per_device + step_at[1], width, block, w_hbm)
    following = Step((me ^ following_at[0]) * per_device + following_at[1], next_ref.shape[2], next_ref.shape[1], w_hbm)

    def body(i, weights):
        at = step.units(i)
        acc_ref[at] = acc_in[at] + product(weights[...], og_ref[...])

    stream(step, following, 4, acc_in.shape[0] // block, head_ref, w_v, next_ref, sems, body)


def last_kernel(step_at, per_device, acc_ref, og_ref, head_ref, w_hbm, a_ref, b_ref, gf_hbm, uf_hbm, gate_ref, up_ref,
                w_v, gf_ref, uf_ref, d_gate_v, d_up_v, sems, factor_sems):
    block, width = head_ref.shape[1:]
    step = Step((lax.axis_index("tensor") ^ step_at[0]) * per_device + step_at[1], width, block, w_hbm)
    factors = [
        pltpu.make_async_copy(src, dst, factor_sems.at[k]) for k, (src, dst) in enumerate(((gf_hbm, gf_ref), (uf_hbm, uf_ref)))
    ]
    start(factors)

    def body(i, weights):
        at = step.units(i)
        hidden_grad = acc_ref[at] + product(weights[...], og_ref[...])
        d_gate_v[at] = (hidden_grad * a_ref[at]).astype(BF16)
        d_up_v[at] = (hidden_grad * b_ref[at]).astype(BF16)

    stream(step, None, 4, acc_ref.shape[0] // block, head_ref, w_v, None, sems, body)
    wait(factors)
    gate_ref[...] = product(gf_ref[...], d_gate_v[...])
    up_ref[...] = product(uf_ref[...], d_up_v[...])


def after_kernel(array_ref, token_ref, same_ref):
    pass


def chip_kernel(mine_ref, theirs_ref, token_ref, chip_ref):
    chip_ref[...] = mine_ref[...] + theirs_ref[...]


def gradients_kernel(chip_ref, other_ref, gate_ref, up_ref, ph_ref, share_ref):
    rank = ph_ref.shape[0]
    total = chip_ref[...] + other_ref[...]
    highest = lax.Precision.HIGHEST
    for s in range(SEQS):
        at = slice(s * LEN, (s + 1) * LEN)
        out = slice(s * rank, (s + 1) * rank)
        share_ref[out, :rank] = rows_by_rows(total[:rank, at], gate_ref[:, at], highest)
        share_ref[out, rank:] = rows_by_rows(total[:rank, at], up_ref[:, at], highest)
        share_ref[SEQS * rank :, out] = rows_by_rows(ph_ref[:, at], total[rank:, at], highest)


def sum_kernel(mine_ref, theirs_ref, gate_ref, up_ref, down_ref):
    rank = gate_ref.shape[1]
    total = mine_ref[...] + theirs_ref[...]
    for s in range(SEQS):
        gate_ref[s] = total[s * rank : (s + 1) * rank, :rank]
        up_ref[s] = total[s * rank : (s + 1) * rank, rank:]
        down_ref[s] = total[SEQS * rank :, s * rank : (s + 1) * rank]


def fast(x_in, out_grad, gate_pre, up_pre, down_weight, x_factor, gate_factor, up_factor, h_factor, dy_factor):
    tokens, width = out_grad.shape
    units, rank = h_factor.shape
    dma = pltpu.SemaphoreType.DMA

    def in_hbm(array):
        return pltpu.with_memory_space_constraint(array, pltpu.HBM)

    def swap(array, bits):
        return lax.ppermute(array, "tensor", [(i, i ^ bits) for i in range(4)])

    def call(kernel, out_shape, in_specs, scratch, mib, flops=0, moved=0, **kwargs):
        several = isinstance(out_shape, tuple)
        return pl.pallas_call(
            kernel,
            out_shape=out_shape,
            in_specs=in_specs,
            out_specs=(VMEM,) * len(out_shape) if several else VMEM,
            scratch_shapes=list(scratch),
            compiler_params=pltpu.CompilerParams(vmem_limit_bytes=mib * MIB),
            cost_estimate=pl.CostEstimate(flops=flops, bytes_accessed=moved, transcendentals=0),
            **kwargs,
        )

    held = pltpu.VMEM((units, tokens), F32)
    per_product = 2 * tokens * width * units
    turns = units // BLOCK
    narrow = pltpu.VMEM((rank, tokens), F32)
    turned = pltpu.VMEM((width, tokens), BF16)
    weight = in_hbm(down_weight)

    def blocks(count, features):
        return pltpu.VMEM((count, BLOCK, features), BF16)

    def chip_blocks(count):
        return pltpu.VMEM((count, CHIP_BLOCK, 2 * width), BF16)

    second = width - FIRST
    own, piece, other_piece = call(
        entry_kernel,
        (turned, pltpu.VMEM((FIRST, tokens), BF16), pltpu.VMEM((second, tokens), BF16)),
        [ANY],
        [pltpu.VMEM((tokens, width), BF16), dma],
        4,
    )(in_hbm(out_grad))
    near_first = swap(piece, 2)
    near_second = swap(other_piece, 2)
    mate = swap(own, 1)
    a, b, ph, pq, head = call(
        elementwise_kernel,
        (held, held, narrow, pltpu.VMEM((2 * rank, tokens), F32), chip_blocks(2)),
        [ANY, VMEM] + [ANY] * 6,
        [
            pltpu.VMEM((tokens, width), BF16),
            pltpu.VMEM((turns, tokens, BLOCK), BF16),
            pltpu.VMEM((turns, tokens, BLOCK), BF16),
            pltpu.VMEM((rank, width), BF16),
            pltpu.VMEM((rank, width), BF16),
            pltpu.VMEM((rank, units), BF16),
            dma((4,)),
            dma((turns,)),
            dma((turns,)),
            dma((2, PARTS)),
        ],
        14,
        per_product // 4,
        4 * units * tokens,
    )(
        in_hbm(x_in),
        own,
        in_hbm(gate_pre),
        in_hbm(up_pre),
        weight,
        in_hbm(x_factor.T),
        in_hbm(dy_factor.T),
        in_hbm(h_factor.T),
    )
    pq_mate = swap(pq, 1)
    acc, head = call(
        chip_features_kernel,
        (held, blocks(4, FIRST)),
        [VMEM] * 3 + [ANY],
        [pltpu.VMEM((2 * width, tokens), BF16), chip_blocks(5), dma((units // CHIP_BLOCK + 4, PARTS))],
        16,
        2 * per_product,
        4 * units * width,
    )(own, mate, head, weight)

    def after(array, token):
        return pl.pallas_call(
            after_kernel,
            out_shape=pltpu.VMEM(array.shape, array.dtype),
            in_specs=[ANY, ANY],
            out_specs=ANY,
            input_output_aliases={0: 0},
            compiler_params=pltpu.CompilerParams(vmem_limit_bytes=MIB),
        )(array, token)

    def add(step_at, following_at, features, acc, head, next_head):
        count, size = head.shape[0], features.shape[0]
        return call(
            functools.partial(add_kernel, step_at, following_at, width),
            (held, next_head),
            [VMEM] * 3 + [ANY],
            [blocks(max(turns - count, 1), size), dma((turns + next_head.shape[0], PARTS))],
            8,
            2 * tokens * size * units,
            2 * units * size,
            input_output_aliases={0: 0},
        )(acc, features, head, weight)

    near_first = after(near_first, head)
    far_first = swap(near_first, 1)
    acc, head = add((2, 0), (3, 0), near_first, acc, head, blocks(2, FIRST))
    acc, head = add((3, 0), (2, FIRST), far_first, acc, head, blocks(3, second))
    near_second = after(near_second, head)
    far_second = swap(near_second, 1)
    acc, head = add((2, FIRST), (3, FIRST), near_second, acc, head, blocks(2, second))
    chip = call(chip_kernel, pltpu.VMEM(pq.shape, F32), [VMEM, VMEM, ANY], [], 1)(pq, pq_mate, head)
    chip_across = swap(chip, 2)
    factor = pltpu.VMEM((rank, units), BF16)
    kept = pltpu.VMEM((units, tokens), BF16)
    q_gate, q_up = call(
        functools.partial(last_kernel, (3, FIRST), width),
        (narrow, narrow),
        [VMEM] * 3 + [ANY] + [VMEM] * 2 + [ANY] * 2,
        [blocks(turns - 2, second), factor, factor, kept, kept, dma((turns, PARTS)), dma((2,))],
        14,
        2 * tokens * second * units,
        2 * units * second,
    )(acc, far_second, head, weight, a, b, in_hbm(gate_factor.T), in_hbm(up_factor.T))
    share = call(gradients_kernel, pltpu.VMEM(((SEQS + 1) * rank, 2 * rank), F32), [VMEM] * 5, [], 4)(
        chip, chip_across, q_gate, q_up, ph
    )
    chip_share = share + swap(share, 1)
    out = jax.ShapeDtypeStruct((SEQS, rank, rank), F32)
    return call(sum_kernel, (out, out, out), [VMEM] * 2, [], 4)(chip_share, swap(chip_share, 2))


def solution(mesh):
    def per_device(*arrays):
        (tokens, width), (units, rank) = arrays[1].shape, arrays[8].shape
        fits = (
            mesh.shape["tensor"] == 4
            and (tokens, rank) == (SEQS * LEN, LEN // 2)
            and width % 128 == 0
            and width > FIRST
            and units % BLOCK == 0
            and units % CHIP_BLOCK == 0
            and units // BLOCK == 4
        )
        return tuple((fast if fits else plain)(*arrays))

    return jax.shard_map(
        per_device,
        mesh=mesh,
        in_specs=(P("dp", "tensor"),) * 4 + (P("tensor", None),) * 6,
        out_specs=(P("dp", None, None),) * 3,
        check_vma=False,
    )
```

```python
import functools

import jax
import jax.numpy as jnp
from jax import lax
from jax.experimental import pallas as pl
from jax.experimental.pallas import tpu as pltpu
from jax.sharding import PartitionSpec as P

SEQS = 2
LEN = 128
BLOCK = 1152
CHIP_BLOCK = 512
PARTS = 2
MIB = 1 << 20
ANY = pl.BlockSpec(memory_space=pl.ANY)
VMEM = pl.BlockSpec(memory_space=pltpu.VMEM)
BF16 = jnp.bfloat16
F32 = jnp.float32


def product(left, right):
    return jnp.dot(left, right, preferred_element_type=F32)


def rows_by_rows(left, right, precision=None):
    return lax.dot_general(
        left, right, (((1,), (1,)), ((), ())), precision=precision, preferred_element_type=F32
    )


def per_sequence(matrix):
    return matrix.reshape(SEQS, matrix.shape[0] // SEQS, matrix.shape[1])


def plain(x_in, out_grad, gate_pre, up_pre, down_weight, x_factor, gate_factor, up_factor, h_factor, dy_factor):
    hidden_grad = rows_by_rows(lax.all_gather(out_grad, "tensor", axis=1, tiled=True), down_weight)
    gate_val = gate_pre.astype(F32)
    up_val = up_pre.astype(F32)
    sigmoid_gate = jax.nn.sigmoid(gate_val)
    silu_gate = gate_val * sigmoid_gate
    hidden = (silu_gate * up_val).astype(BF16)
    d_gate = (hidden_grad * up_val * sigmoid_gate * (1.0 + gate_val * (1.0 - sigmoid_gate))).astype(BF16)
    d_up = (hidden_grad * silu_gate).astype(BF16)
    rows = [
        product(x_in, x_factor),
        product(d_gate, gate_factor),
        product(d_up, up_factor),
        product(hidden, h_factor),
        product(out_grad, dy_factor),
    ]
    totals = lax.psum(jnp.stack(rows), "tensor")
    p_x, q_gate, q_up, p_h, q_y = [per_sequence(totals[i]) for i in range(5)]
    highest = lax.Precision.HIGHEST
    return (
        jnp.einsum("sli,slj->sij", p_x, q_gate, precision=highest),
        jnp.einsum("sli,slj->sij", p_x, q_up, precision=highest),
        jnp.einsum("sli,slj->sij", p_h, q_y, precision=highest),
    )


class Step:
    def __init__(self, owner, width, block, w_hbm):
        self.owner, self.width, self.block, self.w_hbm = owner, width, block, w_hbm

    def units(self, i):
        return pl.ds(pl.multiple_of(i * self.block, self.block), self.block)

    def copies(self, i, dst, sems):
        columns = pl.ds(pl.multiple_of(self.owner * self.width, 128), self.width)
        part = self.block // PARTS
        return [
            pltpu.make_async_copy(
                self.w_hbm.at[pl.ds(pl.multiple_of(i * self.block + k * part, part), part), columns],
                dst.at[pl.ds(k * part, part)],
                sems.at[k],
            )
            for k in range(PARTS)
        ]


def start(copies):
    for copy in copies:
        copy.start()


def wait(copies):
    for copy in copies:
        copy.wait()


def stream(step, following, ahead, blocks, head, w_v, next_head, sems, body):
    heads = head.shape[0]
    slots = w_v.shape[0]

    def copies(j):
        return step.copies(j, w_v.at[(j - heads) % slots], sems.at[j])

    def next_copies(j):
        return following.copies(j, next_head.at[j], sems.at[blocks + j])

    last = blocks + (0 if following is None else next_head.shape[0])

    def begin(j):
        @pl.when(j < blocks)
        def _():
            start(copies(j))

        if following is not None:

            @pl.when((j >= blocks) & (j < last))
            def _():
                start(next_copies(j - blocks))

    for j in range(heads, ahead):
        start(copies(j))

    @pl.loop(0, heads)
    def _(i):
        begin(i + ahead)
        body(i, head.at[i])

    @pl.loop(heads, blocks)
    def _(i):
        begin(i + ahead)
        wait(copies(i))
        body(i, w_v.at[(i - heads) % slots])

    for j in range(blocks + ahead, last):
        start(next_copies(j - blocks))
    for j in range(last - blocks):
        wait(next_copies(j))


def elementwise_kernel(x_hbm, og_hbm, gate_hbm, up_hbm, w_hbm, xf_hbm, yf_hbm, hf_hbm,
                       a_ref, b_ref, ph_ref, pq_ref, head_ref, own_ref,
                       x_v, og_v, gate_v, up_v, xf_v, yf_v, hf_v, sems, gate_sems, up_sems, w_sems):
    units = a_ref.shape[0]
    rank = ph_ref.shape[0]
    turns = units // BLOCK

    def at(i):
        return pl.ds(pl.multiple_of(i * BLOCK, BLOCK), BLOCK)

    def gate_up(i):
        return [
            pltpu.make_async_copy(gate_hbm.at[:, at(i)], gate_v.at[i], gate_sems.at[i]),
            pltpu.make_async_copy(up_hbm.at[:, at(i)], up_v.at[i], up_sems.at[i]),
        ]

    pairs = ((hf_hbm, hf_v), (og_hbm, og_v), (x_hbm, x_v), (xf_hbm, xf_v), (yf_hbm, yf_v))
    small = [pltpu.make_async_copy(src, dst, sems.at[i]) for i, (src, dst) in enumerate(pairs)]
    following = Step(lax.axis_index("tensor") // 2, head_ref.shape[2], head_ref.shape[1], w_hbm)
    heads = head_ref.shape[0]

    start(gate_up(0))
    start(small[:1])
    for i in range(1, turns):
        start(gate_up(i))
    start(small[1:])
    for i in range(heads):
        start(following.copies(i, head_ref.at[i], w_sems.at[i]))
    ph_ref[...] = jnp.zeros_like(ph_ref)
    wait(gate_up(0))
    wait(small[:1])

    @pl.loop(0, turns)
    def _(i):
        @pl.when(i > 0)
        def _():
            wait(gate_up(i))

        g = gate_v[i].T.astype(F32)
        u = up_v[i].T.astype(F32)
        s = 0.5 * jnp.tanh(0.5 * g) + 0.5
        silu = g * s
        a_ref[at(i)] = u * s * ((1.0 + g) - silu)
        b_ref[at(i)] = silu
        ph_ref[...] += product(hf_v[:, at(i)], (silu * u).astype(BF16))

    wait(small[1:])
    pq_ref[:rank] = rows_by_rows(xf_v[...], x_v[...])
    own_ref[...] = og_v[...].T
    pq_ref[rank:] = product(yf_v[...], own_ref[...])
    for i in range(heads):
        wait(following.copies(i, head_ref.at[i], w_sems.at[i]))


def chip_features_kernel(own_ref, mate_ref, head_ref, w_hbm, acc_ref, next_ref, og_v, w_v, sems):
    me = lax.axis_index("tensor")
    width = own_ref.shape[0]
    step = Step(me // 2, 2 * width, w_v.shape[1], w_hbm)
    following = Step(me ^ 2, width, next_ref.shape[1], w_hbm)
    mine = pl.ds(pl.multiple_of(me % 2 * width, 128), width)
    theirs = pl.ds(pl.multiple_of((me + 1) % 2 * width, 128), width)
    og_v[mine] = own_ref[...]
    og_v[theirs] = mate_ref[...].T

    def body(i, weights):
        acc_ref[step.units(i)] = product(weights[...], og_v[...])

    stream(step, following, 3, acc_ref.shape[0] // step.block, head_ref, w_v, next_ref, sems, body)


def add_kernel(bits, following_bits, acc_in, og_ref, head_ref, w_hbm, acc_ref, next_ref, og_v, w_v, sems):
    me = lax.axis_index("tensor")
    _, block, width = w_v.shape
    step = Step(me ^ bits, width, block, w_hbm)
    following = Step(me ^ following_bits, width, block, w_hbm)

    og_v[...] = og_ref[...].T

    def body(i, weights):
        at = step.units(i)
        acc_ref[at] = acc_in[at] + product(weights[...], og_v[...])

    stream(step, following, 4, acc_in.shape[0] // block, head_ref, w_v, next_ref, sems, body)


def far_kernel(bits, acc_ref, og_ref, head_ref, w_hbm, a_ref, b_ref, gf_hbm, uf_hbm, gate_ref, up_ref,
               og_v, w_v, gf_ref, uf_ref, d_gate_v, d_up_v, sems, factor_sems):
    _, block, width = w_v.shape
    step = Step(lax.axis_index("tensor") ^ bits, width, block, w_hbm)
    factors = [
        pltpu.make_async_copy(src, dst, factor_sems.at[k]) for k, (src, dst) in enumerate(((gf_hbm, gf_ref), (uf_hbm, uf_ref)))
    ]
    start(factors)
    og_v[...] = og_ref[...].T

    def body(i, weights):
        at = step.units(i)
        hidden_grad = acc_ref[at] + product(weights[...], og_v[...])
        d_gate_v[at] = (hidden_grad * a_ref[at]).astype(BF16)
        d_up_v[at] = (hidden_grad * b_ref[at]).astype(BF16)

    stream(step, None, 4, acc_ref.shape[0] // block, head_ref, w_v, None, sems, body)
    wait(factors)
    gate_ref[...] = product(gf_ref[...], d_gate_v[...])
    up_ref[...] = product(uf_ref[...], d_up_v[...])


def after_kernel(array_ref, token_ref, same_ref):
    pass


def chip_kernel(mine_ref, theirs_ref, token_ref, chip_ref):
    chip_ref[...] = mine_ref[...] + theirs_ref[...]


def gradients_kernel(chip_ref, other_ref, gate_ref, up_ref, ph_ref, share_ref):
    rank = ph_ref.shape[0]
    total = chip_ref[...] + other_ref[...]
    highest = lax.Precision.HIGHEST
    for s in range(SEQS):
        at = slice(s * LEN, (s + 1) * LEN)
        out = slice(s * rank, (s + 1) * rank)
        share_ref[out, :rank] = rows_by_rows(total[:rank, at], gate_ref[:, at], highest)
        share_ref[out, rank:] = rows_by_rows(total[:rank, at], up_ref[:, at], highest)
        share_ref[SEQS * rank :, out] = rows_by_rows(ph_ref[:, at], total[rank:, at], highest)


def sum_kernel(mine_ref, theirs_ref, gate_ref, up_ref, down_ref):
    rank = gate_ref.shape[1]
    total = mine_ref[...] + theirs_ref[...]
    for s in range(SEQS):
        gate_ref[s] = total[s * rank : (s + 1) * rank, :rank]
        up_ref[s] = total[s * rank : (s + 1) * rank, rank:]
        down_ref[s] = total[SEQS * rank :, s * rank : (s + 1) * rank]


def fast(x_in, out_grad, gate_pre, up_pre, down_weight, x_factor, gate_factor, up_factor, h_factor, dy_factor):
    tokens, width = out_grad.shape
    units, rank = h_factor.shape
    dma = pltpu.SemaphoreType.DMA

    def in_hbm(array):
        return pltpu.with_memory_space_constraint(array, pltpu.HBM)

    def swap(array, bits):
        return lax.ppermute(array, "tensor", [(i, i ^ bits) for i in range(4)])

    def call(kernel, out_shape, in_specs, scratch, mib, flops=0, moved=0, **kwargs):
        several = isinstance(out_shape, tuple)
        return pl.pallas_call(
            kernel,
            out_shape=out_shape,
            in_specs=in_specs,
            out_specs=(VMEM,) * len(out_shape) if several else VMEM,
            scratch_shapes=list(scratch),
            compiler_params=pltpu.CompilerParams(vmem_limit_bytes=mib * MIB),
            cost_estimate=pl.CostEstimate(flops=flops, bytes_accessed=moved, transcendentals=0),
            **kwargs,
        )

    held = pltpu.VMEM((units, tokens), F32)
    per_product = 2 * tokens * width * units
    turns = units // BLOCK
    narrow = pltpu.VMEM((rank, tokens), F32)
    turned = pltpu.VMEM((width, tokens), BF16)
    weight = in_hbm(down_weight)

    def blocks(count):
        return pltpu.VMEM((count, BLOCK, width), BF16)

    def chip_blocks(count):
        return pltpu.VMEM((count, CHIP_BLOCK, 2 * width), BF16)

    near = swap(out_grad, 2)
    mate = swap(out_grad, 1)
    a, b, ph, pq, head, own = call(
        elementwise_kernel,
        (held, held, narrow, pltpu.VMEM((2 * rank, tokens), F32), chip_blocks(2), turned),
        [ANY] * 8,
        [
            pltpu.VMEM((tokens, width), BF16),
            pltpu.VMEM((tokens, width), BF16),
            pltpu.VMEM((turns, tokens, BLOCK), BF16),
            pltpu.VMEM((turns, tokens, BLOCK), BF16),
            pltpu.VMEM((rank, width), BF16),
            pltpu.VMEM((rank, width), BF16),
            pltpu.VMEM((rank, units), BF16),
            dma((5,)),
            dma((turns,)),
            dma((turns,)),
            dma((2, PARTS)),
        ],
        14,
        per_product // 4,
        4 * units * tokens,
    )(
        in_hbm(x_in),
        in_hbm(out_grad),
        in_hbm(gate_pre),
        in_hbm(up_pre),
        weight,
        in_hbm(x_factor.T),
        in_hbm(dy_factor.T),
        in_hbm(h_factor.T),
    )
    pq_mate = swap(pq, 1)
    acc, head = call(
        chip_features_kernel,
        (held, blocks(turns)),
        [VMEM] * 3 + [ANY],
        [pltpu.VMEM((2 * width, tokens), BF16), chip_blocks(4), dma((units // CHIP_BLOCK + turns, PARTS))],
        16,
        2 * per_product,
        4 * units * width,
    )(own, mate, head, weight)

    def after(array, token):
        return pl.pallas_call(
            after_kernel,
            out_shape=pltpu.VMEM(array.shape, array.dtype),
            in_specs=[ANY, ANY],
            out_specs=ANY,
            input_output_aliases={0: 0},
            compiler_params=pltpu.CompilerParams(vmem_limit_bytes=MIB),
        )(array, token)

    chip = call(chip_kernel, pltpu.VMEM(pq.shape, F32), [VMEM, VMEM, ANY], [], 1)(pq, pq_mate, head)
    near = after(near, chip)
    chip = after(chip, near)
    chip_across = swap(chip, 2)
    far = swap(near, 1)
    acc, head = call(
        functools.partial(add_kernel, 2, 3),
        (held, blocks(turns - 1)),
        [VMEM] * 3 + [ANY],
        [turned, blocks(1), dma((2 * turns - 1, PARTS))],
        6,
        per_product,
        2 * units * width,
        input_output_aliases={0: 0},
    )(acc, near, head, weight)
    factor = pltpu.VMEM((rank, units), BF16)
    kept = pltpu.VMEM((units, tokens), BF16)
    q_gate, q_up = call(
        functools.partial(far_kernel, 3),
        (narrow, narrow),
        [VMEM] * 3 + [ANY] + [VMEM] * 2 + [ANY] * 2,
        [turned, blocks(1), factor, factor, kept, kept, dma((turns, PARTS)), dma((2,))],
        16,
        per_product,
        2 * units * width,
    )(acc, far, head, weight, a, b, in_hbm(gate_factor.T), in_hbm(up_factor.T))
    share = call(gradients_kernel, pltpu.VMEM(((SEQS + 1) * rank, 2 * rank), F32), [VMEM] * 5, [], 4)(
        chip, chip_across, q_gate, q_up, ph
    )
    chip_share = share + swap(share, 1)
    out = jax.ShapeDtypeStruct((SEQS, rank, rank), F32)
    return call(sum_kernel, (out, out, out), [VMEM] * 2, [], 4)(chip_share, swap(chip_share, 2))


def solution(mesh):
    def per_device(*arrays):
        (tokens, width), (units, rank) = arrays[1].shape, arrays[8].shape
        fits = (
            mesh.shape["tensor"] == 4
            and (tokens, rank) == (SEQS * LEN, LEN // 2)
            and width % 128 == 0
            and units % BLOCK == 0
            and units % CHIP_BLOCK == 0
            and units // BLOCK > 3
        )
        return tuple((fast if fits else plain)(*arrays))

    return jax.shard_map(
        per_device,
        mesh=mesh,
        in_specs=(P("dp", "tensor"),) * 4 + (P("tensor", None),) * 6,
        out_specs=(P("dp", None, None),) * 3,
        check_vma=False,
    )
```

```python
import jax
import jax.numpy as jnp
from jax import lax
from jax.experimental import pallas as pl
from jax.experimental.pallas import tpu as pltpu
from jax.sharding import PartitionSpec as P

SEQS = 2
LEN = 128
BLOCK = 1152
CHIP_BLOCK = 512
PARTS = 2
MIB = 1 << 20
ANY = pl.BlockSpec(memory_space=pl.ANY)
VMEM = pl.BlockSpec(memory_space=pltpu.VMEM)
BF16 = jnp.bfloat16
F32 = jnp.float32


def product(left, right):
    return jnp.dot(left, right, preferred_element_type=F32)


def rows_by_rows(left, right, precision=None):
    return lax.dot_general(
        left, right, (((1,), (1,)), ((), ())), precision=precision, preferred_element_type=F32
    )


def per_sequence(matrix):
    return matrix.reshape(SEQS, matrix.shape[0] // SEQS, matrix.shape[1])


def plain(x_in, out_grad, gate_pre, up_pre, down_weight, x_factor, gate_factor, up_factor, h_factor, dy_factor):
    hidden_grad = rows_by_rows(lax.all_gather(out_grad, "tensor", axis=1, tiled=True), down_weight)
    gate_val = gate_pre.astype(F32)
    up_val = up_pre.astype(F32)
    sigmoid_gate = jax.nn.sigmoid(gate_val)
    silu_gate = gate_val * sigmoid_gate
    hidden = (silu_gate * up_val).astype(BF16)
    d_gate = (hidden_grad * up_val * sigmoid_gate * (1.0 + gate_val * (1.0 - sigmoid_gate))).astype(BF16)
    d_up = (hidden_grad * silu_gate).astype(BF16)
    rows = [
        product(x_in, x_factor),
        product(d_gate, gate_factor),
        product(d_up, up_factor),
        product(hidden, h_factor),
        product(out_grad, dy_factor),
    ]
    totals = lax.psum(jnp.stack(rows), "tensor")
    p_x, q_gate, q_up, p_h, q_y = [per_sequence(totals[i]) for i in range(5)]
    highest = lax.Precision.HIGHEST
    return (
        jnp.einsum("sli,slj->sij", p_x, q_gate, precision=highest),
        jnp.einsum("sli,slj->sij", p_x, q_up, precision=highest),
        jnp.einsum("sli,slj->sij", p_h, q_y, precision=highest),
    )


class Step:
    def __init__(self, owner, width, block, w_hbm):
        self.owner, self.width, self.block, self.w_hbm = owner, width, block, w_hbm

    def units(self, i):
        return pl.ds(pl.multiple_of(i * self.block, self.block), self.block)

    def copies(self, i, dst, sems):
        columns = pl.ds(pl.multiple_of(self.owner * self.width, 128), self.width)
        part = self.block // PARTS
        return [
            pltpu.make_async_copy(
                self.w_hbm.at[pl.ds(pl.multiple_of(i * self.block + k * part, part), part), columns],
                dst.at[pl.ds(k * part, part)],
                sems.at[k],
            )
            for k in range(PARTS)
        ]


def start(copies):
    for copy in copies:
        copy.start()


def wait(copies):
    for copy in copies:
        copy.wait()


def stream(step, ahead, blocks, head, w_v, sems, body, later):
    heads = head.shape[0]
    slots = w_v.shape[0]

    def copies(j):
        return step.copies(j, w_v.at[(j - heads) % slots], sems.at[j])

    def begin(j):
        @pl.when(j < blocks)
        def _():
            start(copies(j))

        for k, group in enumerate(later):

            @pl.when(j == blocks + k)
            def _():
                start(group)

    for j in range(heads, ahead):
        start(copies(j))

    @pl.loop(0, heads)
    def _(i):
        begin(i + ahead)
        body(i, head.at[i])

    @pl.loop(heads, blocks)
    def _(i):
        begin(i + ahead)
        wait(copies(i))
        body(i, w_v.at[(i - heads) % slots])

    for k, group in enumerate(later):
        if k >= ahead:
            start(group)
    for group in later:
        wait(group)


def elementwise_kernel(x_hbm, og_hbm, gate_hbm, up_hbm, w_hbm, xf_hbm, yf_hbm, hf_hbm,
                       a_ref, b_ref, ph_ref, pq_ref, head_ref, own_ref,
                       x_v, og_v, gate_v, up_v, xf_v, yf_v, hf_v, sems, gate_sems, up_sems, w_sems):
    units = a_ref.shape[0]
    rank = ph_ref.shape[0]
    turns = units // BLOCK

    def at(i):
        return pl.ds(pl.multiple_of(i * BLOCK, BLOCK), BLOCK)

    def gate_up(i):
        return [
            pltpu.make_async_copy(gate_hbm.at[:, at(i)], gate_v.at[i], gate_sems.at[i]),
            pltpu.make_async_copy(up_hbm.at[:, at(i)], up_v.at[i], up_sems.at[i]),
        ]

    pairs = ((hf_hbm, hf_v), (og_hbm, og_v), (x_hbm, x_v), (xf_hbm, xf_v), (yf_hbm, yf_v))
    small = [pltpu.make_async_copy(src, dst, sems.at[i]) for i, (src, dst) in enumerate(pairs)]
    following = Step(lax.axis_index("tensor") // 2, head_ref.shape[2], head_ref.shape[1], w_hbm)
    heads = head_ref.shape[0]

    start(gate_up(0))
    start(small[:1])
    for i in range(1, turns):
        start(gate_up(i))
    start(small[1:])
    for i in range(heads):
        start(following.copies(i, head_ref.at[i], w_sems.at[i]))
    ph_ref[...] = jnp.zeros_like(ph_ref)
    wait(gate_up(0))
    wait(small[:1])

    @pl.loop(0, turns)
    def _(i):
        @pl.when(i > 0)
        def _():
            wait(gate_up(i))

        g = gate_v[i].T.astype(F32)
        u = up_v[i].T.astype(F32)
        s = 0.5 * jnp.tanh(0.5 * g) + 0.5
        silu = g * s
        a_ref[at(i)] = u * s * ((1.0 + g) - silu)
        b_ref[at(i)] = silu
        ph_ref[...] += product(hf_v[:, at(i)], (silu * u).astype(BF16))

    wait(small[1:])
    pq_ref[:rank] = rows_by_rows(xf_v[...], x_v[...])
    own_ref[...] = og_v[...].T
    pq_ref[rank:] = product(yf_v[...], own_ref[...])
    for i in range(heads):
        wait(following.copies(i, head_ref.at[i], w_sems.at[i]))


def chip_features_kernel(own_ref, mate_ref, head_ref, w_hbm, acc_ref, near_ref, far_ref, og_v, w_v, sems, near_sems, far_sems):
    me = lax.axis_index("tensor")
    width = own_ref.shape[0]
    step = Step(me // 2, 2 * width, w_v.shape[1], w_hbm)
    near = Step(me ^ 2, width, near_ref.shape[1], w_hbm)
    far = Step(me ^ 3, width, far_ref.shape[1], w_hbm)
    mine = pl.ds(pl.multiple_of(me % 2 * width, 128), width)
    theirs = pl.ds(pl.multiple_of((me + 1) % 2 * width, 128), width)
    og_v[mine] = own_ref[...]
    og_v[theirs] = mate_ref[...].T

    def body(i, weights):
        acc_ref[step.units(i)] = product(weights[...], og_v[...])

    later = [near.copies(k, near_ref.at[k], near_sems.at[k]) for k in range(near_ref.shape[0])]
    later += [far.copies(k, far_ref.at[k], far_sems.at[k]) for k in range(far_ref.shape[0])]
    stream(step, 3, acc_ref.shape[0] // step.block, head_ref, w_v, sems, body, later)


def near_kernel(acc_in, og_ref, w_ref, w_hbm, acc_ref, far_ref, og_v, sems):
    me = lax.axis_index("tensor")
    blocks, block, width = w_ref.shape
    far = Step(me ^ 3, width, block, w_hbm)
    copies = [far.copies(k + 1, far_ref.at[k], sems.at[k]) for k in range(far_ref.shape[0])]
    for group in copies:
        start(group)
    og_v[...] = og_ref[...].T

    @pl.loop(0, blocks)
    def _(i):
        at = far.units(i)
        acc_ref[at] = acc_in[at] + product(w_ref[i], og_v[...])

    for group in copies:
        wait(group)


def far_kernel(acc_ref, og_ref, first_ref, second_ref, w_hbm, a_ref, b_ref, gf_hbm, uf_hbm, gate_ref, up_ref,
               og_v, w_v, gf_ref, uf_ref, d_gate_v, d_up_v, sems, factor_sems):
    _, block, width = w_v.shape
    step = Step(lax.axis_index("tensor") ^ 3, width, block, w_hbm)
    factors = [
        pltpu.make_async_copy(src, dst, factor_sems.at[k]) for k, (src, dst) in enumerate(((gf_hbm, gf_ref), (uf_hbm, uf_ref)))
    ]
    held = first_ref.shape[0] + second_ref.shape[0]
    copies = [step.copies(held + k, w_v.at[k], sems.at[k]) for k in range(w_v.shape[0])]
    for group in copies:
        start(group)
    start(factors)
    og_v[...] = og_ref[...].T

    def body(i, weights):
        at = step.units(i)
        hidden_grad = acc_ref[at] + product(weights, og_v[...])
        d_gate_v[at] = (hidden_grad * a_ref[at]).astype(BF16)
        d_up_v[at] = (hidden_grad * b_ref[at]).astype(BF16)

    @pl.loop(0, first_ref.shape[0])
    def _(i):
        body(i, first_ref[i])

    @pl.loop(0, second_ref.shape[0])
    def _(i):
        body(first_ref.shape[0] + i, second_ref[i])

    for group in copies:
        wait(group)

    @pl.loop(0, w_v.shape[0])
    def _(i):
        body(held + i, w_v[i])

    wait(factors)
    gate_ref[...] = product(gf_ref[...], d_gate_v[...])
    up_ref[...] = product(uf_ref[...], d_up_v[...])


def after_kernel(array_ref, token_ref, same_ref):
    pass


def chip_kernel(mine_ref, theirs_ref, token_ref, chip_ref):
    chip_ref[...] = mine_ref[...] + theirs_ref[...]


def gradients_kernel(chip_ref, other_ref, gate_ref, up_ref, ph_ref, share_ref):
    rank = ph_ref.shape[0]
    total = chip_ref[...] + other_ref[...]
    highest = lax.Precision.HIGHEST
    for s in range(SEQS):
        at = slice(s * LEN, (s + 1) * LEN)
        out = slice(s * rank, (s + 1) * rank)
        share_ref[out, :rank] = rows_by_rows(total[:rank, at], gate_ref[:, at], highest)
        share_ref[out, rank:] = rows_by_rows(total[:rank, at], up_ref[:, at], highest)
        share_ref[SEQS * rank :, out] = rows_by_rows(ph_ref[:, at], total[rank:, at], highest)


def sum_kernel(mine_ref, theirs_ref, gate_ref, up_ref, down_ref):
    rank = gate_ref.shape[1]
    total = mine_ref[...] + theirs_ref[...]
    for s in range(SEQS):
        gate_ref[s] = total[s * rank : (s + 1) * rank, :rank]
        up_ref[s] = total[s * rank : (s + 1) * rank, rank:]
        down_ref[s] = total[SEQS * rank :, s * rank : (s + 1) * rank]


def fast(x_in, out_grad, gate_pre, up_pre, down_weight, x_factor, gate_factor, up_factor, h_factor, dy_factor):
    tokens, width = out_grad.shape
    units, rank = h_factor.shape
    dma = pltpu.SemaphoreType.DMA

    def in_hbm(array):
        return pltpu.with_memory_space_constraint(array, pltpu.HBM)

    def swap(array, bits):
        return lax.ppermute(array, "tensor", [(i, i ^ bits) for i in range(4)])

    def call(kernel, out_shape, in_specs, scratch, mib, flops=0, moved=0, **kwargs):
        several = isinstance(out_shape, tuple)
        return pl.pallas_call(
            kernel,
            out_shape=out_shape,
            in_specs=in_specs,
            out_specs=(VMEM,) * len(out_shape) if several else VMEM,
            scratch_shapes=list(scratch),
            compiler_params=pltpu.CompilerParams(vmem_limit_bytes=mib * MIB),
            cost_estimate=pl.CostEstimate(flops=flops, bytes_accessed=moved, transcendentals=0),
            **kwargs,
        )

    held = pltpu.VMEM((units, tokens), F32)
    per_product = 2 * tokens * width * units
    turns = units // BLOCK
    narrow = pltpu.VMEM((rank, tokens), F32)
    turned = pltpu.VMEM((width, tokens), BF16)
    weight = in_hbm(down_weight)

    def blocks(count):
        return pltpu.VMEM((count, BLOCK, width), BF16)

    def chip_blocks(count):
        return pltpu.VMEM((count, CHIP_BLOCK, 2 * width), BF16)

    near = swap(out_grad, 2)
    mate = swap(out_grad, 1)
    a, b, ph, pq, head, own = call(
        elementwise_kernel,
        (held, held, narrow, pltpu.VMEM((2 * rank, tokens), F32), chip_blocks(2), turned),
        [ANY] * 8,
        [
            pltpu.VMEM((tokens, width), BF16),
            pltpu.VMEM((tokens, width), BF16),
            pltpu.VMEM((turns, tokens, BLOCK), BF16),
            pltpu.VMEM((turns, tokens, BLOCK), BF16),
            pltpu.VMEM((rank, width), BF16),
            pltpu.VMEM((rank, width), BF16),
            pltpu.VMEM((rank, units), BF16),
            dma((5,)),
            dma((turns,)),
            dma((turns,)),
            dma((2, PARTS)),
        ],
        14,
        per_product // 4,
        4 * units * tokens,
    )(
        in_hbm(x_in),
        in_hbm(out_grad),
        in_hbm(gate_pre),
        in_hbm(up_pre),
        weight,
        in_hbm(x_factor.T),
        in_hbm(dy_factor.T),
        in_hbm(h_factor.T),
    )
    pq_mate = swap(pq, 1)
    acc, w_near, far_first = call(
        chip_features_kernel,
        (held, blocks(turns), blocks(1)),
        [VMEM] * 3 + [ANY],
        [
            pltpu.VMEM((2 * width, tokens), BF16),
            chip_blocks(4),
            dma((units // CHIP_BLOCK, PARTS)),
            dma((turns, PARTS)),
            dma((1, PARTS)),
        ],
        14,
        2 * per_product,
        4 * units * width,
    )(own, mate, head, weight)

    def after(array, token):
        return pl.pallas_call(
            after_kernel,
            out_shape=pltpu.VMEM(array.shape, array.dtype),
            in_specs=[ANY, ANY],
            out_specs=ANY,
            input_output_aliases={0: 0},
            compiler_params=pltpu.CompilerParams(vmem_limit_bytes=MIB),
        )(array, token)

    chip = call(chip_kernel, pltpu.VMEM(pq.shape, F32), [VMEM, VMEM, ANY], [], 1)(pq, pq_mate, far_first)
    near = after(near, chip)
    far = swap(near, 1)
    acc, far_second = call(
        near_kernel,
        (held, blocks(2)),
        [VMEM] * 3 + [ANY],
        [turned, dma((2, PARTS))],
        4,
        per_product,
        2 * units * width,
        input_output_aliases={0: 0},
    )(acc, near, w_near, weight)
    chip = after(chip, far_second)
    chip_across = swap(chip, 2)
    factor = pltpu.VMEM((rank, units), BF16)
    kept = pltpu.VMEM((units, tokens), BF16)
    q_gate, q_up = call(
        far_kernel,
        (narrow, narrow),
        [VMEM] * 4 + [ANY] + [VMEM] * 2 + [ANY] * 2,
        [turned, blocks(turns - 3), factor, factor, kept, kept, dma((turns - 3, PARTS)), dma((2,))],
        14,
        per_product,
        2 * units * width,
    )(acc, far, far_first, far_second, weight, a, b, in_hbm(gate_factor.T), in_hbm(up_factor.T))
    share = call(gradients_kernel, pltpu.VMEM(((SEQS + 1) * rank, 2 * rank), F32), [VMEM] * 5, [], 4)(
        chip, chip_across, q_gate, q_up, ph
    )
    chip_share = share + swap(share, 1)
    out = jax.ShapeDtypeStruct((SEQS, rank, rank), F32)
    return call(sum_kernel, (out, out, out), [VMEM] * 2, [], 4)(chip_share, swap(chip_share, 2))


def solution(mesh):
    def per_device(*arrays):
        (tokens, width), (units, rank) = arrays[1].shape, arrays[8].shape
        fits = (
            mesh.shape["tensor"] == 4
            and (tokens, rank) == (SEQS * LEN, LEN // 2)
            and width % 128 == 0
            and units % BLOCK == 0
            and units % CHIP_BLOCK == 0
            and units // BLOCK > 3
        )
        return tuple((fast if fits else plain)(*arrays))

    return jax.shard_map(
        per_device,
        mesh=mesh,
        in_specs=(P("dp", "tensor"),) * 4 + (P("tensor", None),) * 6,
        out_specs=(P("dp", None, None),) * 3,
        check_vma=False,
    )
```

```python
import jax
import jax.numpy as jnp
from jax import lax
from jax.experimental import pallas as pl
from jax.experimental.pallas import tpu as pltpu
from jax.sharding import PartitionSpec as P

SEQS = 2
LEN = 128
BLOCK = 1152
CHIP_BLOCK = 512
PARTS = 2
MIB = 1 << 20
ANY = pl.BlockSpec(memory_space=pl.ANY)
VMEM = pl.BlockSpec(memory_space=pltpu.VMEM)
BF16 = jnp.bfloat16
F32 = jnp.float32


def product(left, right):
    return jnp.dot(left, right, preferred_element_type=F32)


def rows_by_rows(left, right, precision=None):
    return lax.dot_general(
        left, right, (((1,), (1,)), ((), ())), precision=precision, preferred_element_type=F32
    )


def per_sequence(matrix):
    return matrix.reshape(SEQS, matrix.shape[0] // SEQS, matrix.shape[1])


def plain(x_in, out_grad, gate_pre, up_pre, down_weight, x_factor, gate_factor, up_factor, h_factor, dy_factor):
    hidden_grad = rows_by_rows(lax.all_gather(out_grad, "tensor", axis=1, tiled=True), down_weight)
    gate_val = gate_pre.astype(F32)
    up_val = up_pre.astype(F32)
    sigmoid_gate = jax.nn.sigmoid(gate_val)
    silu_gate = gate_val * sigmoid_gate
    hidden = (silu_gate * up_val).astype(BF16)
    d_gate = (hidden_grad * up_val * sigmoid_gate * (1.0 + gate_val * (1.0 - sigmoid_gate))).astype(BF16)
    d_up = (hidden_grad * silu_gate).astype(BF16)
    rows = [
        product(x_in, x_factor),
        product(d_gate, gate_factor),
        product(d_up, up_factor),
        product(hidden, h_factor),
        product(out_grad, dy_factor),
    ]
    totals = lax.psum(jnp.stack(rows), "tensor")
    p_x, q_gate, q_up, p_h, q_y = [per_sequence(totals[i]) for i in range(5)]
    highest = lax.Precision.HIGHEST
    return (
        jnp.einsum("sli,slj->sij", p_x, q_gate, precision=highest),
        jnp.einsum("sli,slj->sij", p_x, q_up, precision=highest),
        jnp.einsum("sli,slj->sij", p_h, q_y, precision=highest),
    )


class Step:
    def __init__(self, owner, width, block, w_hbm):
        self.owner, self.width, self.block, self.w_hbm = owner, width, block, w_hbm

    def units(self, i):
        return pl.ds(pl.multiple_of(i * self.block, self.block), self.block)

    def copies(self, i, dst, sems):
        columns = pl.ds(pl.multiple_of(self.owner * self.width, 128), self.width)
        part = self.block // PARTS
        return [
            pltpu.make_async_copy(
                self.w_hbm.at[pl.ds(pl.multiple_of(i * self.block + k * part, part), part), columns],
                dst.at[pl.ds(k * part, part)],
                sems.at[k],
            )
            for k in range(PARTS)
        ]


def start(copies):
    for copy in copies:
        copy.start()


def wait(copies):
    for copy in copies:
        copy.wait()


def stream(step, ahead, blocks, head, w_v, sems, body, later):
    heads = head.shape[0]
    slots = w_v.shape[0]

    def copies(j):
        return step.copies(j, w_v.at[(j - heads) % slots], sems.at[j])

    def begin(j):
        @pl.when(j < blocks)
        def _():
            start(copies(j))

        for k, group in enumerate(later):

            @pl.when(j == blocks + k)
            def _():
                start(group)

    for j in range(heads, ahead):
        start(copies(j))

    @pl.loop(0, heads)
    def _(i):
        begin(i + ahead)
        body(i, head.at[i])

    @pl.loop(heads, blocks)
    def _(i):
        begin(i + ahead)
        wait(copies(i))
        body(i, w_v.at[(i - heads) % slots])

    for k, group in enumerate(later):
        if k >= ahead:
            start(group)
    for group in later:
        wait(group)


def elementwise_kernel(x_hbm, og_hbm, gate_hbm, up_hbm, w_hbm, xf_hbm, yf_hbm, hf_hbm,
                       a_ref, b_ref, ph_ref, pq_ref, head_ref, own_ref,
                       x_v, og_v, gate_v, up_v, xf_v, yf_v, hf_v, sems, gate_sems, up_sems, w_sems):
    units = a_ref.shape[0]
    rank = ph_ref.shape[0]
    turns = units // BLOCK

    def at(i):
        return pl.ds(pl.multiple_of(i * BLOCK, BLOCK), BLOCK)

    def gate_up(i):
        return [
            pltpu.make_async_copy(gate_hbm.at[:, at(i)], gate_v.at[i], gate_sems.at[i]),
            pltpu.make_async_copy(up_hbm.at[:, at(i)], up_v.at[i], up_sems.at[i]),
        ]

    pairs = ((hf_hbm, hf_v), (og_hbm, og_v), (x_hbm, x_v), (xf_hbm, xf_v), (yf_hbm, yf_v))
    small = [pltpu.make_async_copy(src, dst, sems.at[i]) for i, (src, dst) in enumerate(pairs)]
    following = Step(lax.axis_index("tensor") // 2, head_ref.shape[2], head_ref.shape[1], w_hbm)
    heads = head_ref.shape[0]

    start(gate_up(0))
    start(small[:1])
    for i in range(1, turns):
        start(gate_up(i))
    start(small[1:])
    for i in range(heads):
        start(following.copies(i, head_ref.at[i], w_sems.at[i]))
    ph_ref[...] = jnp.zeros_like(ph_ref)
    wait(gate_up(0))
    wait(small[:1])

    @pl.loop(0, turns)
    def _(i):
        @pl.when(i > 0)
        def _():
            wait(gate_up(i))

        g = gate_v[i].T.astype(F32)
        u = up_v[i].T.astype(F32)
        s = 0.5 * jnp.tanh(0.5 * g) + 0.5
        silu = g * s
        a_ref[at(i)] = u * s * ((1.0 + g) - silu)
        b_ref[at(i)] = silu
        ph_ref[...] += product(hf_v[:, at(i)], (silu * u).astype(BF16))

    wait(small[1:])
    pq_ref[:rank] = rows_by_rows(xf_v[...], x_v[...])
    own_ref[...] = og_v[...].T
    pq_ref[rank:] = product(yf_v[...], own_ref[...])
    for i in range(heads):
        wait(following.copies(i, head_ref.at[i], w_sems.at[i]))


def chip_features_kernel(own_ref, mate_ref, head_ref, w_hbm, acc_ref, near_ref, og_v, w_v, sems, near_sems):
    me = lax.axis_index("tensor")
    width = own_ref.shape[0]
    step = Step(me // 2, 2 * width, w_v.shape[1], w_hbm)
    near = Step(me ^ 2, width, near_ref.shape[1], w_hbm)
    mine = pl.ds(pl.multiple_of(me % 2 * width, 128), width)
    theirs = pl.ds(pl.multiple_of((me + 1) % 2 * width, 128), width)
    og_v[mine] = own_ref[...]
    og_v[theirs] = mate_ref[...].T

    def body(i, weights):
        acc_ref[step.units(i)] = product(weights[...], og_v[...])

    later = [near.copies(k, near_ref.at[k], near_sems.at[k]) for k in range(near_ref.shape[0])]
    stream(step, 3, acc_ref.shape[0] // step.block, head_ref, w_v, sems, body, later)


def near_kernel(acc_in, og_ref, head_ref, w_hbm, acc_ref, far_ref, og_v, w_v, sems, far_sems):
    me = lax.axis_index("tensor")
    heads, block, width = head_ref.shape
    near, far = Step(me ^ 2, width, block, w_hbm), Step(me ^ 3, width, block, w_hbm)
    rest = [near.copies(heads + k, w_v.at[k], sems.at[k]) for k in range(w_v.shape[0])]
    later = [far.copies(k, far_ref.at[k], far_sems.at[k]) for k in range(far_ref.shape[0])]
    for group in rest + later:
        start(group)
    og_v[...] = og_ref[...].T

    def body(i, weights):
        at = near.units(i)
        acc_ref[at] = acc_in[at] + product(weights, og_v[...])

    @pl.loop(0, heads)
    def _(i):
        body(i, head_ref[i])

    for group in rest:
        wait(group)

    @pl.loop(0, w_v.shape[0])
    def _(i):
        body(heads + i, w_v[i])

    for group in later:
        wait(group)


def far_kernel(acc_ref, og_ref, head_ref, w_hbm, a_ref, b_ref, gf_hbm, uf_hbm, gate_ref, up_ref,
               og_v, w_v, gf_ref, uf_ref, d_gate_v, d_up_v, sems, factor_sems):
    heads, block, width = head_ref.shape
    step = Step(lax.axis_index("tensor") ^ 3, width, block, w_hbm)
    factors = [
        pltpu.make_async_copy(src, dst, factor_sems.at[k]) for k, (src, dst) in enumerate(((gf_hbm, gf_ref), (uf_hbm, uf_ref)))
    ]
    start(step.copies(heads, w_v.at[0], sems.at[0]))
    start(factors)
    og_v[...] = og_ref[...].T

    def body(i, weights):
        at = step.units(i)
        hidden_grad = acc_ref[at] + product(weights, og_v[...])
        d_gate_v[at] = (hidden_grad * a_ref[at]).astype(BF16)
        d_up_v[at] = (hidden_grad * b_ref[at]).astype(BF16)

    @pl.loop(0, heads)
    def _(i):
        @pl.when((i > 0) & (i < w_v.shape[0]))
        def _():
            start(step.copies(heads + i, w_v.at[i], sems.at[i]))

        body(i, head_ref[i])

    @pl.loop(0, w_v.shape[0])
    def _(i):
        wait(step.copies(heads + i, w_v.at[i], sems.at[i]))
        body(heads + i, w_v[i])

    wait(factors)
    gate_ref[...] = product(gf_ref[...], d_gate_v[...])
    up_ref[...] = product(uf_ref[...], d_up_v[...])


def after_kernel(array_ref, token_ref, same_ref):
    pass


def chip_kernel(mine_ref, theirs_ref, token_ref, chip_ref):
    chip_ref[...] = mine_ref[...] + theirs_ref[...]


def gradients_kernel(chip_ref, other_ref, gate_ref, up_ref, ph_ref, share_ref):
    rank = ph_ref.shape[0]
    total = chip_ref[...] + other_ref[...]
    highest = lax.Precision.HIGHEST
    for s in range(SEQS):
        at = slice(s * LEN, (s + 1) * LEN)
        out = slice(s * rank, (s + 1) * rank)
        share_ref[out, :rank] = rows_by_rows(total[:rank, at], gate_ref[:, at], highest)
        share_ref[out, rank:] = rows_by_rows(total[:rank, at], up_ref[:, at], highest)
        share_ref[SEQS * rank :, out] = rows_by_rows(ph_ref[:, at], total[rank:, at], highest)


def sum_kernel(mine_ref, theirs_ref, gate_ref, up_ref, down_ref):
    rank = gate_ref.shape[1]
    total = mine_ref[...].astype(F32) + theirs_ref[...].astype(F32)
    for s in range(SEQS):
        gate_ref[s] = total[s * rank : (s + 1) * rank, :rank]
        up_ref[s] = total[s * rank : (s + 1) * rank, rank:]
        down_ref[s] = total[SEQS * rank :, s * rank : (s + 1) * rank]


def fast(x_in, out_grad, gate_pre, up_pre, down_weight, x_factor, gate_factor, up_factor, h_factor, dy_factor):
    tokens, width = out_grad.shape
    units, rank = h_factor.shape
    dma = pltpu.SemaphoreType.DMA

    def in_hbm(array):
        return pltpu.with_memory_space_constraint(array, pltpu.HBM)

    def swap(array, bits):
        return lax.ppermute(array, "tensor", [(i, i ^ bits) for i in range(4)])

    def call(kernel, out_shape, in_specs, scratch, mib, flops=0, moved=0, **kwargs):
        several = isinstance(out_shape, tuple)
        return pl.pallas_call(
            kernel,
            out_shape=out_shape,
            in_specs=in_specs,
            out_specs=(VMEM,) * len(out_shape) if several else VMEM,
            scratch_shapes=list(scratch),
            compiler_params=pltpu.CompilerParams(vmem_limit_bytes=mib * MIB),
            cost_estimate=pl.CostEstimate(flops=flops, bytes_accessed=moved, transcendentals=0),
            **kwargs,
        )

    held = pltpu.VMEM((units, tokens), F32)
    per_product = 2 * tokens * width * units
    turns = units // BLOCK
    narrow = pltpu.VMEM((rank, tokens), F32)
    turned = pltpu.VMEM((width, tokens), BF16)
    weight = in_hbm(down_weight)

    def blocks(count):
        return pltpu.VMEM((count, BLOCK, width), BF16)

    def chip_blocks(count):
        return pltpu.VMEM((count, CHIP_BLOCK, 2 * width), BF16)

    near = swap(out_grad, 2)
    mate = swap(out_grad, 1)
    a, b, ph, pq, head, own = call(
        elementwise_kernel,
        (held, held, narrow, pltpu.VMEM((2 * rank, tokens), F32), chip_blocks(2), turned),
        [ANY] * 8,
        [
            pltpu.VMEM((tokens, width), BF16),
            pltpu.VMEM((tokens, width), BF16),
            pltpu.VMEM((turns, tokens, BLOCK), BF16),
            pltpu.VMEM((turns, tokens, BLOCK), BF16),
            pltpu.VMEM((rank, width), BF16),
            pltpu.VMEM((rank, width), BF16),
            pltpu.VMEM((rank, units), BF16),
            dma((5,)),
            dma((turns,)),
            dma((turns,)),
            dma((2, PARTS)),
        ],
        14,
        per_product // 4,
        4 * units * tokens,
    )(
        in_hbm(x_in),
        in_hbm(out_grad),
        in_hbm(gate_pre),
        in_hbm(up_pre),
        weight,
        in_hbm(x_factor.T),
        in_hbm(dy_factor.T),
        in_hbm(h_factor.T),
    )
    pq_mate = swap(pq, 1)
    acc, head = call(
        chip_features_kernel,
        (held, blocks(turns - 1)),
        [VMEM] * 3 + [ANY],
        [
            pltpu.VMEM((2 * width, tokens), BF16),
            chip_blocks(4),
            dma((units // CHIP_BLOCK, PARTS)),
            dma((turns - 1, PARTS)),
        ],
        14,
        2 * per_product,
        4 * units * width,
    )(own, mate, head, weight)

    def after(array, token):
        return pl.pallas_call(
            after_kernel,
            out_shape=pltpu.VMEM(array.shape, array.dtype),
            in_specs=[ANY, ANY],
            out_specs=ANY,
            input_output_aliases={0: 0},
            compiler_params=pltpu.CompilerParams(vmem_limit_bytes=MIB),
        )(array, token)

    chip = call(chip_kernel, pltpu.VMEM(pq.shape, F32), [VMEM, VMEM, ANY], [], 1)(pq, pq_mate, head)
    near = after(near, chip)
    far = swap(near, 1)
    acc, head = call(
        near_kernel,
        (held, blocks(2)),
        [VMEM] * 3 + [ANY],
        [turned, blocks(1), dma((1, PARTS)), dma((2, PARTS))],
        6,
        per_product,
        2 * units * width,
        input_output_aliases={0: 0},
    )(acc, near, head, weight)
    chip = after(chip, head)
    chip_across = swap(chip, 2)
    factor = pltpu.VMEM((rank, units), BF16)
    kept = pltpu.VMEM((units, tokens), BF16)
    q_gate, q_up = call(
        far_kernel,
        (narrow, narrow),
        [VMEM] * 3 + [ANY] + [VMEM] * 2 + [ANY] * 2,
        [turned, blocks(turns - 2), factor, factor, kept, kept, dma((turns - 2, PARTS)), dma((2,))],
        16,
        per_product,
        2 * units * width,
    )(acc, far, head, weight, a, b, in_hbm(gate_factor.T), in_hbm(up_factor.T))
    share = call(gradients_kernel, pltpu.VMEM(((SEQS + 1) * rank, 2 * rank), F32), [VMEM] * 5, [], 4)(
        chip, chip_across, q_gate, q_up, ph
    )
    chip_share = (share + swap(share, 1)).astype(BF16)
    out = jax.ShapeDtypeStruct((SEQS, rank, rank), F32)
    return call(sum_kernel, (out, out, out), [VMEM] * 2, [], 4)(chip_share, swap(chip_share, 2))


def solution(mesh):
    def per_device(*arrays):
        (tokens, width), (units, rank) = arrays[1].shape, arrays[8].shape
        fits = (
            mesh.shape["tensor"] == 4
            and (tokens, rank) == (SEQS * LEN, LEN // 2)
            and width % 128 == 0
            and units % BLOCK == 0
            and units % CHIP_BLOCK == 0
            and units // BLOCK == 4
        )
        return tuple((fast if fits else plain)(*arrays))

    return jax.shard_map(
        per_device,
        mesh=mesh,
        in_specs=(P("dp", "tensor"),) * 4 + (P("tensor", None),) * 6,
        out_specs=(P("dp", None, None),) * 3,
        check_vma=False,
    )
```

```python
import jax
import jax.numpy as jnp
from jax import lax
from jax.experimental import pallas as pl
from jax.experimental.pallas import tpu as pltpu
from jax.sharding import PartitionSpec as P

SEQS = 2
LEN = 128
BLOCK = 1152
CHIP_BLOCK = 512
PARTS = 2
MIB = 1 << 20
ANY = pl.BlockSpec(memory_space=pl.ANY)
VMEM = pl.BlockSpec(memory_space=pltpu.VMEM)
BF16 = jnp.bfloat16
F32 = jnp.float32


def product(left, right):
    return jnp.dot(left, right, preferred_element_type=F32)


def rows_by_rows(left, right, precision=None):
    return lax.dot_general(
        left, right, (((1,), (1,)), ((), ())), precision=precision, preferred_element_type=F32
    )


def per_sequence(matrix):
    return matrix.reshape(SEQS, matrix.shape[0] // SEQS, matrix.shape[1])


def plain(x_in, out_grad, gate_pre, up_pre, down_weight, x_factor, gate_factor, up_factor, h_factor, dy_factor):
    hidden_grad = rows_by_rows(lax.all_gather(out_grad, "tensor", axis=1, tiled=True), down_weight)
    gate_val = gate_pre.astype(F32)
    up_val = up_pre.astype(F32)
    sigmoid_gate = jax.nn.sigmoid(gate_val)
    silu_gate = gate_val * sigmoid_gate
    hidden = (silu_gate * up_val).astype(BF16)
    d_gate = (hidden_grad * up_val * sigmoid_gate * (1.0 + gate_val * (1.0 - sigmoid_gate))).astype(BF16)
    d_up = (hidden_grad * silu_gate).astype(BF16)
    rows = [
        product(x_in, x_factor),
        product(d_gate, gate_factor),
        product(d_up, up_factor),
        product(hidden, h_factor),
        product(out_grad, dy_factor),
    ]
    totals = lax.psum(jnp.stack(rows), "tensor")
    p_x, q_gate, q_up, p_h, q_y = [per_sequence(totals[i]) for i in range(5)]
    highest = lax.Precision.HIGHEST
    return (
        jnp.einsum("sli,slj->sij", p_x, q_gate, precision=highest),
        jnp.einsum("sli,slj->sij", p_x, q_up, precision=highest),
        jnp.einsum("sli,slj->sij", p_h, q_y, precision=highest),
    )


class Step:
    def __init__(self, owner, width, block, w_hbm):
        self.owner, self.width, self.block, self.w_hbm = owner, width, block, w_hbm

    def units(self, i):
        return pl.ds(pl.multiple_of(i * self.block, self.block), self.block)

    def copies(self, i, dst, sems):
        columns = pl.ds(pl.multiple_of(self.owner * self.width, 128), self.width)
        part = self.block // PARTS
        return [
            pltpu.make_async_copy(
                self.w_hbm.at[pl.ds(pl.multiple_of(i * self.block + k * part, part), part), columns],
                dst.at[pl.ds(k * part, part)],
                sems.at[k],
            )
            for k in range(PARTS)
        ]


def start(copies):
    for copy in copies:
        copy.start()


def wait(copies):
    for copy in copies:
        copy.wait()


def stream(step, ahead, blocks, head, w_v, sems, body, later):
    heads = head.shape[0]
    slots = w_v.shape[0]

    def copies(j):
        return step.copies(j, w_v.at[(j - heads) % slots], sems.at[j])

    def begin(j):
        @pl.when(j < blocks)
        def _():
            start(copies(j))

        for k, group in enumerate(later):

            @pl.when(j == blocks + k)
            def _():
                start(group)

    for j in range(heads, ahead):
        start(copies(j))

    @pl.loop(0, heads)
    def _(i):
        begin(i + ahead)
        body(i, head.at[i])

    @pl.loop(heads, blocks)
    def _(i):
        begin(i + ahead)
        wait(copies(i))
        body(i, w_v.at[(i - heads) % slots])

    for k, group in enumerate(later):
        if k >= ahead:
            start(group)
    for group in later:
        wait(group)


def elementwise_kernel(x_hbm, og_hbm, gate_hbm, up_hbm, w_hbm, xf_hbm, yf_hbm, hf_hbm,
                       a_ref, b_ref, ph_ref, pq_ref, head_ref, own_ref,
                       x_v, og_v, gate_v, up_v, xf_v, yf_v, hf_v, sems, gate_sems, up_sems, w_sems):
    units = a_ref.shape[0]
    rank = ph_ref.shape[0]
    turns = units // BLOCK

    def at(i):
        return pl.ds(pl.multiple_of(i * BLOCK, BLOCK), BLOCK)

    def gate_up(i):
        return [
            pltpu.make_async_copy(gate_hbm.at[:, at(i)], gate_v.at[i], gate_sems.at[i]),
            pltpu.make_async_copy(up_hbm.at[:, at(i)], up_v.at[i], up_sems.at[i]),
        ]

    pairs = ((hf_hbm, hf_v), (og_hbm, og_v), (x_hbm, x_v), (xf_hbm, xf_v), (yf_hbm, yf_v))
    small = [pltpu.make_async_copy(src, dst, sems.at[i]) for i, (src, dst) in enumerate(pairs)]
    following = Step(lax.axis_index("tensor") // 2, head_ref.shape[2], head_ref.shape[1], w_hbm)
    heads = head_ref.shape[0]

    start(gate_up(0))
    start(small[:1])
    for i in range(1, turns):
        start(gate_up(i))
    start(small[1:])
    for i in range(heads):
        start(following.copies(i, head_ref.at[i], w_sems.at[i]))
    ph_ref[...] = jnp.zeros_like(ph_ref)
    wait(gate_up(0))
    wait(small[:1])

    @pl.loop(0, turns)
    def _(i):
        @pl.when(i > 0)
        def _():
            wait(gate_up(i))

        g = gate_v[i].T.astype(F32)
        u = up_v[i].T.astype(F32)
        s = 0.5 * jnp.tanh(0.5 * g) + 0.5
        silu = g * s
        a_ref[at(i)] = u * s * ((1.0 + g) - silu)
        b_ref[at(i)] = silu
        ph_ref[...] += product(hf_v[:, at(i)], (silu * u).astype(BF16))

    wait(small[1:])
    pq_ref[:rank] = rows_by_rows(xf_v[...], x_v[...])
    own_ref[...] = og_v[...].T
    pq_ref[rank:] = product(yf_v[...], own_ref[...])
    for i in range(heads):
        wait(following.copies(i, head_ref.at[i], w_sems.at[i]))


def chip_features_kernel(own_ref, mate_ref, head_ref, w_hbm, acc_ref, near_ref, og_v, w_v, sems, near_sems):
    me = lax.axis_index("tensor")
    width = own_ref.shape[0]
    step = Step(me // 2, 2 * width, w_v.shape[1], w_hbm)
    near = Step(me ^ 2, width, near_ref.shape[1], w_hbm)
    mine = pl.ds(pl.multiple_of(me % 2 * width, 128), width)
    theirs = pl.ds(pl.multiple_of((me + 1) % 2 * width, 128), width)
    og_v[mine] = own_ref[...]
    og_v[theirs] = mate_ref[...].T

    def body(i, weights):
        acc_ref[step.units(i)] = product(weights[...], og_v[...])

    later = [near.copies(k, near_ref.at[k], near_sems.at[k]) for k in range(near_ref.shape[0])]
    stream(step, 3, acc_ref.shape[0] // step.block, head_ref, w_v, sems, body, later)


def near_kernel(acc_in, og_ref, head_ref, w_hbm, acc_ref, far_ref, og_v, w_v, sems, far_sems):
    me = lax.axis_index("tensor")
    heads, block, width = head_ref.shape
    near, far = Step(me ^ 2, width, block, w_hbm), Step(me ^ 3, width, block, w_hbm)
    rest = [near.copies(heads + k, w_v.at[k], sems.at[k]) for k in range(w_v.shape[0])]
    later = [far.copies(k, far_ref.at[k], far_sems.at[k]) for k in range(far_ref.shape[0])]
    for group in rest + later:
        start(group)
    og_v[...] = og_ref[...].T

    def body(i, weights):
        at = near.units(i)
        acc_ref[at] = acc_in[at] + product(weights, og_v[...])

    @pl.loop(0, heads)
    def _(i):
        body(i, head_ref[i])

    for group in rest:
        wait(group)

    @pl.loop(0, w_v.shape[0])
    def _(i):
        body(heads + i, w_v[i])

    for group in later:
        wait(group)


def far_kernel(acc_ref, og_ref, head_ref, w_hbm, a_ref, b_ref, gf_hbm, uf_hbm, q_ref,
               og_v, w_v, factors_v, d_v, sems, factor_sems):
    heads, block, width = head_ref.shape
    step = Step(lax.axis_index("tensor") ^ 3, width, block, w_hbm)
    rank, tokens = q_ref.shape[0] // 2, q_ref.shape[1]
    factors = [
        pltpu.make_async_copy(src, factors_v.at[pl.ds(k * rank, rank)], factor_sems.at[k])
        for k, src in enumerate((gf_hbm, uf_hbm))
    ]
    start(step.copies(heads, w_v.at[0], sems.at[0]))
    start(factors)
    og_v[...] = og_ref[...].T

    def body(i, weights):
        at = step.units(i)
        hidden_grad = acc_ref[at] + product(weights, og_v[...])
        d_v[at, :tokens] = (hidden_grad * a_ref[at]).astype(BF16)
        d_v[at, tokens:] = (hidden_grad * b_ref[at]).astype(BF16)

    @pl.loop(0, heads)
    def _(i):
        @pl.when((i > 0) & (i < w_v.shape[0]))
        def _():
            start(step.copies(heads + i, w_v.at[i], sems.at[i]))

        body(i, head_ref[i])

    @pl.loop(0, w_v.shape[0])
    def _(i):
        wait(step.copies(heads + i, w_v.at[i], sems.at[i]))
        body(heads + i, w_v[i])

    wait(factors)
    both = product(factors_v[...], d_v[...])
    q_ref[:rank] = both[:rank, :tokens]
    q_ref[rank:] = both[rank:, tokens:]


def after_kernel(array_ref, token_ref, same_ref):
    pass


def chip_kernel(mine_ref, theirs_ref, token_ref, chip_ref):
    chip_ref[...] = mine_ref[...] + theirs_ref[...]


def gradients_kernel(chip_ref, other_ref, q_ref, ph_ref, share_ref):
    rank = ph_ref.shape[0]
    total = chip_ref[...] + other_ref[...]
    highest = lax.Precision.HIGHEST
    for s in range(SEQS):
        at = slice(s * LEN, (s + 1) * LEN)
        out = slice(s * rank, (s + 1) * rank)
        share_ref[out] = rows_by_rows(total[:rank, at], q_ref[:, at], highest)
        share_ref[SEQS * rank :, out] = rows_by_rows(ph_ref[:, at], total[rank:, at], highest)


def sum_kernel(mine_ref, theirs_ref, gate_ref, up_ref, down_ref):
    rank = gate_ref.shape[1]
    total = mine_ref[...].astype(F32) + theirs_ref[...].astype(F32)
    for s in range(SEQS):
        gate_ref[s] = total[s * rank : (s + 1) * rank, :rank]
        up_ref[s] = total[s * rank : (s + 1) * rank, rank:]
        down_ref[s] = total[SEQS * rank :, s * rank : (s + 1) * rank]


def fast(x_in, out_grad, gate_pre, up_pre, down_weight, x_factor, gate_factor, up_factor, h_factor, dy_factor):
    tokens, width = out_grad.shape
    units, rank = h_factor.shape
    dma = pltpu.SemaphoreType.DMA

    def in_hbm(array):
        return pltpu.with_memory_space_constraint(array, pltpu.HBM)

    def swap(array, bits):
        return lax.ppermute(array, "tensor", [(i, i ^ bits) for i in range(4)])

    def call(kernel, out_shape, in_specs, scratch, mib, flops=0, moved=0, **kwargs):
        several = isinstance(out_shape, tuple)
        return pl.pallas_call(
            kernel,
            out_shape=out_shape,
            in_specs=in_specs,
            out_specs=(VMEM,) * len(out_shape) if several else VMEM,
            scratch_shapes=list(scratch),
            compiler_params=pltpu.CompilerParams(vmem_limit_bytes=mib * MIB),
            cost_estimate=pl.CostEstimate(flops=flops, bytes_accessed=moved, transcendentals=0),
            **kwargs,
        )

    held = pltpu.VMEM((units, tokens), F32)
    per_product = 2 * tokens * width * units
    turns = units // BLOCK
    narrow = pltpu.VMEM((rank, tokens), F32)
    turned = pltpu.VMEM((width, tokens), BF16)
    weight = in_hbm(down_weight)

    def blocks(count):
        return pltpu.VMEM((count, BLOCK, width), BF16)

    def chip_blocks(count):
        return pltpu.VMEM((count, CHIP_BLOCK, 2 * width), BF16)

    near = swap(out_grad, 2)
    mate = swap(out_grad, 1)
    a, b, ph, pq, head, own = call(
        elementwise_kernel,
        (held, held, narrow, pltpu.VMEM((2 * rank, tokens), F32), chip_blocks(2), turned),
        [ANY] * 8,
        [
            pltpu.VMEM((tokens, width), BF16),
            pltpu.VMEM((tokens, width), BF16),
            pltpu.VMEM((turns, tokens, BLOCK), BF16),
            pltpu.VMEM((turns, tokens, BLOCK), BF16),
            pltpu.VMEM((rank, width), BF16),
            pltpu.VMEM((rank, width), BF16),
            pltpu.VMEM((rank, units), BF16),
            dma((5,)),
            dma((turns,)),
            dma((turns,)),
            dma((2, PARTS)),
        ],
        14,
        per_product // 4,
        4 * units * tokens,
    )(
        in_hbm(x_in),
        in_hbm(out_grad),
        in_hbm(gate_pre),
        in_hbm(up_pre),
        weight,
        in_hbm(x_factor.T),
        in_hbm(dy_factor.T),
        in_hbm(h_factor.T),
    )
    pq_mate = swap(pq, 1)
    acc, head = call(
        chip_features_kernel,
        (held, blocks(turns - 1)),
        [VMEM] * 3 + [ANY],
        [
            pltpu.VMEM((2 * width, tokens), BF16),
            chip_blocks(4),
            dma((units // CHIP_BLOCK, PARTS)),
            dma((turns - 1, PARTS)),
        ],
        14,
        2 * per_product,
        4 * units * width,
    )(own, mate, head, weight)

    def after(array, token):
        return pl.pallas_call(
            after_kernel,
            out_shape=pltpu.VMEM(array.shape, array.dtype),
            in_specs=[ANY, ANY],
            out_specs=ANY,
            input_output_aliases={0: 0},
            compiler_params=pltpu.CompilerParams(vmem_limit_bytes=MIB),
        )(array, token)

    chip = call(chip_kernel, pltpu.VMEM(pq.shape, F32), [VMEM, VMEM, ANY], [], 1)(pq, pq_mate, head)
    near = after(near, chip)
    far = swap(near, 1)
    acc, head = call(
        near_kernel,
        (held, blocks(2)),
        [VMEM] * 3 + [ANY],
        [turned, blocks(1), dma((1, PARTS)), dma((2, PARTS))],
        6,
        per_product,
        2 * units * width,
        input_output_aliases={0: 0},
    )(acc, near, head, weight)
    chip = after(chip, head)
    chip_across = swap(chip, 2)
    q = call(
        far_kernel,
        pltpu.VMEM((2 * rank, tokens), F32),
        [VMEM] * 3 + [ANY] + [VMEM] * 2 + [ANY] * 2,
        [turned, blocks(turns - 2), pltpu.VMEM((2 * rank, units), BF16), pltpu.VMEM((units, 2 * tokens), BF16), dma((turns - 2, PARTS)), dma((2,))],
        16,
        per_product,
        2 * units * width,
    )(acc, far, head, weight, a, b, in_hbm(gate_factor.T), in_hbm(up_factor.T))
    share = call(gradients_kernel, pltpu.VMEM(((SEQS + 1) * rank, 2 * rank), F32), [VMEM] * 4, [], 4)(chip, chip_across, q, ph)
    chip_share = (share + swap(share, 1)).astype(BF16)
    out = jax.ShapeDtypeStruct((SEQS, rank, rank), F32)
    return call(sum_kernel, (out, out, out), [VMEM] * 2, [], 4)(chip_share, swap(chip_share, 2))


def solution(mesh):
    def per_device(*arrays):
        (tokens, width), (units, rank) = arrays[1].shape, arrays[8].shape
        fits = (
            mesh.shape["tensor"] == 4
            and (tokens, rank) == (SEQS * LEN, LEN // 2)
            and width % 128 == 0
            and units % BLOCK == 0
            and units % CHIP_BLOCK == 0
            and units // BLOCK == 4
        )
        return tuple((fast if fits else plain)(*arrays))

    return jax.shard_map(
        per_device,
        mesh=mesh,
        in_specs=(P("dp", "tensor"),) * 4 + (P("tensor", None),) * 6,
        out_specs=(P("dp", None, None),) * 3,
        check_vma=False,
    )
```

```python
import jax
import jax.numpy as jnp
from jax import lax
from jax.experimental import pallas as pl
from jax.experimental.pallas import tpu as pltpu
from jax.sharding import PartitionSpec as P

SEQS = 2
LEN = 128
BLOCK = 1152
CHIP_BLOCK = 512
FAR_BLOCK = 768
NEAR = 1024
PARTS = 2
MIB = 1 << 20
ANY = pl.BlockSpec(memory_space=pl.ANY)
VMEM = pl.BlockSpec(memory_space=pltpu.VMEM)
BF16 = jnp.bfloat16
F32 = jnp.float32


def product(left, right):
    return jnp.dot(left, right, preferred_element_type=F32)


def rows_by_rows(left, right, precision=None):
    return lax.dot_general(
        left, right, (((1,), (1,)), ((), ())), precision=precision, preferred_element_type=F32
    )


def per_sequence(matrix):
    return matrix.reshape(SEQS, matrix.shape[0] // SEQS, matrix.shape[1])


def plain(x_in, out_grad, gate_pre, up_pre, down_weight, x_factor, gate_factor, up_factor, h_factor, dy_factor):
    hidden_grad = rows_by_rows(lax.all_gather(out_grad, "tensor", axis=1, tiled=True), down_weight)
    gate_val = gate_pre.astype(F32)
    up_val = up_pre.astype(F32)
    sigmoid_gate = jax.nn.sigmoid(gate_val)
    silu_gate = gate_val * sigmoid_gate
    hidden = (silu_gate * up_val).astype(BF16)
    d_gate = (hidden_grad * up_val * sigmoid_gate * (1.0 + gate_val * (1.0 - sigmoid_gate))).astype(BF16)
    d_up = (hidden_grad * silu_gate).astype(BF16)
    rows = [
        product(x_in, x_factor),
        product(d_gate, gate_factor),
        product(d_up, up_factor),
        product(hidden, h_factor),
        product(out_grad, dy_factor),
    ]
    totals = lax.psum(jnp.stack(rows), "tensor")
    p_x, q_gate, q_up, p_h, q_y = [per_sequence(totals[i]) for i in range(5)]
    highest = lax.Precision.HIGHEST
    return (
        jnp.einsum("sli,slj->sij", p_x, q_gate, precision=highest),
        jnp.einsum("sli,slj->sij", p_x, q_up, precision=highest),
        jnp.einsum("sli,slj->sij", p_h, q_y, precision=highest),
    )


class Step:
    def __init__(self, column, width, block, w_hbm):
        self.column, self.width, self.block, self.w_hbm = column, width, block, w_hbm

    def units(self, i):
        return pl.ds(pl.multiple_of(i * self.block, self.block), self.block)

    def copies(self, i, dst, sems):
        columns = pl.ds(pl.multiple_of(self.column, 128), self.width)
        part = self.block // PARTS
        return [
            pltpu.make_async_copy(
                self.w_hbm.at[pl.ds(pl.multiple_of(i * self.block + k * part, part), part), columns],
                dst.at[pl.ds(k * part, part)],
                sems.at[k],
            )
            for k in range(PARTS)
        ]


def near_step(per_device, ref, w_hbm):
    me = lax.axis_index("tensor")
    return Step((1 - me // 2) * 2 * per_device + me % 2 * (2 * per_device - NEAR), NEAR, ref.shape[1], w_hbm)


def far_step(per_device, ref, w_hbm):
    me = lax.axis_index("tensor")
    return Step((1 - me // 2) * 2 * per_device + (1 - me % 2) * NEAR, 2 * per_device - NEAR, ref.shape[1], w_hbm)


def start(copies):
    for copy in copies:
        copy.start()


def wait(copies):
    for copy in copies:
        copy.wait()


def stream(step, ahead, blocks, head, w_v, sems, body, later):
    heads = head.shape[0]
    slots = w_v.shape[0]

    def copies(j):
        return step.copies(j, w_v.at[(j - heads) % slots], sems.at[j])

    def begin(j):
        @pl.when(j < blocks)
        def _():
            start(copies(j))

        for k, group in enumerate(later):

            @pl.when(j == blocks + k)
            def _():
                start(group)

    for j in range(heads, ahead):
        start(copies(j))

    @pl.loop(0, heads)
    def _(i):
        begin(i + ahead)
        body(i, head.at[i])

    @pl.loop(heads, blocks)
    def _(i):
        begin(i + ahead)
        wait(copies(i))
        body(i, w_v.at[(i - heads) % slots])

    for k, group in enumerate(later):
        if k >= ahead:
            start(group)
    for group in later:
        wait(group)


def elementwise_kernel(x_hbm, og_hbm, gate_hbm, up_hbm, w_hbm, xf_hbm, yf_hbm, hf_hbm,
                       a_ref, b_ref, ph_ref, pq_ref, head_ref, own_ref,
                       x_v, og_v, gate_v, up_v, xf_v, yf_v, hf_v, sems, gate_sems, up_sems, w_sems):
    units = a_ref.shape[0]
    rank = ph_ref.shape[0]
    turns = units // BLOCK

    def at(i):
        return pl.ds(pl.multiple_of(i * BLOCK, BLOCK), BLOCK)

    def gate_up(i):
        return [
            pltpu.make_async_copy(gate_hbm.at[:, at(i)], gate_v.at[i], gate_sems.at[i]),
            pltpu.make_async_copy(up_hbm.at[:, at(i)], up_v.at[i], up_sems.at[i]),
        ]

    pairs = ((hf_hbm, hf_v), (og_hbm, og_v), (x_hbm, x_v), (xf_hbm, xf_v), (yf_hbm, yf_v))
    small = [pltpu.make_async_copy(src, dst, sems.at[i]) for i, (src, dst) in enumerate(pairs)]
    following = Step(lax.axis_index("tensor") // 2 * head_ref.shape[2], head_ref.shape[2], head_ref.shape[1], w_hbm)
    heads = head_ref.shape[0]

    start(gate_up(0))
    start(small[:1])
    for i in range(1, turns):
        start(gate_up(i))
    start(small[1:])
    for i in range(heads):
        start(following.copies(i, head_ref.at[i], w_sems.at[i]))
    ph_ref[...] = jnp.zeros_like(ph_ref)
    wait(gate_up(0))
    wait(small[:1])

    @pl.loop(0, turns)
    def _(i):
        @pl.when(i > 0)
        def _():
            wait(gate_up(i))

        g = gate_v[i].T.astype(F32)
        u = up_v[i].T.astype(F32)
        s = 0.5 * jnp.tanh(0.5 * g) + 0.5
        silu = g * s
        a_ref[at(i)] = u * s * ((1.0 + g) - silu)
        b_ref[at(i)] = silu
        ph_ref[...] += product(hf_v[:, at(i)], (silu * u).astype(BF16))

    wait(small[1:])
    pq_ref[:rank] = rows_by_rows(xf_v[...], x_v[...])
    own_ref[...] = og_v[...].T
    pq_ref[rank:] = product(yf_v[...], own_ref[...])
    for i in range(heads):
        wait(following.copies(i, head_ref.at[i], w_sems.at[i]))


def chip_features_kernel(own_ref, mate_ref, head_ref, w_hbm, acc_ref, near_ref, og_v, w_v, sems, near_sems):
    me = lax.axis_index("tensor")
    width = own_ref.shape[0]
    step = Step(me // 2 * 2 * width, 2 * width, w_v.shape[1], w_hbm)
    near = near_step(width, near_ref, w_hbm)
    mine = pl.ds(pl.multiple_of(me % 2 * width, 128), width)
    theirs = pl.ds(pl.multiple_of((me + 1) % 2 * width, 128), width)
    og_v[mine] = own_ref[...]
    og_v[theirs] = mate_ref[...].T

    def body(i, weights):
        acc_ref[step.units(i)] = product(weights[...], og_v[...])

    later = [near.copies(k, near_ref.at[k], near_sems.at[k]) for k in range(near_ref.shape[0])]
    stream(step, 3, acc_ref.shape[0] // step.block, head_ref, w_v, sems, body, later)


def near_kernel(acc_in, og_ref, head_ref, w_hbm, acc_ref, left_ref, far_ref, og_v, far_sems):
    core = lax.axis_index("tensor") % 2
    width = og_ref.shape[1]
    step = near_step(width, head_ref, w_hbm)
    far = far_step(width, far_ref, w_hbm)
    later = [far.copies(k, far_ref.at[k], far_sems.at[k]) for k in range(far_ref.shape[0])]
    for group in later:
        start(group)
    og_v[...] = og_ref[...].T
    left_ref[...] = og_v[pl.ds(pl.multiple_of((1 - core) * NEAR, 16), width - NEAR)]

    @pl.loop(0, head_ref.shape[0])
    def _(i):
        at = step.units(i)
        features = og_v[pl.ds(pl.multiple_of(core * (width - NEAR), 16), NEAR)]
        acc_ref[at] = acc_in[at] + product(head_ref[i], features)

    for group in later:
        wait(group)


def far_kernel(acc_ref, og_ref, left_ref, head_ref, w_hbm, a_ref, b_ref, gf_hbm, uf_hbm, gate_ref, up_ref,
               og_v, w_v, gf_ref, uf_ref, d_gate_v, d_up_v, sems, factor_sems):
    core = lax.axis_index("tensor") % 2
    heads = head_ref.shape[0]
    width, left = og_ref.shape[1], left_ref.shape[0]
    step = far_step(width, head_ref, w_hbm)
    factors = [
        pltpu.make_async_copy(src, dst, factor_sems.at[k]) for k, (src, dst) in enumerate(((gf_hbm, gf_ref), (uf_hbm, uf_ref)))
    ]
    rest = w_v.shape[0]
    ahead = rest - heads
    for k in range(ahead):
        start(step.copies(heads + k, w_v.at[k], sems.at[k]))
    start(factors)
    og_v[pl.ds(pl.multiple_of(core * width, 16), left)] = left_ref[...]
    og_v[pl.ds(pl.multiple_of((1 - core) * left, 16), width)] = og_ref[...].T

    def body(i, weights):
        at = step.units(i)
        hidden_grad = acc_ref[at] + product(weights, og_v[...])
        d_gate_v[at] = (hidden_grad * a_ref[at]).astype(BF16)
        d_up_v[at] = (hidden_grad * b_ref[at]).astype(BF16)

    @pl.loop(0, heads)
    def _(i):
        start(step.copies(heads + ahead + i, w_v.at[ahead + i], sems.at[ahead + i]))
        body(i, head_ref[i])

    @pl.loop(0, rest)
    def _(i):
        wait(step.copies(heads + i, w_v.at[i], sems.at[i]))
        body(heads + i, w_v[i])

    wait(factors)
    gate_ref[...] = product(gf_ref[...], d_gate_v[...])
    up_ref[...] = product(uf_ref[...], d_up_v[...])


def after_kernel(array_ref, token_ref, same_ref):
    pass


def chip_kernel(mine_ref, theirs_ref, token_ref, chip_ref):
    chip_ref[...] = mine_ref[...] + theirs_ref[...]


def gradients_kernel(chip_ref, other_ref, gate_ref, up_ref, ph_ref, share_ref):
    rank = ph_ref.shape[0]
    total = chip_ref[...] + other_ref[...]
    highest = lax.Precision.HIGHEST
    for s in range(SEQS):
        at = slice(s * LEN, (s + 1) * LEN)
        out = slice(s * rank, (s + 1) * rank)
        share_ref[out, :rank] = rows_by_rows(total[:rank, at], gate_ref[:, at], highest)
        share_ref[out, rank:] = rows_by_rows(total[:rank, at], up_ref[:, at], highest)
        share_ref[SEQS * rank :, out] = rows_by_rows(ph_ref[:, at], total[rank:, at], highest)


def sum_kernel(mine_ref, theirs_ref, gate_ref, up_ref, down_ref):
    rank = gate_ref.shape[1]
    total = mine_ref[...].astype(F32) + theirs_ref[...].astype(F32)
    for s in range(SEQS):
        gate_ref[s] = total[s * rank : (s + 1) * rank, :rank]
        up_ref[s] = total[s * rank : (s + 1) * rank, rank:]
        down_ref[s] = total[SEQS * rank :, s * rank : (s + 1) * rank]


def fast(x_in, out_grad, gate_pre, up_pre, down_weight, x_factor, gate_factor, up_factor, h_factor, dy_factor):
    tokens, width = out_grad.shape
    units, rank = h_factor.shape
    dma = pltpu.SemaphoreType.DMA

    def in_hbm(array):
        return pltpu.with_memory_space_constraint(array, pltpu.HBM)

    def swap(array, bits):
        return lax.ppermute(array, "tensor", [(i, i ^ bits) for i in range(4)])

    def call(kernel, out_shape, in_specs, scratch, mib, flops=0, moved=0, **kwargs):
        several = isinstance(out_shape, tuple)
        return pl.pallas_call(
            kernel,
            out_shape=out_shape,
            in_specs=in_specs,
            out_specs=(VMEM,) * len(out_shape) if several else VMEM,
            scratch_shapes=list(scratch),
            compiler_params=pltpu.CompilerParams(vmem_limit_bytes=mib * MIB),
            cost_estimate=pl.CostEstimate(flops=flops, bytes_accessed=moved, transcendentals=0),
            **kwargs,
        )

    held = pltpu.VMEM((units, tokens), F32)
    per_product = 2 * tokens * width * units
    turns = units // BLOCK
    narrow = pltpu.VMEM((rank, tokens), F32)
    turned = pltpu.VMEM((width, tokens), BF16)
    weight = in_hbm(down_weight)

    def chip_blocks(count):
        return pltpu.VMEM((count, CHIP_BLOCK, 2 * width), BF16)

    near = swap(out_grad, 2)
    mate = swap(out_grad, 1)
    a, b, ph, pq, head, own = call(
        elementwise_kernel,
        (held, held, narrow, pltpu.VMEM((2 * rank, tokens), F32), chip_blocks(2), turned),
        [ANY] * 8,
        [
            pltpu.VMEM((tokens, width), BF16),
            pltpu.VMEM((tokens, width), BF16),
            pltpu.VMEM((turns, tokens, BLOCK), BF16),
            pltpu.VMEM((turns, tokens, BLOCK), BF16),
            pltpu.VMEM((rank, width), BF16),
            pltpu.VMEM((rank, width), BF16),
            pltpu.VMEM((rank, units), BF16),
            dma((5,)),
            dma((turns,)),
            dma((turns,)),
            dma((2, PARTS)),
        ],
        14,
        per_product // 4,
        4 * units * tokens,
    )(
        in_hbm(x_in),
        in_hbm(out_grad),
        in_hbm(gate_pre),
        in_hbm(up_pre),
        weight,
        in_hbm(x_factor.T),
        in_hbm(dy_factor.T),
        in_hbm(h_factor.T),
    )
    pq_mate = swap(pq, 1)
    acc, head = call(
        chip_features_kernel,
        (held, pltpu.VMEM((turns, BLOCK, NEAR), BF16)),
        [VMEM] * 3 + [ANY],
        [
            pltpu.VMEM((2 * width, tokens), BF16),
            chip_blocks(4),
            dma((units // CHIP_BLOCK, PARTS)),
            dma((turns, PARTS)),
        ],
        14,
        2 * per_product,
        4 * units * width,
    )(own, mate, head, weight)

    def after(array, token):
        return pl.pallas_call(
            after_kernel,
            out_shape=pltpu.VMEM(array.shape, array.dtype),
            in_specs=[ANY, ANY],
            out_specs=ANY,
            input_output_aliases={0: 0},
            compiler_params=pltpu.CompilerParams(vmem_limit_bytes=MIB),
        )(array, token)

    chip = call(chip_kernel, pltpu.VMEM(pq.shape, F32), [VMEM, VMEM, ANY], [], 1)(pq, pq_mate, head)
    near = after(near, chip)
    far = swap(near, 1)
    wide = 2 * width - NEAR
    far_turns = units // FAR_BLOCK
    acc, left, head = call(
        near_kernel,
        (held, pltpu.VMEM((width - NEAR, tokens), BF16), pltpu.VMEM((2, FAR_BLOCK, wide), BF16)),
        [VMEM] * 3 + [ANY],
        [turned, dma((2, PARTS))],
        6,
        2 * tokens * NEAR * units,
        2 * units * NEAR,
        input_output_aliases={0: 0},
    )(acc, near, head, weight)
    chip = after(chip, head)
    chip_across = swap(chip, 2)
    factor = pltpu.VMEM((rank, units), BF16)
    kept = pltpu.VMEM((units, tokens), BF16)
    q_gate, q_up = call(
        far_kernel,
        (narrow, narrow),
        [VMEM] * 4 + [ANY] + [VMEM] * 2 + [ANY] * 2,
        [
            pltpu.VMEM((wide, tokens), BF16),
            pltpu.VMEM((far_turns - 2, FAR_BLOCK, wide), BF16),
            factor,
            factor,
            kept,
            kept,
            dma((far_turns - 2, PARTS)),
            dma((2,)),
        ],
        20,
        2 * tokens * wide * units,
        2 * units * wide,
    )(acc, far, left, head, weight, a, b, in_hbm(gate_factor.T), in_hbm(up_factor.T))
    share = call(gradients_kernel, pltpu.VMEM(((SEQS + 1) * rank, 2 * rank), F32), [VMEM] * 5, [], 4)(
        chip, chip_across, q_gate, q_up, ph
    )
    chip_share = (share + swap(share, 1)).astype(BF16)
    out = jax.ShapeDtypeStruct((SEQS, rank, rank), F32)
    return call(sum_kernel, (out, out, out), [VMEM] * 2, [], 4)(chip_share, swap(chip_share, 2))


def solution(mesh):
    def per_device(*arrays):
        (tokens, width), (units, rank) = arrays[1].shape, arrays[8].shape
        fits = (
            mesh.shape["tensor"] == 4
            and (tokens, rank) == (SEQS * LEN, LEN // 2)
            and width % 128 == 0
            and width > NEAR
            and units % BLOCK == 0
            and units % CHIP_BLOCK == 0
            and units // FAR_BLOCK == 6
            and units // BLOCK == 4
        )
        return tuple((fast if fits else plain)(*arrays))

    return jax.shard_map(
        per_device,
        mesh=mesh,
        in_specs=(P("dp", "tensor"),) * 4 + (P("tensor", None),) * 6,
        out_specs=(P("dp", None, None),) * 3,
        check_vma=False,
    )
```

```python
import jax
import jax.numpy as jnp
from jax import lax
from jax.experimental import pallas as pl
from jax.experimental.pallas import tpu as pltpu
from jax.sharding import PartitionSpec as P

SEQS = 2
LEN = 128
BLOCK = 1152
CHIP_BLOCK = 512
PARTS = 2
MIB = 1 << 20
ANY = pl.BlockSpec(memory_space=pl.ANY)
VMEM = pl.BlockSpec(memory_space=pltpu.VMEM)
BF16 = jnp.bfloat16
F32 = jnp.float32


def product(left, right):
    return jnp.dot(left, right, preferred_element_type=F32)


def rows_by_rows(left, right, precision=None):
    return lax.dot_general(
        left, right, (((1,), (1,)), ((), ())), precision=precision, preferred_element_type=F32
    )


def per_sequence(matrix):
    return matrix.reshape(SEQS, matrix.shape[0] // SEQS, matrix.shape[1])


def plain(x_in, out_grad, gate_pre, up_pre, down_weight, x_factor, gate_factor, up_factor, h_factor, dy_factor):
    hidden_grad = rows_by_rows(lax.all_gather(out_grad, "tensor", axis=1, tiled=True), down_weight)
    gate_val = gate_pre.astype(F32)
    up_val = up_pre.astype(F32)
    sigmoid_gate = jax.nn.sigmoid(gate_val)
    silu_gate = gate_val * sigmoid_gate
    hidden = (silu_gate * up_val).astype(BF16)
    d_gate = (hidden_grad * up_val * sigmoid_gate * (1.0 + gate_val * (1.0 - sigmoid_gate))).astype(BF16)
    d_up = (hidden_grad * silu_gate).astype(BF16)
    rows = [
        product(x_in, x_factor),
        product(d_gate, gate_factor),
        product(d_up, up_factor),
        product(hidden, h_factor),
        product(out_grad, dy_factor),
    ]
    totals = lax.psum(jnp.stack(rows), "tensor")
    p_x, q_gate, q_up, p_h, q_y = [per_sequence(totals[i]) for i in range(5)]
    highest = lax.Precision.HIGHEST
    return (
        jnp.einsum("sli,slj->sij", p_x, q_gate, precision=highest),
        jnp.einsum("sli,slj->sij", p_x, q_up, precision=highest),
        jnp.einsum("sli,slj->sij", p_h, q_y, precision=highest),
    )


class Step:
    def __init__(self, owner, width, block, w_hbm):
        self.owner, self.width, self.block, self.w_hbm = owner, width, block, w_hbm

    def units(self, i):
        return pl.ds(pl.multiple_of(i * self.block, self.block), self.block)

    def copies(self, i, dst, sems):
        columns = pl.ds(pl.multiple_of(self.owner * self.width, 128), self.width)
        part = self.block // PARTS
        return [
            pltpu.make_async_copy(
                self.w_hbm.at[pl.ds(pl.multiple_of(i * self.block + k * part, part), part), columns],
                dst.at[pl.ds(k * part, part)],
                sems.at[k],
            )
            for k in range(PARTS)
        ]


def start(copies):
    for copy in copies:
        copy.start()


def wait(copies):
    for copy in copies:
        copy.wait()


def stream(step, ahead, blocks, head, w_v, sems, body, later):
    heads = head.shape[0]
    slots = w_v.shape[0]

    def copies(j):
        return step.copies(j, w_v.at[(j - heads) % slots], sems.at[j])

    def begin(j):
        @pl.when(j < blocks)
        def _():
            start(copies(j))

        for k, group in enumerate(later):

            @pl.when(j == blocks + k)
            def _():
                start(group)

    for j in range(heads, ahead):
        start(copies(j))

    @pl.loop(0, heads)
    def _(i):
        begin(i + ahead)
        body(i, head.at[i])

    @pl.loop(heads, blocks)
    def _(i):
        begin(i + ahead)
        wait(copies(i))
        body(i, w_v.at[(i - heads) % slots])

    for k, group in enumerate(later):
        if k >= ahead:
            start(group)
    for group in later:
        wait(group)


def elementwise_kernel(x_hbm, og_hbm, gate_hbm, up_hbm, w_hbm, xf_hbm, yf_hbm, hf_hbm,
                       a_ref, b_ref, ph_ref, pq_ref, head_ref, own_ref,
                       x_v, og_v, gate_v, up_v, xf_v, yf_v, hf_v, sems, gate_sems, up_sems, w_sems):
    units = a_ref.shape[0]
    rank = ph_ref.shape[0]
    turns = units // BLOCK

    def at(i):
        return pl.ds(pl.multiple_of(i * BLOCK, BLOCK), BLOCK)

    def gate_up(i):
        return [
            pltpu.make_async_copy(gate_hbm.at[:, at(i)], gate_v.at[i], gate_sems.at[i]),
            pltpu.make_async_copy(up_hbm.at[:, at(i)], up_v.at[i], up_sems.at[i]),
        ]

    pairs = ((hf_hbm, hf_v), (og_hbm, og_v), (x_hbm, x_v), (xf_hbm, xf_v), (yf_hbm, yf_v))
    small = [pltpu.make_async_copy(src, dst, sems.at[i]) for i, (src, dst) in enumerate(pairs)]
    following = Step(lax.axis_index("tensor") // 2, head_ref.shape[2], head_ref.shape[1], w_hbm)
    heads = head_ref.shape[0]

    start(gate_up(0))
    start(small[:1])
    for i in range(1, turns):
        start(gate_up(i))
    start(small[1:])
    for i in range(heads):
        start(following.copies(i, head_ref.at[i], w_sems.at[i]))
    ph_ref[...] = jnp.zeros_like(ph_ref)
    wait(gate_up(0))
    wait(small[:1])

    @pl.loop(0, turns)
    def _(i):
        @pl.when(i > 0)
        def _():
            wait(gate_up(i))

        g = gate_v[i].T.astype(F32)
        u = up_v[i].T.astype(F32)
        s = 0.5 * jnp.tanh(0.5 * g) + 0.5
        silu = g * s
        a_ref[at(i)] = u * s * ((1.0 + g) - silu)
        b_ref[at(i)] = silu
        ph_ref[...] += product(hf_v[:, at(i)], (silu * u).astype(BF16))

    wait(small[1:])
    pq_ref[:rank] = rows_by_rows(xf_v[...], x_v[...])
    own_ref[...] = og_v[...].T
    pq_ref[rank:] = product(yf_v[...], own_ref[...])
    for i in range(heads):
        wait(following.copies(i, head_ref.at[i], w_sems.at[i]))


def chip_features_kernel(own_ref, mate_ref, head_ref, w_hbm, acc_ref, near_ref, og_v, w_v, sems, near_sems):
    me = lax.axis_index("tensor")
    width = own_ref.shape[0]
    step = Step(me // 2, 2 * width, w_v.shape[1], w_hbm)
    near = Step(me ^ 2, width, near_ref.shape[1], w_hbm)
    mine = pl.ds(pl.multiple_of(me % 2 * width, 128), width)
    theirs = pl.ds(pl.multiple_of((me + 1) % 2 * width, 128), width)
    og_v[mine] = own_ref[...]
    og_v[theirs] = mate_ref[...].T

    def body(i, weights):
        acc_ref[step.units(i)] = product(weights[...], og_v[...])

    later = [near.copies(k, near_ref.at[k], near_sems.at[k]) for k in range(near_ref.shape[0])]
    stream(step, 3, acc_ref.shape[0] // step.block, head_ref, w_v, sems, body, later)


def near_kernel(acc_in, og_ref, head_ref, w_hbm, acc_ref, far_ref, og_v, w_v, sems, far_sems):
    me = lax.axis_index("tensor")
    heads, block, width = head_ref.shape
    near, far = Step(me ^ 2, width, block, w_hbm), Step(me ^ 3, width, block, w_hbm)
    rest = [near.copies(heads + k, w_v.at[k], sems.at[k]) for k in range(w_v.shape[0])]
    later = [far.copies(k, far_ref.at[k], far_sems.at[k]) for k in range(far_ref.shape[0])]
    for group in rest + later:
        start(group)
    og_v[...] = og_ref[...].T

    def body(first, weights):
        rows = weights.shape[0] * block
        at = slice(first * block, first * block + rows)
        acc_ref[at] = acc_in[at] + product(weights.reshape(rows, width), og_v[...])

    body(0, head_ref[:2])
    body(2, head_ref[2:])
    for group in rest:
        wait(group)
    body(heads, w_v[...])

    for group in later:
        wait(group)


def far_kernel(acc_ref, og_ref, head_ref, w_hbm, a_ref, b_ref, gf_hbm, uf_hbm, gate_ref, up_ref,
               og_v, w_v, gf_ref, uf_ref, d_gate_v, d_up_v, sems, factor_sems):
    heads, block, width = head_ref.shape
    step = Step(lax.axis_index("tensor") ^ 3, width, block, w_hbm)
    factors = [
        pltpu.make_async_copy(src, dst, factor_sems.at[k]) for k, (src, dst) in enumerate(((gf_hbm, gf_ref), (uf_hbm, uf_ref)))
    ]
    def body(first, weights):
        rows = weights.shape[0] * block
        at = slice(first * block, first * block + rows)
        hidden_grad = acc_ref[at] + product(weights.reshape(rows, width), og_v[...])
        d_gate_v[at] = (hidden_grad * a_ref[at]).astype(BF16)
        d_up_v[at] = (hidden_grad * b_ref[at]).astype(BF16)

    rest = [step.copies(heads + k, w_v.at[k], sems.at[k]) for k in range(w_v.shape[0])]
    for group in rest:
        start(group)
    start(factors)
    og_v[...] = og_ref[...].T
    body(0, head_ref[...])
    for group in rest:
        wait(group)
    body(heads, w_v[...])
    wait(factors)
    gate_ref[...] = product(gf_ref[...], d_gate_v[...])
    up_ref[...] = product(uf_ref[...], d_up_v[...])


def after_kernel(array_ref, token_ref, same_ref):
    pass


def chip_kernel(mine_ref, theirs_ref, token_ref, chip_ref):
    chip_ref[...] = mine_ref[...] + theirs_ref[...]


def gradients_kernel(chip_ref, other_ref, gate_ref, up_ref, ph_ref, share_ref):
    rank = ph_ref.shape[0]
    total = chip_ref[...] + other_ref[...]
    highest = lax.Precision.HIGHEST
    for s in range(SEQS):
        at = slice(s * LEN, (s + 1) * LEN)
        out = slice(s * rank, (s + 1) * rank)
        share_ref[out, :rank] = rows_by_rows(total[:rank, at], gate_ref[:, at], highest)
        share_ref[out, rank:] = rows_by_rows(total[:rank, at], up_ref[:, at], highest)
        share_ref[SEQS * rank :, out] = rows_by_rows(ph_ref[:, at], total[rank:, at], highest)


def sum_kernel(mine_ref, theirs_ref, gate_ref, up_ref, down_ref):
    rank = gate_ref.shape[1]
    total = mine_ref[...].astype(F32) + theirs_ref[...].astype(F32)
    for s in range(SEQS):
        gate_ref[s] = total[s * rank : (s + 1) * rank, :rank]
        up_ref[s] = total[s * rank : (s + 1) * rank, rank:]
        down_ref[s] = total[SEQS * rank :, s * rank : (s + 1) * rank]


def fast(x_in, out_grad, gate_pre, up_pre, down_weight, x_factor, gate_factor, up_factor, h_factor, dy_factor):
    tokens, width = out_grad.shape
    units, rank = h_factor.shape
    dma = pltpu.SemaphoreType.DMA

    def in_hbm(array):
        return pltpu.with_memory_space_constraint(array, pltpu.HBM)

    def swap(array, bits):
        return lax.ppermute(array, "tensor", [(i, i ^ bits) for i in range(4)])

    def call(kernel, out_shape, in_specs, scratch, mib, flops=0, moved=0, **kwargs):
        several = isinstance(out_shape, tuple)
        return pl.pallas_call(
            kernel,
            out_shape=out_shape,
            in_specs=in_specs,
            out_specs=(VMEM,) * len(out_shape) if several else VMEM,
            scratch_shapes=list(scratch),
            compiler_params=pltpu.CompilerParams(vmem_limit_bytes=mib * MIB),
            cost_estimate=pl.CostEstimate(flops=flops, bytes_accessed=moved, transcendentals=0),
            **kwargs,
        )

    held = pltpu.VMEM((units, tokens), F32)
    per_product = 2 * tokens * width * units
    turns = units // BLOCK
    narrow = pltpu.VMEM((rank, tokens), F32)
    turned = pltpu.VMEM((width, tokens), BF16)
    weight = in_hbm(down_weight)

    def blocks(count):
        return pltpu.VMEM((count, BLOCK, width), BF16)

    def chip_blocks(count):
        return pltpu.VMEM((count, CHIP_BLOCK, 2 * width), BF16)

    near = swap(out_grad, 2)
    mate = swap(out_grad, 1)
    a, b, ph, pq, head, own = call(
        elementwise_kernel,
        (held, held, narrow, pltpu.VMEM((2 * rank, tokens), F32), chip_blocks(2), turned),
        [ANY] * 8,
        [
            pltpu.VMEM((tokens, width), BF16),
            pltpu.VMEM((tokens, width), BF16),
            pltpu.VMEM((turns, tokens, BLOCK), BF16),
            pltpu.VMEM((turns, tokens, BLOCK), BF16),
            pltpu.VMEM((rank, width), BF16),
            pltpu.VMEM((rank, width), BF16),
            pltpu.VMEM((rank, units), BF16),
            dma((5,)),
            dma((turns,)),
            dma((turns,)),
            dma((2, PARTS)),
        ],
        14,
        per_product // 4,
        4 * units * tokens,
    )(
        in_hbm(x_in),
        in_hbm(out_grad),
        in_hbm(gate_pre),
        in_hbm(up_pre),
        weight,
        in_hbm(x_factor.T),
        in_hbm(dy_factor.T),
        in_hbm(h_factor.T),
    )
    pq_mate = swap(pq, 1)
    acc, head = call(
        chip_features_kernel,
        (held, blocks(turns - 1)),
        [VMEM] * 3 + [ANY],
        [
            pltpu.VMEM((2 * width, tokens), BF16),
            chip_blocks(4),
            dma((units // CHIP_BLOCK, PARTS)),
            dma((turns - 1, PARTS)),
        ],
        14,
        2 * per_product,
        4 * units * width,
    )(own, mate, head, weight)

    def after(array, token):
        return pl.pallas_call(
            after_kernel,
            out_shape=pltpu.VMEM(array.shape, array.dtype),
            in_specs=[ANY, ANY],
            out_specs=ANY,
            input_output_aliases={0: 0},
            compiler_params=pltpu.CompilerParams(vmem_limit_bytes=MIB),
        )(array, token)

    chip = call(chip_kernel, pltpu.VMEM(pq.shape, F32), [VMEM, VMEM, ANY], [], 1)(pq, pq_mate, head)
    near = after(near, chip)
    far = swap(near, 1)
    acc, head = call(
        near_kernel,
        (held, blocks(2)),
        [VMEM] * 3 + [ANY],
        [turned, blocks(1), dma((1, PARTS)), dma((2, PARTS))],
        10,
        per_product,
        2 * units * width,
        input_output_aliases={0: 0},
    )(acc, near, head, weight)
    chip = after(chip, head)
    chip_across = swap(chip, 2)
    factor = pltpu.VMEM((rank, units), BF16)
    kept = pltpu.VMEM((units, tokens), BF16)
    q_gate, q_up = call(
        far_kernel,
        (narrow, narrow),
        [VMEM] * 3 + [ANY] + [VMEM] * 2 + [ANY] * 2,
        [turned, blocks(turns - 2), factor, factor, kept, kept, dma((turns - 2, PARTS)), dma((2,))],
        20,
        per_product,
        2 * units * width,
    )(acc, far, head, weight, a, b, in_hbm(gate_factor.T), in_hbm(up_factor.T))
    share = call(gradients_kernel, pltpu.VMEM(((SEQS + 1) * rank, 2 * rank), F32), [VMEM] * 5, [], 4)(
        chip, chip_across, q_gate, q_up, ph
    )
    chip_share = (share + swap(share, 1)).astype(BF16)
    out = jax.ShapeDtypeStruct((SEQS, rank, rank), F32)
    return call(sum_kernel, (out, out, out), [VMEM] * 2, [], 4)(chip_share, swap(chip_share, 2))


def solution(mesh):
    def per_device(*arrays):
        (tokens, width), (units, rank) = arrays[1].shape, arrays[8].shape
        fits = (
            mesh.shape["tensor"] == 4
            and (tokens, rank) == (SEQS * LEN, LEN // 2)
            and width % 128 == 0
            and units % BLOCK == 0
            and units % CHIP_BLOCK == 0
            and units // BLOCK == 4
        )
        return tuple((fast if fits else plain)(*arrays))

    return jax.shard_map(
        per_device,
        mesh=mesh,
        in_specs=(P("dp", "tensor"),) * 4 + (P("tensor", None),) * 6,
        out_specs=(P("dp", None, None),) * 3,
        check_vma=False,
    )
```

```python
import jax
import jax.numpy as jnp
from jax import lax
from jax.experimental import pallas as pl
from jax.experimental.pallas import tpu as pltpu
from jax.sharding import PartitionSpec as P

SEQS = 2
LEN = 128
BLOCK = 1152
CHIP_BLOCK = 512
PARTS = 2
SPLIT = 2
MIB = 1 << 20
ANY = pl.BlockSpec(memory_space=pl.ANY)
VMEM = pl.BlockSpec(memory_space=pltpu.VMEM)
BF16 = jnp.bfloat16
F32 = jnp.float32


def product(left, right):
    return jnp.dot(left, right, preferred_element_type=F32)


def rows_by_rows(left, right, precision=None):
    return lax.dot_general(
        left, right, (((1,), (1,)), ((), ())), precision=precision, preferred_element_type=F32
    )


def per_sequence(matrix):
    return matrix.reshape(SEQS, matrix.shape[0] // SEQS, matrix.shape[1])


def plain(x_in, out_grad, gate_pre, up_pre, down_weight, x_factor, gate_factor, up_factor, h_factor, dy_factor):
    hidden_grad = rows_by_rows(lax.all_gather(out_grad, "tensor", axis=1, tiled=True), down_weight)
    gate_val = gate_pre.astype(F32)
    up_val = up_pre.astype(F32)
    sigmoid_gate = jax.nn.sigmoid(gate_val)
    silu_gate = gate_val * sigmoid_gate
    hidden = (silu_gate * up_val).astype(BF16)
    d_gate = (hidden_grad * up_val * sigmoid_gate * (1.0 + gate_val * (1.0 - sigmoid_gate))).astype(BF16)
    d_up = (hidden_grad * silu_gate).astype(BF16)
    rows = [
        product(x_in, x_factor),
        product(d_gate, gate_factor),
        product(d_up, up_factor),
        product(hidden, h_factor),
        product(out_grad, dy_factor),
    ]
    totals = lax.psum(jnp.stack(rows), "tensor")
    p_x, q_gate, q_up, p_h, q_y = [per_sequence(totals[i]) for i in range(5)]
    highest = lax.Precision.HIGHEST
    return (
        jnp.einsum("sli,slj->sij", p_x, q_gate, precision=highest),
        jnp.einsum("sli,slj->sij", p_x, q_up, precision=highest),
        jnp.einsum("sli,slj->sij", p_h, q_y, precision=highest),
    )


class Step:
    def __init__(self, owner, width, block, w_hbm):
        self.owner, self.width, self.block, self.w_hbm = owner, width, block, w_hbm

    def units(self, i):
        return pl.ds(pl.multiple_of(i * self.block, self.block), self.block)

    def copies(self, i, dst, sems):
        columns = pl.ds(pl.multiple_of(self.owner * self.width, 128), self.width)
        part = self.block // PARTS
        return [
            pltpu.make_async_copy(
                self.w_hbm.at[pl.ds(pl.multiple_of(i * self.block + k * part, part), part), columns],
                dst.at[pl.ds(k * part, part)],
                sems.at[k],
            )
            for k in range(PARTS)
        ]


def start(copies):
    for copy in copies:
        copy.start()


def wait(copies):
    for copy in copies:
        copy.wait()


def stream(step, ahead, blocks, head, w_v, sems, body, later):
    heads = head.shape[0]
    slots = w_v.shape[0]

    def copies(j):
        return step.copies(j, w_v.at[(j - heads) % slots], sems.at[j])

    def begin(j):
        @pl.when(j < blocks)
        def _():
            start(copies(j))

        for k, group in enumerate(later):

            @pl.when(j == blocks + k)
            def _():
                start(group)

    for j in range(heads, ahead):
        start(copies(j))

    @pl.loop(0, heads)
    def _(i):
        begin(i + ahead)
        body(i, head.at[i])

    @pl.loop(heads, blocks)
    def _(i):
        begin(i + ahead)
        wait(copies(i))
        body(i, w_v.at[(i - heads) % slots])

    for k, group in enumerate(later):
        if k >= ahead:
            start(group)
    for group in later:
        wait(group)


def elementwise_kernel(x_hbm, og_hbm, gate_hbm, up_hbm, w_hbm, xf_hbm, yf_hbm, hf_hbm,
                       a_ref, b_ref, ph_ref, pq_ref, head_ref, own_ref,
                       x_v, og_v, gate_v, up_v, xf_v, yf_v, hf_v, sems, gate_sems, up_sems, w_sems):
    units = a_ref.shape[0]
    rank = ph_ref.shape[0]
    turns = units // BLOCK

    def at(i):
        return pl.ds(pl.multiple_of(i * BLOCK, BLOCK), BLOCK)

    def gate_up(i):
        return [
            pltpu.make_async_copy(gate_hbm.at[:, at(i)], gate_v.at[i], gate_sems.at[i]),
            pltpu.make_async_copy(up_hbm.at[:, at(i)], up_v.at[i], up_sems.at[i]),
        ]

    pairs = ((hf_hbm, hf_v), (og_hbm, og_v), (x_hbm, x_v), (xf_hbm, xf_v), (yf_hbm, yf_v))
    small = [pltpu.make_async_copy(src, dst, sems.at[i]) for i, (src, dst) in enumerate(pairs)]
    following = Step(lax.axis_index("tensor") // 2, head_ref.shape[2], head_ref.shape[1], w_hbm)
    heads = head_ref.shape[0]

    start(gate_up(0))
    start(small[:1])
    for i in range(1, turns):
        start(gate_up(i))
    start(small[1:])
    for i in range(heads):
        start(following.copies(i, head_ref.at[i], w_sems.at[i]))
    ph_ref[...] = jnp.zeros_like(ph_ref)
    wait(gate_up(0))
    wait(small[:1])

    @pl.loop(0, turns)
    def _(i):
        @pl.when(i > 0)
        def _():
            wait(gate_up(i))

        g = gate_v[i].T.astype(F32)
        u = up_v[i].T.astype(F32)
        s = 0.5 * jnp.tanh(0.5 * g) + 0.5
        silu = g * s
        a_ref[at(i)] = u * s * ((1.0 + g) - silu)
        b_ref[at(i)] = silu
        ph_ref[...] += product(hf_v[:, at(i)], (silu * u).astype(BF16))

    wait(small[1:])
    pq_ref[:rank] = rows_by_rows(xf_v[...], x_v[...])
    own_ref[...] = og_v[...].T
    pq_ref[rank:] = product(yf_v[...], own_ref[...])
    for i in range(heads):
        wait(following.copies(i, head_ref.at[i], w_sems.at[i]))


def chip_features_kernel(own_ref, mate_ref, head_ref, w_hbm, acc_ref, near_ref, og_v, w_v, sems, near_sems):
    me = lax.axis_index("tensor")
    width = own_ref.shape[0]
    step = Step(me // 2, 2 * width, w_v.shape[1], w_hbm)
    near = Step(me ^ 2, width, near_ref.shape[1], w_hbm)
    mine = pl.ds(pl.multiple_of(me % 2 * width, 128), width)
    theirs = pl.ds(pl.multiple_of((me + 1) % 2 * width, 128), width)
    og_v[mine] = own_ref[...]
    og_v[theirs] = mate_ref[...].T

    def body(i, weights):
        acc_ref[step.units(i)] = product(weights[...], og_v[...])

    later = [near.copies(k, near_ref.at[k], near_sems.at[k]) for k in range(near_ref.shape[0])]
    stream(step, 3, acc_ref.shape[0] // step.block, head_ref, w_v, sems, body, later)


def near_kernel(acc_in, og_ref, head_ref, w_hbm, acc_ref, far_ref, og_v, w_v, sems, far_sems):
    me = lax.axis_index("tensor")
    heads, block, width = head_ref.shape
    near, far = Step(me ^ 2, width, block, w_hbm), Step(me ^ 3, width, block, w_hbm)
    rest = [near.copies(heads + k, w_v.at[k], sems.at[k]) for k in range(w_v.shape[0])]
    later = [far.copies(k, far_ref.at[k], far_sems.at[k]) for k in range(far_ref.shape[0])]
    for group in rest + later:
        start(group)
    og_v[...] = og_ref[...].T

    turn = block // SPLIT

    def body(i, ref, j):
        at = pl.ds(pl.multiple_of(i * turn, turn), turn)
        part = pl.ds(pl.multiple_of(j % SPLIT * turn, turn), turn)
        acc_ref[at] = acc_in[at] + product(ref[j // SPLIT, part], og_v[...])

    @pl.loop(0, heads * SPLIT)
    def _(i):
        body(i, head_ref, i)

    for group in rest:
        wait(group)

    @pl.loop(0, w_v.shape[0] * SPLIT)
    def _(i):
        body(heads * SPLIT + i, w_v, i)

    for group in later:
        wait(group)


def far_kernel(acc_ref, og_ref, head_ref, w_hbm, a_ref, b_ref, gf_hbm, uf_hbm, gate_ref, up_ref,
               og_v, w_v, gf_ref, uf_ref, d_gate_v, d_up_v, sems, factor_sems):
    heads, block, width = head_ref.shape
    step = Step(lax.axis_index("tensor") ^ 3, width, block, w_hbm)
    factors = [
        pltpu.make_async_copy(src, dst, factor_sems.at[k]) for k, (src, dst) in enumerate(((gf_hbm, gf_ref), (uf_hbm, uf_ref)))
    ]
    start(step.copies(heads, w_v.at[0], sems.at[0]))
    start(factors)
    og_v[...] = og_ref[...].T

    turn = block // SPLIT

    def body(i, ref, j):
        at = pl.ds(pl.multiple_of(i * turn, turn), turn)
        part = pl.ds(pl.multiple_of(j % SPLIT * turn, turn), turn)
        hidden_grad = acc_ref[at] + product(ref[j // SPLIT, part], og_v[...])
        d_gate_v[at] = (hidden_grad * a_ref[at]).astype(BF16)
        d_up_v[at] = (hidden_grad * b_ref[at]).astype(BF16)

    @pl.loop(0, heads * SPLIT)
    def _(i):
        @pl.when(i == SPLIT)
        def _():
            start(step.copies(heads + 1, w_v.at[1], sems.at[1]))

        body(i, head_ref, i)

    @pl.loop(0, w_v.shape[0] * SPLIT)
    def _(i):
        @pl.when(i % SPLIT == 0)
        def _():
            k = i // SPLIT
            wait(step.copies(heads + k, w_v.at[k], sems.at[k]))

        body(heads * SPLIT + i, w_v, i)

    wait(factors)
    gate_ref[...] = product(gf_ref[...], d_gate_v[...])
    up_ref[...] = product(uf_ref[...], d_up_v[...])


def after_kernel(array_ref, token_ref, same_ref):
    pass


def chip_kernel(mine_ref, theirs_ref, token_ref, chip_ref):
    chip_ref[...] = mine_ref[...] + theirs_ref[...]


def gradients_kernel(chip_ref, other_ref, gate_ref, up_ref, ph_ref, share_ref):
    rank = ph_ref.shape[0]
    total = chip_ref[...] + other_ref[...]
    highest = lax.Precision.HIGHEST
    for s in range(SEQS):
        at = slice(s * LEN, (s + 1) * LEN)
        out = slice(s * rank, (s + 1) * rank)
        share_ref[out, :rank] = rows_by_rows(total[:rank, at], gate_ref[:, at], highest)
        share_ref[out, rank:] = rows_by_rows(total[:rank, at], up_ref[:, at], highest)
        share_ref[SEQS * rank :, out] = rows_by_rows(ph_ref[:, at], total[rank:, at], highest)


def sum_kernel(mine_ref, theirs_ref, gate_ref, up_ref, down_ref):
    rank = gate_ref.shape[1]
    total = mine_ref[...].astype(F32) + theirs_ref[...].astype(F32)
    for s in range(SEQS):
        gate_ref[s] = total[s * rank : (s + 1) * rank, :rank]
        up_ref[s] = total[s * rank : (s + 1) * rank, rank:]
        down_ref[s] = total[SEQS * rank :, s * rank : (s + 1) * rank]


def fast(x_in, out_grad, gate_pre, up_pre, down_weight, x_factor, gate_factor, up_factor, h_factor, dy_factor):
    tokens, width = out_grad.shape
    units, rank = h_factor.shape
    dma = pltpu.SemaphoreType.DMA

    def in_hbm(array):
        return pltpu.with_memory_space_constraint(array, pltpu.HBM)

    def swap(array, bits):
        return lax.ppermute(array, "tensor", [(i, i ^ bits) for i in range(4)])

    def call(kernel, out_shape, in_specs, scratch, mib, flops=0, moved=0, **kwargs):
        several = isinstance(out_shape, tuple)
        return pl.pallas_call(
            kernel,
            out_shape=out_shape,
            in_specs=in_specs,
            out_specs=(VMEM,) * len(out_shape) if several else VMEM,
            scratch_shapes=list(scratch),
            compiler_params=pltpu.CompilerParams(vmem_limit_bytes=mib * MIB),
            cost_estimate=pl.CostEstimate(flops=flops, bytes_accessed=moved, transcendentals=0),
            **kwargs,
        )

    held = pltpu.VMEM((units, tokens), F32)
    per_product = 2 * tokens * width * units
    turns = units // BLOCK
    narrow = pltpu.VMEM((rank, tokens), F32)
    turned = pltpu.VMEM((width, tokens), BF16)
    weight = in_hbm(down_weight)

    def blocks(count):
        return pltpu.VMEM((count, BLOCK, width), BF16)

    def chip_blocks(count):
        return pltpu.VMEM((count, CHIP_BLOCK, 2 * width), BF16)

    near = swap(out_grad, 2)
    mate = swap(out_grad, 1)
    a, b, ph, pq, head, own = call(
        elementwise_kernel,
        (held, held, narrow, pltpu.VMEM((2 * rank, tokens), F32), chip_blocks(2), turned),
        [ANY] * 8,
        [
            pltpu.VMEM((tokens, width), BF16),
            pltpu.VMEM((tokens, width), BF16),
            pltpu.VMEM((turns, tokens, BLOCK), BF16),
            pltpu.VMEM((turns, tokens, BLOCK), BF16),
            pltpu.VMEM((rank, width), BF16),
            pltpu.VMEM((rank, width), BF16),
            pltpu.VMEM((rank, units), BF16),
            dma((5,)),
            dma((turns,)),
            dma((turns,)),
            dma((2, PARTS)),
        ],
        14,
        per_product // 4,
        4 * units * tokens,
    )(
        in_hbm(x_in),
        in_hbm(out_grad),
        in_hbm(gate_pre),
        in_hbm(up_pre),
        weight,
        in_hbm(x_factor.T),
        in_hbm(dy_factor.T),
        in_hbm(h_factor.T),
    )
    pq_mate = swap(pq, 1)
    acc, head = call(
        chip_features_kernel,
        (held, blocks(turns - 1)),
        [VMEM] * 3 + [ANY],
        [
            pltpu.VMEM((2 * width, tokens), BF16),
            chip_blocks(4),
            dma((units // CHIP_BLOCK, PARTS)),
            dma((turns - 1, PARTS)),
        ],
        14,
        2 * per_product,
        4 * units * width,
    )(own, mate, head, weight)

    def after(array, token):
        return pl.pallas_call(
            after_kernel,
            out_shape=pltpu.VMEM(array.shape, array.dtype),
            in_specs=[ANY, ANY],
            out_specs=ANY,
            input_output_aliases={0: 0},
            compiler_params=pltpu.CompilerParams(vmem_limit_bytes=MIB),
        )(array, token)

    chip = call(chip_kernel, pltpu.VMEM(pq.shape, F32), [VMEM, VMEM, ANY], [], 1)(pq, pq_mate, head)
    near = after(near, chip)
    far = swap(near, 1)
    acc, head = call(
        near_kernel,
        (held, blocks(2)),
        [VMEM] * 3 + [ANY],
        [turned, blocks(1), dma((1, PARTS)), dma((2, PARTS))],
        6,
        per_product,
        2 * units * width,
        input_output_aliases={0: 0},
    )(acc, near, head, weight)
    chip = after(chip, head)
    chip_across = swap(chip, 2)
    factor = pltpu.VMEM((rank, units), BF16)
    kept = pltpu.VMEM((units, tokens), BF16)
    q_gate, q_up = call(
        far_kernel,
        (narrow, narrow),
        [VMEM] * 3 + [ANY] + [VMEM] * 2 + [ANY] * 2,
        [turned, blocks(turns - 2), factor, factor, kept, kept, dma((turns - 2, PARTS)), dma((2,))],
        16,
        per_product,
        2 * units * width,
    )(acc, far, head, weight, a, b, in_hbm(gate_factor.T), in_hbm(up_factor.T))
    share = call(gradients_kernel, pltpu.VMEM(((SEQS + 1) * rank, 2 * rank), F32), [VMEM] * 5, [], 4)(
        chip, chip_across, q_gate, q_up, ph
    )
    chip_share = (share + swap(share, 1)).astype(BF16)
    out = jax.ShapeDtypeStruct((SEQS, rank, rank), F32)
    return call(sum_kernel, (out, out, out), [VMEM] * 2, [], 4)(chip_share, swap(chip_share, 2))


def solution(mesh):
    def per_device(*arrays):
        (tokens, width), (units, rank) = arrays[1].shape, arrays[8].shape
        fits = (
            mesh.shape["tensor"] == 4
            and (tokens, rank) == (SEQS * LEN, LEN // 2)
            and width % 128 == 0
            and units % BLOCK == 0
            and units % CHIP_BLOCK == 0
            and units // BLOCK == 4
        )
        return tuple((fast if fits else plain)(*arrays))

    return jax.shard_map(
        per_device,
        mesh=mesh,
        in_specs=(P("dp", "tensor"),) * 4 + (P("tensor", None),) * 6,
        out_specs=(P("dp", None, None),) * 3,
        check_vma=False,
    )
```

```python
import jax
import jax.numpy as jnp
from jax import lax
from jax.experimental import pallas as pl
from jax.experimental.pallas import tpu as pltpu
from jax.sharding import PartitionSpec as P

SEQS = 2
LEN = 128
BLOCK = 1152
CHIP_BLOCK = 512
PARTS = 4
MIB = 1 << 20
ANY = pl.BlockSpec(memory_space=pl.ANY)
VMEM = pl.BlockSpec(memory_space=pltpu.VMEM)
BF16 = jnp.bfloat16
F32 = jnp.float32


def product(left, right):
    return jnp.dot(left, right, preferred_element_type=F32)


def rows_by_rows(left, right, precision=None):
    return lax.dot_general(
        left, right, (((1,), (1,)), ((), ())), precision=precision, preferred_element_type=F32
    )


def per_sequence(matrix):
    return matrix.reshape(SEQS, matrix.shape[0] // SEQS, matrix.shape[1])


def plain(x_in, out_grad, gate_pre, up_pre, down_weight, x_factor, gate_factor, up_factor, h_factor, dy_factor):
    hidden_grad = rows_by_rows(lax.all_gather(out_grad, "tensor", axis=1, tiled=True), down_weight)
    gate_val = gate_pre.astype(F32)
    up_val = up_pre.astype(F32)
    sigmoid_gate = jax.nn.sigmoid(gate_val)
    silu_gate = gate_val * sigmoid_gate
    hidden = (silu_gate * up_val).astype(BF16)
    d_gate = (hidden_grad * up_val * sigmoid_gate * (1.0 + gate_val * (1.0 - sigmoid_gate))).astype(BF16)
    d_up = (hidden_grad * silu_gate).astype(BF16)
    rows = [
        product(x_in, x_factor),
        product(d_gate, gate_factor),
        product(d_up, up_factor),
        product(hidden, h_factor),
        product(out_grad, dy_factor),
    ]
    totals = lax.psum(jnp.stack(rows), "tensor")
    p_x, q_gate, q_up, p_h, q_y = [per_sequence(totals[i]) for i in range(5)]
    highest = lax.Precision.HIGHEST
    return (
        jnp.einsum("sli,slj->sij", p_x, q_gate, precision=highest),
        jnp.einsum("sli,slj->sij", p_x, q_up, precision=highest),
        jnp.einsum("sli,slj->sij", p_h, q_y, precision=highest),
    )


class Step:
    def __init__(self, owner, width, block, w_hbm):
        self.owner, self.width, self.block, self.w_hbm = owner, width, block, w_hbm

    def units(self, i):
        return pl.ds(pl.multiple_of(i * self.block, self.block), self.block)

    def copies(self, i, dst, sems):
        columns = pl.ds(pl.multiple_of(self.owner * self.width, 128), self.width)
        part = self.block // PARTS
        return [
            pltpu.make_async_copy(
                self.w_hbm.at[pl.ds(pl.multiple_of(i * self.block + k * part, part), part), columns],
                dst.at[pl.ds(k * part, part)],
                sems.at[k],
            )
            for k in range(PARTS)
        ]


def start(copies):
    for copy in copies:
        copy.start()


def wait(copies):
    for copy in copies:
        copy.wait()


def stream(step, ahead, blocks, head, w_v, sems, body, later):
    heads = head.shape[0]
    slots = w_v.shape[0]

    def copies(j):
        return step.copies(j, w_v.at[(j - heads) % slots], sems.at[j])

    def begin(j):
        @pl.when(j < blocks)
        def _():
            start(copies(j))

        for k, group in enumerate(later):

            @pl.when(j == blocks + k)
            def _():
                start(group)

    for j in range(heads, ahead):
        start(copies(j))

    @pl.loop(0, heads)
    def _(i):
        begin(i + ahead)
        body(i, head.at[i])

    @pl.loop(heads, blocks)
    def _(i):
        begin(i + ahead)
        wait(copies(i))
        body(i, w_v.at[(i - heads) % slots])

    for k, group in enumerate(later):
        if k >= ahead:
            start(group)
    for group in later:
        wait(group)


def elementwise_kernel(x_hbm, og_hbm, gate_hbm, up_hbm, w_hbm, xf_hbm, yf_hbm, hf_hbm,
                       a_ref, b_ref, ph_ref, pq_ref, head_ref, own_ref,
                       x_v, og_v, gate_v, up_v, xf_v, yf_v, hf_v, sems, gate_sems, up_sems, w_sems):
    units = a_ref.shape[0]
    rank = ph_ref.shape[0]
    turns = units // BLOCK

    def at(i):
        return pl.ds(pl.multiple_of(i * BLOCK, BLOCK), BLOCK)

    def gate_up(i):
        return [
            pltpu.make_async_copy(gate_hbm.at[:, at(i)], gate_v.at[i], gate_sems.at[i]),
            pltpu.make_async_copy(up_hbm.at[:, at(i)], up_v.at[i], up_sems.at[i]),
        ]

    pairs = ((hf_hbm, hf_v), (og_hbm, og_v), (x_hbm, x_v), (xf_hbm, xf_v), (yf_hbm, yf_v))
    small = [pltpu.make_async_copy(src, dst, sems.at[i]) for i, (src, dst) in enumerate(pairs)]
    following = Step(lax.axis_index("tensor") // 2, head_ref.shape[2], head_ref.shape[1], w_hbm)
    heads = head_ref.shape[0]

    start(gate_up(0))
    start(small[:1])
    for i in range(1, turns):
        start(gate_up(i))
    start(small[1:])
    for i in range(heads):
        start(following.copies(i, head_ref.at[i], w_sems.at[i]))
    ph_ref[...] = jnp.zeros_like(ph_ref)
    wait(gate_up(0))
    wait(small[:1])

    @pl.loop(0, turns)
    def _(i):
        @pl.when(i > 0)
        def _():
            wait(gate_up(i))

        g = gate_v[i].T.astype(F32)
        u = up_v[i].T.astype(F32)
        s = 0.5 * jnp.tanh(0.5 * g) + 0.5
        silu = g * s
        a_ref[at(i)] = u * s * ((1.0 + g) - silu)
        b_ref[at(i)] = silu
        ph_ref[...] += product(hf_v[:, at(i)], (silu * u).astype(BF16))

    wait(small[1:])
    pq_ref[:rank] = rows_by_rows(xf_v[...], x_v[...])
    own_ref[...] = og_v[...].T
    pq_ref[rank:] = product(yf_v[...], own_ref[...])
    for i in range(heads):
        wait(following.copies(i, head_ref.at[i], w_sems.at[i]))


def chip_features_kernel(own_ref, mate_ref, head_ref, w_hbm, acc_ref, near_ref, og_v, w_v, sems, near_sems):
    me = lax.axis_index("tensor")
    width = own_ref.shape[0]
    step = Step(me // 2, 2 * width, w_v.shape[1], w_hbm)
    near = Step(me ^ 2, width, near_ref.shape[1], w_hbm)
    mine = pl.ds(pl.multiple_of(me % 2 * width, 128), width)
    theirs = pl.ds(pl.multiple_of((me + 1) % 2 * width, 128), width)
    og_v[mine] = own_ref[...]
    og_v[theirs] = mate_ref[...].T

    def body(i, weights):
        acc_ref[step.units(i)] = product(weights[...], og_v[...])

    later = [near.copies(k, near_ref.at[k], near_sems.at[k]) for k in range(near_ref.shape[0])]
    stream(step, 3, acc_ref.shape[0] // step.block, head_ref, w_v, sems, body, later)


def near_kernel(acc_in, og_ref, head_ref, w_hbm, acc_ref, far_ref, og_v, w_v, sems, far_sems):
    me = lax.axis_index("tensor")
    heads, block, width = head_ref.shape
    near, far = Step(me ^ 2, width, block, w_hbm), Step(me ^ 3, width, block, w_hbm)
    rest = [near.copies(heads + k, w_v.at[k], sems.at[k]) for k in range(w_v.shape[0])]
    later = [far.copies(k, far_ref.at[k], far_sems.at[k]) for k in range(far_ref.shape[0])]
    for group in rest + later:
        start(group)
    og_v[...] = og_ref[...].T

    def body(i, weights):
        at = near.units(i)
        acc_ref[at] = acc_in[at] + product(weights, og_v[...])

    @pl.loop(0, heads)
    def _(i):
        body(i, head_ref[i])

    for group in rest:
        wait(group)

    @pl.loop(0, w_v.shape[0])
    def _(i):
        body(heads + i, w_v[i])

    for group in later:
        wait(group)


def far_kernel(acc_ref, og_ref, head_ref, w_hbm, a_ref, b_ref, gf_hbm, uf_hbm, gate_ref, up_ref,
               og_v, w_v, gf_ref, uf_ref, d_gate_v, d_up_v, sems, factor_sems):
    heads, block, width = head_ref.shape
    step = Step(lax.axis_index("tensor") ^ 3, width, block, w_hbm)
    factors = [
        pltpu.make_async_copy(src, dst, factor_sems.at[k]) for k, (src, dst) in enumerate(((gf_hbm, gf_ref), (uf_hbm, uf_ref)))
    ]
    start(step.copies(heads, w_v.at[0], sems.at[0]))
    start(factors)
    og_v[...] = og_ref[...].T

    def body(i, weights):
        at = step.units(i)
        hidden_grad = acc_ref[at] + product(weights, og_v[...])
        d_gate_v[at] = (hidden_grad * a_ref[at]).astype(BF16)
        d_up_v[at] = (hidden_grad * b_ref[at]).astype(BF16)

    @pl.loop(0, heads)
    def _(i):
        @pl.when((i > 0) & (i < w_v.shape[0]))
        def _():
            start(step.copies(heads + i, w_v.at[i], sems.at[i]))

        body(i, head_ref[i])

    @pl.loop(0, w_v.shape[0])
    def _(i):
        wait(step.copies(heads + i, w_v.at[i], sems.at[i]))
        body(heads + i, w_v[i])

    wait(factors)
    gate_ref[...] = product(gf_ref[...], d_gate_v[...])
    up_ref[...] = product(uf_ref[...], d_up_v[...])


def after_kernel(array_ref, token_ref, same_ref):
    pass


def chip_kernel(mine_ref, theirs_ref, token_ref, chip_ref):
    chip_ref[...] = mine_ref[...] + theirs_ref[...]


def gradients_kernel(chip_ref, other_ref, gate_ref, up_ref, ph_ref, share_ref):
    rank = ph_ref.shape[0]
    total = chip_ref[...] + other_ref[...]
    highest = lax.Precision.HIGHEST
    for s in range(SEQS):
        at = slice(s * LEN, (s + 1) * LEN)
        out = slice(s * rank, (s + 1) * rank)
        share_ref[out, :rank] = rows_by_rows(total[:rank, at], gate_ref[:, at], highest)
        share_ref[out, rank:] = rows_by_rows(total[:rank, at], up_ref[:, at], highest)
        share_ref[SEQS * rank :, out] = rows_by_rows(ph_ref[:, at], total[rank:, at], highest)


def sum_kernel(mine_ref, theirs_ref, gate_ref, up_ref, down_ref):
    rank = gate_ref.shape[1]
    total = mine_ref[...].astype(F32) + theirs_ref[...].astype(F32)
    for s in range(SEQS):
        gate_ref[s] = total[s * rank : (s + 1) * rank, :rank]
        up_ref[s] = total[s * rank : (s + 1) * rank, rank:]
        down_ref[s] = total[SEQS * rank :, s * rank : (s + 1) * rank]


def fast(x_in, out_grad, gate_pre, up_pre, down_weight, x_factor, gate_factor, up_factor, h_factor, dy_factor):
    tokens, width = out_grad.shape
    units, rank = h_factor.shape
    dma = pltpu.SemaphoreType.DMA

    def in_hbm(array):
        return pltpu.with_memory_space_constraint(array, pltpu.HBM)

    def swap(array, bits):
        return lax.ppermute(array, "tensor", [(i, i ^ bits) for i in range(4)])

    def call(kernel, out_shape, in_specs, scratch, mib, flops=0, moved=0, **kwargs):
        several = isinstance(out_shape, tuple)
        return pl.pallas_call(
            kernel,
            out_shape=out_shape,
            in_specs=in_specs,
            out_specs=(VMEM,) * len(out_shape) if several else VMEM,
            scratch_shapes=list(scratch),
            compiler_params=pltpu.CompilerParams(vmem_limit_bytes=mib * MIB),
            cost_estimate=pl.CostEstimate(flops=flops, bytes_accessed=moved, transcendentals=0),
            **kwargs,
        )

    held = pltpu.VMEM((units, tokens), F32)
    per_product = 2 * tokens * width * units
    turns = units // BLOCK
    narrow = pltpu.VMEM((rank, tokens), F32)
    turned = pltpu.VMEM((width, tokens), BF16)
    weight = in_hbm(down_weight)

    def blocks(count):
        return pltpu.VMEM((count, BLOCK, width), BF16)

    def chip_blocks(count):
        return pltpu.VMEM((count, CHIP_BLOCK, 2 * width), BF16)

    near = swap(out_grad, 2)
    mate = swap(out_grad, 1)
    a, b, ph, pq, head, own = call(
        elementwise_kernel,
        (held, held, narrow, pltpu.VMEM((2 * rank, tokens), F32), chip_blocks(2), turned),
        [ANY] * 8,
        [
            pltpu.VMEM((tokens, width), BF16),
            pltpu.VMEM((tokens, width), BF16),
            pltpu.VMEM((turns, tokens, BLOCK), BF16),
            pltpu.VMEM((turns, tokens, BLOCK), BF16),
            pltpu.VMEM((rank, width), BF16),
            pltpu.VMEM((rank, width), BF16),
            pltpu.VMEM((rank, units), BF16),
            dma((5,)),
            dma((turns,)),
            dma((turns,)),
            dma((2, PARTS)),
        ],
        14,
        per_product // 4,
        4 * units * tokens,
    )(
        in_hbm(x_in),
        in_hbm(out_grad),
        in_hbm(gate_pre),
        in_hbm(up_pre),
        weight,
        in_hbm(x_factor.T),
        in_hbm(dy_factor.T),
        in_hbm(h_factor.T),
    )
    pq_mate = swap(pq, 1)
    acc, head = call(
        chip_features_kernel,
        (held, blocks(turns - 1)),
        [VMEM] * 3 + [ANY],
        [
            pltpu.VMEM((2 * width, tokens), BF16),
            chip_blocks(4),
            dma((units // CHIP_BLOCK, PARTS)),
            dma((turns - 1, PARTS)),
        ],
        14,
        2 * per_product,
        4 * units * width,
    )(own, mate, head, weight)

    def after(array, token):
        return pl.pallas_call(
            after_kernel,
            out_shape=pltpu.VMEM(array.shape, array.dtype),
            in_specs=[ANY, ANY],
            out_specs=ANY,
            input_output_aliases={0: 0},
            compiler_params=pltpu.CompilerParams(vmem_limit_bytes=MIB),
        )(array, token)

    chip = call(chip_kernel, pltpu.VMEM(pq.shape, F32), [VMEM, VMEM, ANY], [], 1)(pq, pq_mate, head)
    near = after(near, chip)
    far = swap(near, 1)
    acc, head = call(
        near_kernel,
        (held, blocks(2)),
        [VMEM] * 3 + [ANY],
        [turned, blocks(1), dma((1, PARTS)), dma((2, PARTS))],
        6,
        per_product,
        2 * units * width,
        input_output_aliases={0: 0},
    )(acc, near, head, weight)
    chip = after(chip, head)
    chip_across = swap(chip, 2)
    factor = pltpu.VMEM((rank, units), BF16)
    kept = pltpu.VMEM((units, tokens), BF16)
    q_gate, q_up = call(
        far_kernel,
        (narrow, narrow),
        [VMEM] * 3 + [ANY] + [VMEM] * 2 + [ANY] * 2,
        [turned, blocks(turns - 2), factor, factor, kept, kept, dma((turns - 2, PARTS)), dma((2,))],
        16,
        per_product,
        2 * units * width,
    )(acc, far, head, weight, a, b, in_hbm(gate_factor.T), in_hbm(up_factor.T))
    share = call(gradients_kernel, pltpu.VMEM(((SEQS + 1) * rank, 2 * rank), F32), [VMEM] * 5, [], 4)(
        chip, chip_across, q_gate, q_up, ph
    )
    chip_share = (share + swap(share, 1)).astype(BF16)
    out = jax.ShapeDtypeStruct((SEQS, rank, rank), F32)
    return call(sum_kernel, (out, out, out), [VMEM] * 2, [], 4)(chip_share, swap(chip_share, 2))


def solution(mesh):
    def per_device(*arrays):
        (tokens, width), (units, rank) = arrays[1].shape, arrays[8].shape
        fits = (
            mesh.shape["tensor"] == 4
            and (tokens, rank) == (SEQS * LEN, LEN // 2)
            and width % 128 == 0
            and units % BLOCK == 0
            and units % CHIP_BLOCK == 0
            and units // BLOCK == 4
        )
        return tuple((fast if fits else plain)(*arrays))

    return jax.shard_map(
        per_device,
        mesh=mesh,
        in_specs=(P("dp", "tensor"),) * 4 + (P("tensor", None),) * 6,
        out_specs=(P("dp", None, None),) * 3,
        check_vma=False,
    )
```
